256 devices in a mesh: lat: 16 (over z, x_lo), lon: 16 (over y, x_hi, core).
Axes of the slice: x: 4 (x_hi: 2, x_lo: 2; x = x_hi * 2 + x_lo), y: 4, z: 8, core: 2. Of those that a mesh axis runs over, the one named last changes fastest.
Arguments:
- state: bfloat16 [2, 96, 384, 192], P(None, 'lat', 'lon'), may hold values from -6 to 6
- out_cot: bfloat16 [2, 96, 384, 192], P(None, 'lat', 'lon'), may hold values from -6 to 6
- qkv_weight: bfloat16 [2, 192, 576], replicated, may hold values from -0.4375 to 0.4375
- proj_weight: bfloat16 [2, 192, 192], replicated, may hold values from -0.4375 to 0.4375
- fc1_weight: bfloat16 [2, 192, 768], replicated, may hold values from -0.4375 to 0.4375
- fc2_weight: bfloat16 [2, 768, 192], replicated, may hold values from -0.21875 to 0.21875
- norm_gain: float32 [2, 2, 192], replicated, may hold values from 0.5 to 1.5
- bias_table: float32 [2, 16, 1, 6, 3312], P(None, 'lat'), may hold values from -3 to 303
Outputs:
- state_grad: float32 [2, 96, 384, 192], P(None, 'lat', 'lon')
- qkv_grad: float32 [2, 192, 576], P(None, 'lat', 'lon')
- proj_grad: float32 [2, 192, 192], P(None, 'lat', 'lon')
- fc1_grad: float32 [2, 192, 768], P(None, 'lat', 'lon')
- fc2_grad: float32 [2, 768, 192], P(None, 'lat', 'lon')
- norm_gain_grad: float32 [2, 2, 192], replicated
- bias_table_grad: float32 [2, 16, 1, 6, 3312], P(None, 'lat', None, None, 'lon')
The draws below stay inside these ranges and needn't reach their ends.
All inputs are finite; a program needn't handle non-finite values.
Results may differ from the reference program's by a relative error of at most 0.028.
Values may be sent and summed in bfloat16 or wider, within the bound.
A program may use at most 128 MiB of HBM per device.

```python
import jax
import jax.numpy as jnp
from jax import lax

C = 192
HEADS = 6
HID = 768
Z = 2
WZ = 2
WH = 6
WW = 12
LAT = 96
LON = 384
NLATWIN = 16
ZWIN = 1
POS = 3312


def draw_bias_table(key, part):
    keys = jax.random.split(jax.random.fold_in(key, 17), 1)
    shape = (2, NLATWIN, ZWIN, HEADS, POS)
    return jnp.clip(jax.random.normal(keys[0], shape, jnp.float32), -3.0, 3.0)


def shard_levels(own_key, dims, cuts, low, top_value):
    def one(position, shards_of):
        draws = jax.random.uniform(jax.random.fold_in(jax.random.fold_in(own_key, 6), position), (shards_of,), jnp.float32, low / len(cuts), top_value / len(cuts))
        return jnp.repeat(jnp.exp(draws), dims[position] // shards_of).reshape((-1,) + (1,) * (len(dims) - position - 1))

    factor_of = one(*cuts[0])
    for cut in cuts[1:]:
        factor_of = factor_of * one(*cut)
    return factor_of


def scatter_about(rng, extent, spread, most, cuts=(), kind=jnp.bfloat16):
    values = jax.random.normal(rng, extent, jnp.float32) * spread
    if len(cuts) > 0:
        values = shard_levels(rng, extent, cuts, -0.22, 0.18) * values
    return jnp.clip(values, min=-most, max=most).astype(kind)


def setup_inputs(seed: int = 0) -> dict:
    streams_of = jax.random.split(jax.random.key(seed), 9)
    state = scatter_about(streams_of[0], (Z, LAT, LON, C), 1.0, 6.0, ((1, 16), (2, 16)))
    out_cot = scatter_about(streams_of[1], (Z, LAT, LON, C), 1.0, 6.0, ((1, 16), (2, 16)))
    qkv_weight = scatter_about(streams_of[2], (2, C, 3 * C), C ** -0.5, 0.4375)
    proj_weight = scatter_about(streams_of[3], (2, C, C), C ** -0.5, 0.4375)
    fc1_weight = scatter_about(streams_of[4], (2, C, HID), C ** -0.5, 0.4375)
    fc2_weight = scatter_about(streams_of[5], (2, HID, C), HID ** -0.5, 0.21875)
    norm_gain = jnp.clip(1.0 + 0.1 * jax.random.normal(streams_of[6], (2, 2, C), jnp.float32), 0.5, 1.5)
    bias_table = draw_bias_table(jax.random.fold_in(streams_of[8], 71), 0)
    return {"state": state, "out_cot": out_cot, "qkv_weight": qkv_weight, "proj_weight": proj_weight, "fc1_weight": fc1_weight, "fc2_weight": fc2_weight, "norm_gain": norm_gain, "bias_table": bias_table}


def position_index():
    tokens = jnp.arange(WZ * WH * WW, dtype=jnp.int32)
    level_in = tokens // (WH * WW)
    row_in = tokens // WW % WH
    column_in = tokens % WW
    level_part = (level_in[:, None] * WZ + level_in[None, :]) * (WH * WH * (2 * WW - 1))
    row_part = (row_in[:, None] * WH + row_in[None, :]) * (2 * WW - 1)
    return (level_part + row_part + column_in[:, None] - column_in[None, :] + WW - 1).astype(jnp.int32)

def shifted_labels(lat_windows, level_windows, lat_start, lat_total):
    tokens = jnp.arange(WZ * WH * WW, dtype=jnp.int32)
    level_in = tokens // (WH * WW)
    row_in = tokens // WW % WH
    global_level = jnp.arange(level_windows, dtype=jnp.int32)[None, :, None] * WZ + level_in[None, None, :]
    global_row = lat_start + jnp.arange(lat_windows, dtype=jnp.int32)[:, None, None] * WH + row_in[None, None, :]
    level_mark = (global_level >= level_windows * WZ - 1).astype(jnp.int32)
    row_mark = (global_row >= lat_total - WH // 2).astype(jnp.int32)
    return (2 * level_mark + row_mark).astype(jnp.int32)

def to_windows(brick):
    levels, rows, columns, model_width = brick.shape
    shaped = brick.reshape(levels // WZ, WZ, rows // WH, WH, columns // WW, WW, model_width)
    shaped = shaped.transpose(2, 0, 4, 1, 3, 5, 6)
    return shaped.reshape(rows // WH, levels // WZ, columns // WW, WZ * WH * WW, model_width)

def from_windows(windows):
    lat_windows, level_windows, lon_windows, window_size, model_width = windows.shape
    shaped = windows.reshape(lat_windows, level_windows, lon_windows, WZ, WH, WW, model_width)
    shaped = shaped.transpose(1, 3, 0, 4, 2, 5, 6)
    return shaped.reshape(level_windows * WZ, lat_windows * WH, lon_windows * WW, model_width)

def layer_norm(values, gain):
    average = lax.optimization_barrier(jnp.mean(values, -1, keepdims=True))
    centred = values - average
    variance = lax.optimization_barrier(jnp.mean(centred * centred, -1, keepdims=True))
    return centred * lax.rsqrt(variance + 1e-05) * gain

def rounded(values):
    return lax.optimization_barrier(values.astype(jnp.bfloat16)).astype(jnp.float32)

def run_block(values, gain_pair, table_part, offsets, labels, weights):
    w_qkv, w_proj, w_fc1, w_fc2 = weights
    head_count = table_part.shape[2]
    model_width = values.shape[-1]
    head_size = model_width // head_count
    normed = layer_norm(values, gain_pair[0]).astype(jnp.bfloat16)
    qkv_out = jnp.dot(normed, w_qkv, preferred_element_type=jnp.float32) + offsets[0]
    projected = rounded(qkv_out).reshape(values.shape[:-1] + (3, head_count, head_size))
    queries = projected[..., 0, :, :]
    key_vectors = projected[..., 1, :, :]
    value_vectors = projected[..., 2, :, :]
    scores = jnp.einsum('abcqhd,abckhd->abchqk', queries, key_vectors) * head_size ** (-0.5)
    bias_full = jnp.take(table_part, position_index(), axis=3)
    allowed = (labels[:, :, :, None] == labels[:, :, None, :])[:, :, None, None]
    scores = jnp.where(allowed, scores + bias_full[:, :, None], -1e+30)
    attention = rounded(jax.nn.softmax(scores, axis=-1))
    attended = jnp.einsum('abchqk,abckhd->abcqhd', attention, value_vectors).reshape(values.shape)
    joined = attended.astype(jnp.bfloat16)
    middle = values + jnp.dot(joined, w_proj, preferred_element_type=jnp.float32) + offsets[1]
    normed_two = layer_norm(middle, gain_pair[1]).astype(jnp.bfloat16)
    expanded = jnp.dot(normed_two, w_fc1, preferred_element_type=jnp.float32) + offsets[2]
    hidden = jax.nn.gelu(expanded, approximate=False).astype(jnp.bfloat16)
    result = middle + jnp.dot(hidden, w_fc2, preferred_element_type=jnp.float32) + offsets[3]
    return (result, (normed, joined, normed_two, hidden))

def open_block(values, gain_pair, table_part, labels, weights):
    lead = values.shape[:-1]
    model_width = values.shape[-1]
    offsets = (jnp.zeros(lead + (3 * model_width,), jnp.float32), jnp.zeros(lead + (model_width,), jnp.float32), jnp.zeros(lead + (weights[2].shape[1],), jnp.float32), jnp.zeros(lead + (model_width,), jnp.float32))

    def forward(inputs, gains_in, table_in, offsets_in):
        return run_block(inputs, gains_in, table_in, offsets_in, labels, weights)
    return jax.vjp(forward, values, gain_pair, table_part, offsets, has_aux=True)

def close_block(pullback, stored, cotangent):
    value_grad, gain_grad, table_grad, output_grads = pullback(cotangent)
    weight_grads = tuple((lax.dot_general(inputs_act.reshape(-1, inputs_act.shape[-1]), grad_out.reshape(-1, grad_out.shape[-1]).astype(jnp.bfloat16), (((0,), (0,)), ((), ())), preferred_element_type=jnp.float32) for inputs_act, grad_out in zip(stored, output_grads)))
    return (value_grad, weight_grads, gain_grad, table_grad)

def stripe_grads(values, cotangents, gain_pair, table_part, labels, weights):

    def one_stripe(carry, stripe):
        piece, cotangent, table_row, label_row = stripe
        result, pullback, stored = open_block(piece[None], gain_pair, table_row[None], label_row[None], weights)
        value_grad, weight_grads, gain_grad, table_grad = close_block(pullback, stored, cotangent[None])
        summed = tuple((left + right for left, right in zip(carry[0], weight_grads)))
        return ((summed, carry[1] + gain_grad), (value_grad[0], table_grad[0]))
    initial = (tuple((jnp.zeros(w.shape, jnp.float32) for w in weights)), jnp.zeros(gain_pair.shape, jnp.float32))
    (weight_grads, gain_grad), (value_grad, table_grad) = lax.scan(one_stripe, initial, (values, cotangents, table_part, labels))
    return (value_grad, weight_grads, gain_grad, table_grad)

def reference(state, out_cot, qkv_weight, proj_weight, fc1_weight, fc2_weight, norm_gain, bias_table):
    matrices = (qkv_weight, proj_weight, fc1_weight, fc2_weight)
    first_weights = tuple((w[0] for w in matrices))
    second_weights = tuple((w[1] for w in matrices))
    windows_in = to_windows(state.astype(jnp.float32))
    unmasked = jnp.zeros((NLATWIN, ZWIN, WZ * WH * WW), jnp.int32)

    def forward_stripe(stripe):
        piece, table_row, label_row = stripe
        result = open_block(piece[None], norm_gain[0], table_row[None], label_row[None], first_weights)[0]
        return result[0]
    first_out = lax.map(forward_stripe, (windows_in, bias_table[0], unmasked))
    state_one = from_windows(first_out).astype(jnp.bfloat16)
    shifts = (-(WZ // 2), -(WH // 2), -(WW // 2))
    rolled = jnp.roll(state_one, shifts, (0, 1, 2)).astype(jnp.float32)
    cot_rolled = jnp.roll(out_cot, shifts, (0, 1, 2)).astype(jnp.float32)
    shifted = shifted_labels(NLATWIN, ZWIN, 0, LAT)
    rolled_grad, second_grads, second_gains, second_table = stripe_grads(to_windows(rolled), to_windows(cot_rolled), norm_gain[1], bias_table[1], shifted, second_weights)
    state_one_grad = jnp.roll(from_windows(rolled_grad), (WZ // 2, WH // 2, WW // 2), (0, 1, 2))
    state_grad, first_grads, first_gains, first_table = stripe_grads(windows_in, to_windows(state_one_grad), norm_gain[0], bias_table[0], unmasked, first_weights)
    stacked = tuple((jnp.stack((left, right)) for left, right in zip(first_grads, second_grads)))
    return (from_windows(state_grad), stacked[0], stacked[1], stacked[2], stacked[3], jnp.stack((first_gains, second_gains)), jnp.stack((first_table, second_table)))
```

```python
import functools

import jax
import jax.numpy as jnp
import ml_dtypes
import numpy as np
from jax import lax
from jax.experimental import pallas as pl
from jax.experimental.pallas import tpu as pltpu
from jax.sharding import Mesh
from jax.sharding import PartitionSpec as P

WZ = 2
WH = 6
WW = 12
LAT = ("lat_0", "lat_1")
LON = ("lon_0", "lon_1", "lon_2")
LAT_LON = ("lat_0", "lat_1", "lon_0", "lon_1", "lon_2")
BF = jnp.bfloat16
F32 = jnp.float32
HEADS = 6
DIM = 192
HEAD = 32
WIN = 144
TOK = 288
HID = 768
POS = 3312
SCALE = HEAD**-0.5


def token_order():
    order = np.zeros((TOK, TOK), np.float32)
    row = 0
    for n in range(2):
        for ih in range(2):
            for w in range(WW):
                for z in range(2):
                    for il in range(3):
                        source = (z * 6 + ih * 3 + il) * 24 + n * WW + w
                        order[row, source] = 1
                        row += 1
    return order.astype(ml_dtypes.bfloat16)


def lane_order():
    order = np.zeros((276, 512), np.float32)
    for a in range(12):
        for d in range(23):
            order[a * 23 + d, (a // 6) * 256 + d * 6 + a % 6] = 1
    return order.astype(ml_dtypes.bfloat16)


def table_offsets(flip):
    offsets = {}
    for b in range(12):
        for a in range(12):
            hk, zk, lk = b // 6, b % 6 // 3, b % 3
            hq, zq, lq = a // 6, a % 6 // 3, a % 3
            if flip:
                hk, zk, hq, zq = 1 - hk, 1 - zk, 1 - hq, 1 - zq
            offsets[b, a] = (zq * 2 + zk) * 828 + ((hq * 3 + lq) * 6 + hk * 3 + lk) * 23
    return offsets


def nn(a, b):
    return lax.dot_general(a, b, (((1,), (0,)), ((), ())), preferred_element_type=F32)


def nt(a, b):
    return lax.dot_general(a, b, (((1,), (1,)), ((), ())), preferred_element_type=F32)


def tn(a, b):
    return lax.dot_general(a, b, (((0,), (0,)), ((), ())), preferred_element_type=F32)


def two_pieces(x):
    high = x.astype(BF)
    return high, (x - high.astype(F32)).astype(BF)


def three_pieces(x):
    high = x.astype(BF)
    rest = x - high.astype(F32)
    middle = rest.astype(BF)
    return high, middle, (rest - middle.astype(F32)).astype(BF)


def expand_bias(table, lanes, flip, bias_ref):
    offsets = table_offsets(flip)
    rows = []
    for b in range(12):
        rows.append(
            jnp.concatenate(
                [table[:, offsets[b, a] : offsets[b, a] + 23] for a in range(12)], axis=1
            )
        )
    stacked = jnp.concatenate(rows, axis=0)
    high, middle, low = three_pieces(stacked)
    spread = nn(high, lanes) + nn(middle, lanes) + nn(low, lanes)
    for b in range(12):
        block = spread[b * 8 : b * 8 + 8]
        for w in range(WW):
            start = (11 - w) * 6
            both = jnp.concatenate(
                (block[:, start : start + 72], block[:, 256 + start : 256 + start + 72]), axis=1
            )
            row = (b // 6) * 72 + w * 6 + b % 6
            right = jnp.concatenate((both[:, 128:], jnp.zeros((8, 112), F32)), axis=1)
            bias_ref[0, pl.ds(row, 8, stride=WIN), :] = both[:, :128]
            bias_ref[1, pl.ds(row, 8, stride=WIN), :] = right


def reduce_bias(grad_ref, lanes, flip):
    offsets = table_offsets(flip)
    rows = []
    for b in range(12):
        left = jnp.zeros((8, 256), F32)
        right = jnp.zeros((8, 256), F32)
        for w in range(WW):
            start = (11 - w) * 6
            row = (b // 6) * 72 + w * 6 + b % 6
            both = jnp.concatenate(
                (
                    grad_ref[0, pl.ds(row, 8, stride=WIN), :],
                    grad_ref[1, pl.ds(row, 8, stride=WIN), :][:, :16],
                ),
                axis=1,
            )
            left = left + jnp.pad(both[:, :72], ((0, 0), (start, 184 - start)))
            right = right + jnp.pad(both[:, 72:], ((0, 0), (start, 184 - start)))
        rows.append(jnp.concatenate((left, right), axis=1))
    stacked = jnp.concatenate(rows, axis=0)
    high, low = two_pieces(stacked)
    packed = nt(high, lanes) + nt(low, lanes)
    places = sorted((start, b, a) for (b, a), start in offsets.items())
    return jnp.concatenate(
        [packed[b * 8 : b * 8 + 8, a * 23 : a * 23 + 23] for _, b, a in places], axis=1
    )


def normed(u):
    mean = jnp.mean(u, -1, keepdims=True)
    centred = u - mean
    scale = lax.rsqrt(jnp.mean(centred * centred, -1, keepdims=True) + 1e-05)
    return centred * scale, scale


def normed_back(grad, unit, scale):
    mean = jnp.mean(grad, -1, keepdims=True)
    product = jnp.mean(grad * unit, -1, keepdims=True)
    return scale * (grad - mean - unit * product)


def head_masks():
    lane = lax.broadcasted_iota(jnp.int32, (1, DIM), 1) // HEAD
    return [(lane == h).astype(F32) for h in range(HEADS)]


def by_head(x, masks):
    return jnp.concatenate([x * m.astype(BF) for m in masks], axis=0)


def from_heads(x, masks):
    total = x[:WIN] * masks[0]
    for h in range(1, HEADS):
        total = total + x[h * WIN : h * WIN + WIN] * masks[h]
    return total


def forward(u, gains, w_qkv, w_proj, w_fc1, w_fc2, bias_ref, allowed, prob_ref):
    masks = head_masks()
    unit, _ = normed(u)
    n1 = (unit * gains[0:1]).astype(BF)
    q, k, v = (
        nn(n1, w_qkv[:, i * DIM : i * DIM + DIM]) for i in range(3)
    )
    joined = []
    for n in range(2):
        part = slice(n * WIN, n * WIN + WIN)
        scores = nt(by_head(k[part].astype(BF), masks), q[part].astype(BF))
        v_t = jnp.transpose(v[part]).astype(BF)
        out_t = []
        for h in range(HEADS):
            rows = slice(h * WIN, h * WIN + WIN)
            bias = jnp.concatenate((bias_ref[0, rows, :], bias_ref[1, rows, :16]), axis=1)
            s = scores[rows] * SCALE + bias
            if allowed is not None:
                s = jnp.where(allowed, s, -1e30)
            e = jnp.exp(s - jnp.max(s, 0, keepdims=True))
            p = (e * (1.0 / jnp.sum(e, 0, keepdims=True))).astype(BF)
            prob_ref[n, rows, :] = p
            out_t.append(nn(v_t[h * HEAD : h * HEAD + HEAD], p))
        joined.append(jnp.transpose(jnp.concatenate(out_t, axis=0)))
    o = jnp.concatenate(joined, axis=0).astype(BF)
    m = u + nn(o, w_proj)
    unit2, _ = normed(m)
    n2 = (unit2 * gains[1:2]).astype(BF)
    e = nn(n2, w_fc1)
    cdf = 0.5 * (1.0 + lax.erf(e * (0.5**0.5)))
    g = (e * cdf).astype(BF)
    slope = cdf + e * jnp.exp(e * e * -0.5) * 0.3989422804014327
    return q.astype(BF), k.astype(BF), v.astype(BF), o, m, g, slope.astype(BF)


def backward(u, q, k, v, o, m, g, slope, cot, gains, w_qkv, w_proj, w_fc1, w_fc2, prob_ref, grad_ref, outs):
    qkv_ref, proj_ref, fc1_ref, fc2_ref, gain_ref = outs
    masks = head_masks()
    unit, scale = normed(u)
    n1 = (unit * gains[0:1]).astype(BF)
    unit2, scale2 = normed(m)
    n2 = (unit2 * gains[1:2]).astype(BF)
    y2 = cot.astype(BF)
    fc2_ref[...] = tn(y2, g).astype(fc2_ref.dtype)
    dg = nt(y2, w_fc2).astype(BF).astype(F32)
    y1 = (dg * slope.astype(F32)).astype(BF)
    fc1_ref[...] = tn(y1, n2).astype(fc1_ref.dtype)
    dn2 = nt(y1, w_fc1).astype(BF).astype(F32)
    gain_ref[1:2, :] = jnp.sum(dn2 * unit2, 0, keepdims=True)
    dm = cot + normed_back(dn2 * gains[1:2], unit2, scale2)
    yp = dm.astype(BF)
    proj_ref[...] = tn(yp, o).astype(proj_ref.dtype)
    do = nt(yp, w_proj).astype(BF)
    dqs, dks, dvs = [], [], []
    for n in range(2):
        part = slice(n * WIN, n * WIN + WIN)
        do_n, q_n, k_n, v_n = do[part], q[part], k[part], v[part]
        dp = nt(by_head(v_n, masks), do_n)
        dvs.append(from_heads(nn(prob_ref[n], do_n), masks))
        k_t = jnp.transpose(k_n.astype(F32)).astype(BF)
        ds_all, dq_t = [], []
        for h in range(HEADS):
            rows = slice(h * WIN, h * WIN + WIN)
            p = prob_ref[n, rows, :].astype(F32)
            dp_h = dp[rows].astype(BF).astype(F32)
            ds = p * (dp_h - jnp.sum(p * dp_h, 0, keepdims=True))
            if n == 0:
                grad_ref[0, rows, :] = ds[:, :128]
                grad_ref[1, rows, :16] = ds[:, 128:]
            else:
                grad_ref[0, rows, :] += ds[:, :128]
                grad_ref[1, rows, :16] += ds[:, 128:]
            ds = (ds * SCALE).astype(BF)
            ds_all.append(ds)
            dq_t.append(nn(k_t[h * HEAD : h * HEAD + HEAD], ds))
        dqs.append(jnp.transpose(jnp.concatenate(dq_t, axis=0)))
        dks.append(from_heads(nn(jnp.concatenate(ds_all, axis=0), q_n), masks))
    dn1 = jnp.zeros((TOK, DIM), F32)
    for i, parts in enumerate((dqs, dks, dvs)):
        d = jnp.concatenate(parts, axis=0).astype(BF)
        qkv_ref[i * DIM : i * DIM + DIM, :] = tn(d, n1).astype(qkv_ref.dtype)
        dn1 = dn1 + nt(d, w_qkv[:, i * DIM : i * DIM + DIM])
    dn1 = dn1.astype(BF).astype(F32)
    gain_ref[0:1, :] = jnp.sum(dn1 * unit, 0, keepdims=True)
    return dm + normed_back(dn1 * gains[0:1], unit, scale)


def flat_rows(ref):
    return jnp.concatenate([ref[z, i].astype(F32) for z in range(2) for i in range(6)], axis=0)


def first_kernel(state, cot, order, lanes, table, gains, w_qkv, w_proj, w_fc1, w_fc2,
                 out_ref, cot_ref, x_ref, q_ref, k_ref, v_ref, o_ref, m_ref, g_ref, slope_ref, prob_ref, bias_ref):
    perm = order[...]
    x = nn(perm, flat_rows(state).astype(BF))
    cot_ref[...] = nn(perm, flat_rows(cot).astype(BF)).astype(BF)
    x_ref[...] = x.astype(BF)
    expand_bias(table[...], lanes[...], False, bias_ref)
    q, k, v, o, m, g, slope = forward(
        x, gains[0], w_qkv[0], w_proj[0], w_fc1[0], w_fc2[0], bias_ref, None, prob_ref
    )
    out_ref[...] = (m + nn(g, w_fc2[0])).astype(BF)
    for ref, value in ((q_ref, q), (k_ref, k), (v_ref, v), (o_ref, o), (m_ref, m), (g_ref, g), (slope_ref, slope)):
        ref[...] = value


def second_kernel(last, u_ref, cot_ref, lanes, table, gains, w_qkv, w_proj, w_fc1, w_fc2,
                  du_ref, qkv_ref, proj_ref, fc1_ref, fc2_ref, gain_ref, table_ref, bias_ref, prob_ref, grad_ref):
    expand_bias(table[...], lanes[...], True, bias_ref)
    row = lax.broadcasted_iota(jnp.int32, (WIN, WIN), 0)
    lane = lax.broadcasted_iota(jnp.int32, (WIN, WIN), 1)
    same_z = (row % 6 // 3) == (lane % 6 // 3)
    same_h = (row // 72) == (lane // 72)
    allowed = same_z & (same_h | (jnp.full((WIN, WIN), last[0], jnp.int32) == 0))
    u = u_ref[...].astype(F32)
    weights = (w_qkv[0], w_proj[0], w_fc1[0], w_fc2[0])
    saved = forward(u, gains[0], *weights, bias_ref, allowed, prob_ref)
    grad_ref[...] = jnp.zeros_like(grad_ref)
    du_ref[...] = backward(
        u, *saved, cot_ref[...].astype(F32), gains[0], *weights, prob_ref, grad_ref,
        (qkv_ref, proj_ref, fc1_ref, fc2_ref, gain_ref),
    )
    table_ref[...] = reduce_bias(grad_ref, lanes[...], True)


def third_kernel(x_ref, q_ref, k_ref, v_ref, o_ref, m_ref, g_ref, slope_ref, prob_ref, cot_ref, order, lanes,
                 gains, w_qkv, w_proj, w_fc1, w_fc2,
                 du_ref, qkv_ref, proj_ref, fc1_ref, fc2_ref, gain_ref, table_ref, grad_ref):
    weights = (w_qkv[0], w_proj[0], w_fc1[0], w_fc2[0])
    grad_ref[...] = jnp.zeros_like(grad_ref)
    du = backward(
        x_ref[...].astype(F32), q_ref[...], k_ref[...], v_ref[...], o_ref[...], m_ref[...], g_ref[...],
        slope_ref[...], cot_ref[...], gains[0], *weights, prob_ref, grad_ref,
        (qkv_ref, proj_ref, fc1_ref, fc2_ref, gain_ref),
    )
    high, low = two_pieces(du)
    flat = tn(order[...], high) + tn(order[...], low)
    for z in range(2):
        for i in range(6):
            start = (z * 6 + i) * 24
            du_ref[z, i] = flat[start : start + 24]
    table_ref[...] = reduce_bias(grad_ref, lanes[...], False)


def whole(shape):
    return pl.BlockSpec(shape, lambda i: (0,) * len(shape))


def of_block(block, shape):
    return pl.BlockSpec((1,) + shape, lambda i: (block,) + (0,) * len(shape))


def weight_specs(block):
    return [
        of_block(block, (2, DIM)),
        of_block(block, (DIM, 3 * DIM)),
        of_block(block, (DIM, DIM)),
        of_block(block, (DIM, HID)),
        of_block(block, (HID, DIM)),
    ]


PARAMS = pltpu.CompilerParams(vmem_limit_bytes=48 * 1024 * 1024)
GRADS = (
    ((3 * DIM, DIM), BF),
    ((DIM, DIM), BF),
    ((HID, DIM), BF),
    ((DIM, HID), BF),
    ((2, DIM), F32),
    ((8, POS), F32),
)


def call(kernel, in_specs, outs, scratch, args):
    return pl.pallas_call(
        kernel,
        grid=(1,),
        in_specs=in_specs,
        out_specs=[whole(s) for s, _ in outs],
        out_shape=[jax.ShapeDtypeStruct(s, d) for s, d in outs],
        scratch_shapes=scratch,
        compiler_params=PARAMS,
    )(*args)


def first(state, cot, table, weights):
    full = (2, 6, 24, DIM)
    return call(
        first_kernel,
        [whole(full), whole(full), whole((TOK, TOK)), whole((276, 512)), whole((8, POS))] + weight_specs(0),
        [((TOK, DIM), BF)] * 6 + [((TOK, DIM), BF), ((TOK, DIM), F32), ((TOK, HID), BF), ((TOK, HID), BF),
         ((2, HEADS * WIN, WIN), BF)],
        [pltpu.VMEM((2, 8 * WIN, 128), F32)],
        (state, cot, token_order(), lane_order(), table) + weights,
    )


def second(last, u, cot, table, weights):
    return call(
        second_kernel,
        [pl.BlockSpec(memory_space=pltpu.SMEM), whole((TOK, DIM)), whole((TOK, DIM)), whole((276, 512)),
         whole((8, POS))] + weight_specs(1),
        [((TOK, DIM), F32)] + list(GRADS),
        [pltpu.VMEM((2, 8 * WIN, 128), F32), pltpu.VMEM((2, HEADS * WIN, WIN), BF), pltpu.VMEM((2, 8 * WIN, 128), F32)],
        (last, u, cot, lane_order(), table) + weights,
    )


def third(saved, cot, weights):
    return call(
        third_kernel,
        [whole((TOK, DIM))] * 6 + [whole((TOK, HID))] * 2 + [whole((2, HEADS * WIN, WIN)), whole((TOK, DIM)),
         whole((TOK, TOK)), whole((276, 512))] + weight_specs(0),
        [((2, 6, 24, DIM), F32)] + list(GRADS),
        [pltpu.VMEM((2, 8 * WIN, 128), F32)],
        tuple(saved) + (cot, token_order(), lane_order()) + weights,
    )


def from_behind(value, axis, steps):
    count = lax.axis_size(axis)
    pairs = [(source, (source + steps) % count) for source in range(count)]
    return lax.ppermute(value, axis, pairs)


def sent_and_summed(array, axis, dim):
    count = lax.axis_size(axis)
    dims = array.shape
    parts = array.reshape(*dims[:dim], count, dims[dim] // count, *dims[dim + 1 :])
    parts = lax.all_to_all(jnp.moveaxis(parts, dim, 0), axis, 0, 0, tiled=True)
    return jnp.sum(parts.astype(F32), axis=0)


def body(state, out_cot, qkv_weight, proj_weight, fc1_weight, fc2_weight, norm_gain, bias_table):
    weights = (norm_gain, qkv_weight, proj_weight, fc1_weight, fc2_weight)
    tables = jnp.pad(bias_table[:, 0, 0], ((0, 0), (0, 2), (0, 0)))
    one, cot, *saved = first(state, out_cot, tables[0], weights)
    paired = jnp.stack((one, cot)).reshape(2, 2, 2, 72, DIM)
    arrived = from_behind(paired[:, :, 0], LAT, -1)
    paired = jnp.stack((arrived, paired[:, :, 1]), 2)
    arrived = from_behind(paired[:, 0, :, :36], LON, -1)
    following = jnp.stack((paired[:, 1, :, :36], arrived), 1)
    paired = jnp.concatenate((paired[:, :, :, 36:], following), 3).reshape(2, TOK, DIM)
    last = (lax.axis_index(LAT) == lax.axis_size(LAT) - 1).astype(jnp.int32).reshape(1)
    du, *second_grads = second(last, paired[0], paired[1], tables[1], weights)
    du = du.reshape(2, 2, 72, DIM)
    arrived = from_behind(du[1, :, 36:].astype(BF), LON, 1).astype(F32)
    before = jnp.stack((arrived, du[0, :, 36:]))
    du = jnp.concatenate((before, du[:, :, :36]), 2)
    arrived = from_behind(du[:, 0].astype(BF), LAT, 1).astype(F32)
    du = jnp.stack((arrived, du[:, 1]), 1).reshape(TOK, DIM)
    state_grad, *first_grads = third(saved[:], du, weights)
    summed = []
    for i in range(4):
        both = jnp.stack((first_grads[i], second_grads[i]))
        both = lax.psum_scatter(both, LON, scatter_dimension=1, tiled=True)
        summed.append(jnp.swapaxes(sent_and_summed(both, LAT, 2), 1, 2))
    gain_grad = lax.psum(jnp.stack((first_grads[4], second_grads[4])), LAT_LON)
    table_grad = jnp.stack((first_grads[5], second_grads[5]))[:, None, None, :6].astype(BF)
    table_grad = sent_and_summed(table_grad, LON, 4)
    return (state_grad, *summed, gain_grad, table_grad)


def solution(mesh):
    split = Mesh(mesh.devices.reshape(8, 2, 4, 2, 2), ("lat_0", "lat_1", "lon_0", "lon_1", "lon_2"))
    placed = (
        P(None, LAT, LON, None),
        P(None, LAT, LON, None),
        P(),
        P(),
        P(),
        P(),
        P(),
        P(None, LAT, None, None, None),
    )
    return jax.shard_map(
        body,
        mesh=split,
        in_specs=placed,
        out_specs=(
            P(None, LAT, LON, None),
            P(None, LAT, LON),
            P(None, LAT, LON),
            P(None, LAT, LON),
            P(None, LAT, LON),
            P(),
            P(None, LAT, None, None, LON),
        ),
        check_vma=False,
    )
```

```python
import functools

import jax
import jax.numpy as jnp
import ml_dtypes
import numpy as np
from jax import lax
from jax.experimental import pallas as pl
from jax.experimental.pallas import tpu as pltpu
from jax.sharding import Mesh
from jax.sharding import PartitionSpec as P

WZ = 2
WH = 6
WW = 12
LAT = ("lat_0", "lat_1")
LON = ("lon_0", "lon_1", "lon_2")
LAT_LON = ("lat_0", "lat_1", "lon_0", "lon_1", "lon_2")
BF = jnp.bfloat16
F32 = jnp.float32
HEADS = 6
DIM = 192
HEAD = 32
WIN = 144
TOK = 288
HID = 768
POS = 3312
SCALE = HEAD**-0.5


def token_order():
    order = np.zeros((TOK, TOK), np.float32)
    row = 0
    for n in range(2):
        for ih in range(2):
            for w in range(WW):
                for z in range(2):
                    for il in range(3):
                        source = (z * 6 + ih * 3 + il) * 24 + n * WW + w
                        order[row, source] = 1
                        row += 1
    return order.astype(ml_dtypes.bfloat16)


def lane_order():
    order = np.zeros((276, 512), np.float32)
    for a in range(12):
        for d in range(23):
            order[a * 23 + d, (a // 6) * 256 + d * 6 + a % 6] = 1
    return order.astype(ml_dtypes.bfloat16)


def table_offsets(flip):
    offsets = {}
    for b in range(12):
        for a in range(12):
            hk, zk, lk = b // 6, b % 6 // 3, b % 3
            hq, zq, lq = a // 6, a % 6 // 3, a % 3
            if flip:
                hk, zk, hq, zq = 1 - hk, 1 - zk, 1 - hq, 1 - zq
            offsets[b, a] = (zq * 2 + zk) * 828 + ((hq * 3 + lq) * 6 + hk * 3 + lk) * 23
    return offsets


def nn(a, b):
    return lax.dot_general(a, b, (((1,), (0,)), ((), ())), preferred_element_type=F32)


def nt(a, b):
    return lax.dot_general(a, b, (((1,), (1,)), ((), ())), preferred_element_type=F32)


def tn(a, b):
    return lax.dot_general(a, b, (((0,), (0,)), ((), ())), preferred_element_type=F32)


def two_pieces(x):
    high = x.astype(BF)
    return high, (x - high.astype(F32)).astype(BF)


def three_pieces(x):
    high = x.astype(BF)
    rest = x - high.astype(F32)
    middle = rest.astype(BF)
    return high, middle, (rest - middle.astype(F32)).astype(BF)


def expand_bias(table, lanes, flip, bias_ref):
    offsets = table_offsets(flip)
    rows = []
    for b in range(12):
        rows.append(
            jnp.concatenate(
                [table[:, offsets[b, a] : offsets[b, a] + 23] for a in range(12)], axis=1
            )
        )
    stacked = jnp.concatenate(rows, axis=0)
    high, middle, low = three_pieces(stacked)
    spread = nn(high, lanes) + nn(middle, lanes) + nn(low, lanes)
    for b in range(12):
        block = spread[b * 8 : b * 8 + 8]
        for w in range(WW):
            start = (11 - w) * 6
            both = jnp.concatenate(
                (block[:, start : start + 72], block[:, 256 + start : 256 + start + 72]), axis=1
            )
            row = (b // 6) * 72 + w * 6 + b % 6
            right = jnp.concatenate((both[:, 128:], jnp.zeros((8, 112), F32)), axis=1)
            bias_ref[0, pl.ds(row, 8, stride=WIN), :] = both[:, :128]
            bias_ref[1, pl.ds(row, 8, stride=WIN), :] = right


def reduce_bias(grad_ref, lanes, flip):
    offsets = table_offsets(flip)
    rows = []
    for b in range(12):
        left = jnp.zeros((8, 256), F32)
        right = jnp.zeros((8, 256), F32)
        for w in range(WW):
            start = (11 - w) * 6
            row = (b // 6) * 72 + w * 6 + b % 6
            both = jnp.concatenate(
                (
                    grad_ref[0, pl.ds(row, 8, stride=WIN), :],
                    grad_ref[1, pl.ds(row, 8, stride=WIN), :][:, :16],
                ),
                axis=1,
            )
            left = left + jnp.pad(both[:, :72], ((0, 0), (start, 184 - start)))
            right = right + jnp.pad(both[:, 72:], ((0, 0), (start, 184 - start)))
        rows.append(jnp.concatenate((left, right), axis=1))
    stacked = jnp.concatenate(rows, axis=0)
    high, low = two_pieces(stacked)
    packed = nt(high, lanes) + nt(low, lanes)
    places = sorted((start, b, a) for (b, a), start in offsets.items())
    return jnp.concatenate(
        [packed[b * 8 : b * 8 + 8, a * 23 : a * 23 + 23] for _, b, a in places], axis=1
    )


def pack_chunks(qkv, proj, fc1, fc2, table, out_ref):
    table = jnp.concatenate((table, jnp.zeros((8, 256), F32)), axis=1)
    for b in range(16):
        rows = jnp.concatenate(
            [qkv[36 * b : 36 * b + 36], proj[12 * b : 12 * b + 12], fc1[48 * b : 48 * b + 48]]
            + [part[12 * b : 12 * b + 12] for part in fc2],
            axis=0,
        )
        right = rows[:, 128:]
        own = table[:, 207 * b : 207 * b + 207]
        own = jnp.concatenate((own, jnp.zeros((8, 49), F32)), axis=1)
        chunk = jnp.concatenate(
            (
                rows[:, :128],
                jnp.concatenate((right[:72], right[72:]), axis=1),
                own[:, :128],
                own[:, 128:],
                jnp.zeros((8, 128), F32),
            ),
            axis=0,
        )
        y, x, core = b // 4, b // 2 % 2, b % 2
        out_ref[core * 8 + y * 2 + x] = chunk.astype(BF)


def unpack_chunk(chunk):
    right = jnp.concatenate((chunk[144:216, :64], chunk[144:216, 64:]), axis=0)
    return jnp.concatenate((chunk[:144], right), axis=1)


def normed(u):
    mean = jnp.mean(u, -1, keepdims=True)
    centred = u - mean
    scale = lax.rsqrt(jnp.mean(centred * centred, -1, keepdims=True) + 1e-05)
    return centred * scale, scale


def normed_back(grad, unit, scale):
    mean = jnp.mean(grad, -1, keepdims=True)
    product = jnp.mean(grad * unit, -1, keepdims=True)
    return scale * (grad - mean - unit * product)


def head_masks():
    lane = lax.broadcasted_iota(jnp.int32, (1, DIM), 1) // HEAD
    return [(lane == h).astype(F32) for h in range(HEADS)]


def by_head(x, masks):
    return jnp.concatenate([x * m.astype(BF) for m in masks], axis=0)


def from_heads(x, masks):
    total = x[:WIN] * masks[0]
    for h in range(1, HEADS):
        total = total + x[h * WIN : h * WIN + WIN] * masks[h]
    return total


def forward(u, gains, w_qkv, w_proj, w_fc1, w_fc2, bias_ref, allowed, prob_ref):
    masks = head_masks()
    unit, _ = normed(u)
    n1 = (unit * gains[0:1]).astype(BF)
    q, k, v = (
        nn(n1, w_qkv[:, i * DIM : i * DIM + DIM]) for i in range(3)
    )
    joined = []
    for n in range(2):
        part = slice(n * WIN, n * WIN + WIN)
        scores = nt(by_head(k[part].astype(BF), masks), q[part].astype(BF))
        v_t = jnp.transpose(v[part]).astype(BF)
        out_t = []
        for h in range(HEADS):
            rows = slice(h * WIN, h * WIN + WIN)
            bias = jnp.concatenate((bias_ref[0, rows, :], bias_ref[1, rows, :16]), axis=1)
            s = scores[rows] * SCALE + bias
            if allowed is not None:
                s = jnp.where(allowed, s, -1e30)
            e = jnp.exp(s - jnp.max(s, 0, keepdims=True))
            p = (e * (1.0 / jnp.sum(e, 0, keepdims=True))).astype(BF)
            prob_ref[n, rows, :] = p
            out_t.append(nn(v_t[h * HEAD : h * HEAD + HEAD], p))
        joined.append(jnp.transpose(jnp.concatenate(out_t, axis=0)))
    o = jnp.concatenate(joined, axis=0).astype(BF)
    m = u + nn(o, w_proj)
    unit2, _ = normed(m)
    n2 = (unit2 * gains[1:2]).astype(BF)
    e = nn(n2, w_fc1)
    cdf = 0.5 * (1.0 + lax.erf(e * (0.5**0.5)))
    g = (e * cdf).astype(BF)
    slope = cdf + e * jnp.exp(e * e * -0.5) * 0.3989422804014327
    return q.astype(BF), k.astype(BF), v.astype(BF), o, m, g, slope.astype(BF)


def backward(u, q, k, v, o, m, g, slope, cot, gains, w_qkv, w_proj, w_fc1, w_fc2, lanes, flip, prob_ref, grad_ref, gain_ref, chunk_ref):
    grad_ref[...] = jnp.zeros_like(grad_ref)
    masks = head_masks()
    unit, scale = normed(u)
    n1 = (unit * gains[0:1]).astype(BF)
    unit2, scale2 = normed(m)
    n2 = (unit2 * gains[1:2]).astype(BF)
    y2 = cot.astype(BF)
    fc2 = [tn(y2, g[:, DIM * i : DIM * i + DIM]) for i in range(4)]
    dg = nt(y2, w_fc2).astype(BF).astype(F32)
    y1 = (dg * slope.astype(F32)).astype(BF)
    fc1 = tn(y1, n2)
    dn2 = nt(y1, w_fc1).astype(BF).astype(F32)
    gain_ref[1:2, :] = jnp.sum(dn2 * unit2, 0, keepdims=True)
    dm = cot + normed_back(dn2 * gains[1:2], unit2, scale2)
    yp = dm.astype(BF)
    proj = tn(yp, o)
    do = nt(yp, w_proj).astype(BF)
    dqs, dks, dvs = [], [], []
    for n in range(2):
        part = slice(n * WIN, n * WIN + WIN)
        do_n, q_n, k_n, v_n = do[part], q[part], k[part], v[part]
        dp = nt(by_head(v_n, masks), do_n)
        dvs.append(from_heads(nn(prob_ref[n], do_n), masks))
        k_t = jnp.transpose(k_n.astype(F32)).astype(BF)
        ds_all, dq_t = [], []
        for h in range(HEADS):
            rows = slice(h * WIN, h * WIN + WIN)
            p = prob_ref[n, rows, :].astype(F32)
            dp_h = dp[rows].astype(BF).astype(F32)
            ds = p * (dp_h - jnp.sum(p * dp_h, 0, keepdims=True))
            if n == 0:
                grad_ref[0, rows, :] = ds[:, :128]
                grad_ref[1, rows, :16] = ds[:, 128:]
            else:
                grad_ref[0, rows, :] += ds[:, :128]
                grad_ref[1, rows, :16] += ds[:, 128:]
            ds = (ds * SCALE).astype(BF)
            ds_all.append(ds)
            dq_t.append(nn(k_t[h * HEAD : h * HEAD + HEAD], ds))
        dqs.append(jnp.transpose(jnp.concatenate(dq_t, axis=0)))
        dks.append(from_heads(nn(jnp.concatenate(ds_all, axis=0), q_n), masks))
    dn1 = jnp.zeros((TOK, DIM), F32)
    qkv = []
    for i, parts in enumerate((dqs, dks, dvs)):
        d = jnp.concatenate(parts, axis=0).astype(BF)
        qkv.append(tn(d, n1))
        dn1 = dn1 + nt(d, w_qkv[:, i * DIM : i * DIM + DIM])
    dn1 = dn1.astype(BF).astype(F32)
    gain_ref[0:1, :] = jnp.sum(dn1 * unit, 0, keepdims=True)
    table = reduce_bias(grad_ref, lanes, flip)
    pack_chunks(jnp.concatenate(qkv, axis=0), proj, fc1, fc2, table, chunk_ref)
    return dm + normed_back(dn1 * gains[0:1], unit, scale)


def quarters(x):
    return {
        (n, ih, half): x[n * WIN + ih * 72 + half * 36 :][:36]
        for n in range(2)
        for ih in range(2)
        for half in range(2)
    }


def padded(pieces, rows):
    have = sum(p.shape[0] for p in pieces)
    return jnp.concatenate(list(pieces) + [jnp.zeros((rows - have, DIM), F32)], axis=0).astype(BF)


OWN = ((0, 1, 1), (1, 1, 0), (1, 1, 1))
BY_LAT = ((0, 0, 1), (1, 0, 0), (1, 0, 1))
BY_LON = ((0, 1, 0),)
BY_BOTH = ((0, 0, 0),)


def shifted(have):
    order = []
    for n in range(2):
        for ih in range(2):
            order += [(n, ih, 1), ((n + 1) % 2, ih, 0)]
    return jnp.concatenate([have[key] for key in order], axis=0)


def unshifted(x):
    have = {}
    row = 0
    for n in range(2):
        for ih in range(2):
            for key in ((n, ih, 1), ((n + 1) % 2, ih, 0)):
                have[key] = x[row : row + 36]
                row += 36
    return have


def whole_block(have):
    return jnp.concatenate(
        [have[n, ih, half] for n in range(2) for ih in range(2) for half in range(2)], axis=0
    )


def flat_rows(ref):
    return jnp.concatenate([ref[z, i].astype(F32) for z in range(2) for i in range(6)], axis=0)


def first_kernel(state, cot, order, lanes, table, gains, w_qkv, w_proj, w_fc1, w_fc2,
                 own_ref, lat_ref, lon_ref, both_ref,
                 x_ref, q_ref, k_ref, v_ref, o_ref, m_ref, g_ref, slope_ref, prob_ref, bias_ref):
    perm = order[...]
    x = nn(perm, flat_rows(state).astype(BF))
    cot_rows = nn(perm, flat_rows(cot).astype(BF))
    x_ref[...] = x.astype(BF)
    expand_bias(table[...], lanes[...], False, bias_ref)
    q, k, v, o, m, g, slope = forward(
        x, gains[0], w_qkv[0], w_proj[0], w_fc1[0], w_fc2[0], bias_ref, None, prob_ref
    )
    out = quarters(m + nn(g, w_fc2[0]))
    given = quarters(cot_rows)
    for ref, keys in ((own_ref, OWN), (lat_ref, BY_LAT), (lon_ref, BY_LON), (both_ref, BY_BOTH)):
        ref[...] = padded([out[key] for key in keys] + [given[key] for key in keys], ref.shape[0])
    for ref, value in ((q_ref, q), (k_ref, k), (v_ref, v), (o_ref, o), (m_ref, m), (g_ref, g), (slope_ref, slope)):
        ref[...] = value


def second_kernel(last, own_ref, lat_ref, lon_ref, both_ref, lanes, table, gains, w_qkv, w_proj, w_fc1, w_fc2,
                  mine_ref, to_lat_ref, to_lon_ref, to_both_ref, gain_ref, chunk_ref,
                  bias_ref, prob_ref, grad_ref):
    expand_bias(table[...], lanes[...], True, bias_ref)
    row = lax.broadcasted_iota(jnp.int32, (WIN, WIN), 0)
    lane = lax.broadcasted_iota(jnp.int32, (WIN, WIN), 1)
    same_z = (row % 6 // 3) == (lane % 6 // 3)
    same_h = (row // 72) == (lane // 72)
    allowed = same_z & (same_h | (jnp.full((WIN, WIN), last[0], jnp.int32) == 0))
    out, given = {}, {}
    for ref, keys in ((own_ref, OWN), (lat_ref, BY_LAT), (lon_ref, BY_LON), (both_ref, BY_BOTH)):
        rows = ref[...].astype(F32)
        for i, key in enumerate(keys):
            out[key] = rows[36 * i : 36 * i + 36]
            given[key] = rows[36 * (i + len(keys)) :][:36]
    u = shifted(out)
    weights = (w_qkv[0], w_proj[0], w_fc1[0], w_fc2[0])
    saved = forward(u, gains[0], *weights, bias_ref, allowed, prob_ref)
    du = backward(
        u, *saved, shifted(given), gains[0], *weights, lanes[...], True, prob_ref, grad_ref, gain_ref, chunk_ref
    )
    have = unshifted(du)
    mine_ref[...] = jnp.concatenate([have[key] for key in OWN] + [jnp.zeros((4, DIM), F32)], axis=0)
    for ref, keys in ((to_lat_ref, BY_LAT), (to_lon_ref, BY_LON), (to_both_ref, BY_BOTH)):
        ref[...] = padded([have[key] for key in keys], ref.shape[0])


def third_kernel(x_ref, q_ref, k_ref, v_ref, o_ref, m_ref, g_ref, slope_ref, prob_ref,
                 mine_ref, lat_ref, lon_ref, both_ref, order, lanes,
                 gains, w_qkv, w_proj, w_fc1, w_fc2,
                 du_ref, gain_ref, chunk_ref, grad_ref):
    weights = (w_qkv[0], w_proj[0], w_fc1[0], w_fc2[0])
    have = {}
    for ref, keys in ((mine_ref, OWN), (lat_ref, BY_LAT), (lon_ref, BY_LON), (both_ref, BY_BOTH)):
        rows = ref[...].astype(F32)
        for i, key in enumerate(keys):
            have[key] = rows[36 * i : 36 * i + 36]
    du = backward(
        x_ref[...].astype(F32), q_ref[...], k_ref[...], v_ref[...], o_ref[...], m_ref[...], g_ref[...],
        slope_ref[...], whole_block(have), gains[0], *weights, lanes[...], False, prob_ref, grad_ref,
        gain_ref, chunk_ref,
    )
    high, low = two_pieces(du)
    flat = tn(order[...], high) + tn(order[...], low)
    for z in range(2):
        for i in range(6):
            start = (z * 6 + i) * 24
            du_ref[z, i] = flat[start : start + 24]


MESH = pl.DeviceIdType.MESH


def ring(names):
    sizes = [lax.axis_size(name) for name in names]
    me = 0
    for name, size in zip(names, sizes):
        me = me * size + lax.axis_index(name)
    total = 1
    for size in sizes:
        total *= size

    def at(index):
        where = {}
        for name, size in reversed(list(zip(names, sizes))):
            where[name] = lax.rem(index, size)
            index = index // size
        return where

    return me, total, at


def greet(devices):
    barrier = pltpu.get_barrier_semaphore()
    for device in devices:
        pl.semaphore_signal(barrier, inc=1, device_id=device, device_id_type=MESH)
    pl.semaphore_wait(barrier, len(devices))


def halo_kernel(step, lat_in, lon_in, both_in, lat_out, lon_out, both_out, send_sem, recv_sem):
    lat_me, lat_count, lat_at = ring(LAT)
    lon_me, lon_count, lon_at = ring(LON)

    def neighbours(way):
        lat = lat_at(lax.rem(lat_me + way + lat_count, lat_count))
        lon = lon_at(lax.rem(lon_me + way + lon_count, lon_count))
        return lat, lon, {**lat, **lon}

    greet(neighbours(-step))
    copies = []
    targets = neighbours(step)
    for i, (source, target) in enumerate(((lat_in, lat_out), (lon_in, lon_out), (both_in, both_out))):
        copy = pltpu.make_async_remote_copy(
            src_ref=source, dst_ref=target, send_sem=send_sem.at[i], recv_sem=recv_sem.at[i],
            device_id=targets[i], device_id_type=MESH,
        )
        copy.start()
        copies.append(copy)
    for copy in copies:
        copy.wait()


def halo(arrays, step, collective_id):
    vmem = pl.BlockSpec(memory_space=pltpu.VMEM)
    return pl.pallas_call(
        functools.partial(halo_kernel, step),
        in_specs=[vmem] * 3,
        out_specs=[vmem] * 3,
        out_shape=[jax.ShapeDtypeStruct(a.shape, a.dtype) for a in arrays],
        scratch_shapes=[pltpu.SemaphoreType.DMA((3,)), pltpu.SemaphoreType.DMA((3,))],
        compiler_params=pltpu.CompilerParams(collective_id=collective_id, has_side_effects=True),
    )(*arrays)


def reduce_kernel(first_w, second_w, first_g, second_g,
                  qkv_ref, proj_ref, fc1_ref, fc2_ref, gain_ref, table_ref,
                  got_a, sum_a, got_b, sum_b, got_c, sent_d, got_d,
                  gain_s, gain_a, gain_b, gain_c, gain_d,
                  send_a, recv_a, send_b, recv_b, send_c, recv_c, send_d, recv_d):
    core = lax.axis_index("lon_2")
    side = lax.axis_index("lon_1")
    y, y_count = lax.axis_index("lon_0"), lax.axis_size("lon_0")
    lat_me, lat_count, lat_at = ring(LAT)
    core_peer = {"lon_2": 1 - core}
    side_peer = {"lon_1": 1 - side}

    def y_peer(o):
        return lax.rem(y + o, y_count)

    def lat_peer(o):
        return lax.rem(lat_me + o, lat_count)

    greet(
        [core_peer, side_peer]
        + [{"lon_0": y_peer(o)} for o in range(1, y_count)]
        + [lat_at(lat_peer(o)) for o in range(1, lat_count)]
    )

    def send(source, target, sems, i, device):
        copy = pltpu.make_async_remote_copy(
            src_ref=source, dst_ref=target, send_sem=sems[0].at[i], recv_sem=sems[1].at[i],
            device_id=device, device_id_type=MESH,
        )
        copy.start()
        return copy

    parts = (second_w, first_w)
    flights_a = [
        send(w.at[pl.ds((1 - core) * 8, 8)], got_a.at[i], (send_a, recv_a), i, core_peer)
        for i, w in enumerate(parts)
    ]
    pad = jnp.zeros((2, 64), F32)
    gain_s[0] = jnp.concatenate(
        (
            jnp.concatenate((first_g[...], pad), axis=1),
            jnp.concatenate((second_g[...], pad), axis=1),
            jnp.zeros((4, 256), F32),
        ),
        axis=0,
    )
    flights_a.append(send(gain_s.at[0], gain_a, (send_a, recv_a), 2, core_peer))
    flights_b = []
    for i, w in enumerate(parts):
        flights_a[i].wait()
        sum_a[i] = (w[pl.ds(core * 8, 8)].astype(F32) + got_a[i].astype(F32)).astype(BF)
        for o in range(1, y_count):
            flights_b.append(
                send(sum_a.at[i, pl.ds(y_peer(o) * 2, 2)], got_b.at[i, y], (send_b, recv_b),
                     i * (y_count - 1) + o - 1, {"lon_0": y_peer(o)})
            )
        got_b[i, pl.ds(y, 1)] = sum_a[i, pl.ds(y * 2, 2)][None]
    flights_a[2].wait()
    gain_s[1] = gain_s[0] + gain_a[...]
    for o in range(1, y_count):
        flights_b.append(
            send(gain_s.at[1], gain_b.at[y], (send_b, recv_b), 2 * (y_count - 1) + o - 1, {"lon_0": y_peer(o)})
        )
    gain_b[pl.ds(y, 1)] = gain_s[pl.ds(1, 1)]
    flights_c = []
    for i in range(3):
        for flight in flights_b[i * (y_count - 1) : (i + 1) * (y_count - 1)]:
            flight.wait()
        if i < 2:
            total = got_b[i, 0].astype(F32)
            for o in range(1, y_count):
                total = total + got_b[i, o].astype(F32)
            sum_b[i] = total.astype(BF)
            flights_c.append(send(sum_b.at[i, 1 - side], got_c.at[i], (send_c, recv_c), i, side_peer))
        else:
            total = gain_b[0]
            for o in range(1, y_count):
                total = total + gain_b[o]
            gain_s[2] = total
            flights_c.append(send(gain_s.at[2], gain_c, (send_c, recv_c), 2, side_peer))
    rows = [None, None]
    for i in range(2):
        flights_c[i].wait()
        chunk = sum_b[i, pl.ds(side, 1)][0].astype(F32) + got_c[i].astype(F32)
        table_ref[1 - i] = jnp.concatenate((chunk[216:224], chunk[224:232]), axis=1)[:6, :207]
        rows[1 - i] = unpack_chunk(chunk)
    across = jnp.concatenate([jnp.transpose(x[:96]) for x in rows], axis=1)
    for a in range(16):
        down, right = 96 + 12 * (a // 4), 48 * (a % 4)
        piece = jnp.concatenate(
            [across[12 * a : 12 * a + 12]]
            + [x[down : down + 12, right : right + 48] for x in rows]
            + [jnp.zeros((12, 96), F32)],
            axis=1,
        )
        sent_d[a] = jnp.concatenate((piece, jnp.zeros((4, 384), F32)), axis=0).astype(BF)
    flights_d = [
        send(sent_d.at[lat_peer(o)], got_d.at[lat_me], (send_d, recv_d), o - 1, lat_at(lat_peer(o)))
        for o in range(1, lat_count)
    ]
    flights_c[2].wait()
    gain_s[3] = gain_s[2] + gain_c[...]
    flights_d += [
        send(gain_s.at[3], gain_d.at[lat_me], (send_d, recv_d), lat_count - 2 + o, lat_at(lat_peer(o)))
        for o in range(1, lat_count)
    ]
    got_d[pl.ds(lat_me, 1)] = sent_d[pl.ds(lat_me, 1)]
    gain_d[pl.ds(lat_me, 1)] = gain_s[pl.ds(3, 1)]
    for flight in flights_d:
        flight.wait()
    total = jnp.sum(got_d[...].astype(F32), axis=0)
    turned = jnp.transpose(total[:, 192:288])
    for i in range(2):
        qkv_ref[i] = total[:12, 96 * i : 96 * i + 36]
        proj_ref[i] = total[:12, 96 * i + 36 : 96 * i + 48]
        fc1_ref[i] = total[:12, 96 * i + 48 : 96 * i + 96]
        fc2_ref[i] = turned[48 * i : 48 * i + 48, :12]
    gains = gain_d[0]
    for o in range(1, lat_count):
        gains = gains + gain_d[o]
    for i in range(2):
        gain_ref[i] = gains[2 * i : 2 * i + 2, :DIM]


def reduce_all(first_w, second_w, first_g, second_g):
    vmem = pl.BlockSpec(memory_space=pltpu.VMEM)
    dma = pltpu.SemaphoreType.DMA
    shapes = ((2, 12, 36), (2, 12, 12), (2, 12, 48), (2, 48, 12), (2, 2, DIM), (2, 6, 207))
    return pl.pallas_call(
        reduce_kernel,
        in_specs=[vmem] * 4,
        out_specs=[vmem] * 6,
        out_shape=[jax.ShapeDtypeStruct(s, F32) for s in shapes],
        scratch_shapes=[
            pltpu.VMEM((2, 8, 240, 128), BF),
            pltpu.VMEM((2, 8, 240, 128), BF),
            pltpu.VMEM((2, 4, 2, 240, 128), BF),
            pltpu.VMEM((2, 2, 240, 128), BF),
            pltpu.VMEM((2, 240, 128), BF),
            pltpu.VMEM((16, 16, 384), BF),
            pltpu.VMEM((16, 16, 384), BF),
            pltpu.VMEM((4, 8, 256), F32),
            pltpu.VMEM((8, 256), F32),
            pltpu.VMEM((4, 8, 256), F32),
            pltpu.VMEM((8, 256), F32),
            pltpu.VMEM((16, 8, 256), F32),
            dma((3,)), dma((3,)), dma((9,)), dma((9,)), dma((3,)), dma((3,)), dma((30,)), dma((30,)),
        ],
        compiler_params=pltpu.CompilerParams(
            collective_id=2, has_side_effects=True, vmem_limit_bytes=48 * 1024 * 1024
        ),
    )(first_w, second_w, first_g, second_g)


def whole(shape):
    return pl.BlockSpec(shape, lambda i: (0,) * len(shape))


def of_block(block, shape):
    return pl.BlockSpec((1,) + shape, lambda i: (block,) + (0,) * len(shape))


def weight_specs(block):
    return [
        of_block(block, (2, DIM)),
        of_block(block, (DIM, 3 * DIM)),
        of_block(block, (DIM, DIM)),
        of_block(block, (DIM, HID)),
        of_block(block, (HID, DIM)),
    ]


PARAMS = pltpu.CompilerParams(vmem_limit_bytes=48 * 1024 * 1024)
GRADS = [((2, DIM), F32), ((16, 240, 128), BF)]
SENT = [((112, DIM), BF), ((48, DIM), BF), ((48, DIM), BF)]


def call(kernel, in_specs, outs, scratch, args):
    return pl.pallas_call(
        kernel,
        grid=(1,),
        in_specs=in_specs,
        out_specs=[whole(s) for s, _ in outs],
        out_shape=[jax.ShapeDtypeStruct(s, d) for s, d in outs],
        scratch_shapes=scratch,
        compiler_params=PARAMS,
    )(*args)


def first(state, cot, table, weights):
    full = (2, 6, 24, DIM)
    return call(
        first_kernel,
        [whole(full), whole(full), whole((TOK, TOK)), whole((276, 512)), whole((8, POS))] + weight_specs(0),
        [((224, DIM), BF), ((224, DIM), BF), ((80, DIM), BF), ((80, DIM), BF)] + [((TOK, DIM), BF)] * 5
        + [((TOK, DIM), F32), ((TOK, HID), BF), ((TOK, HID), BF), ((2, HEADS * WIN, WIN), BF)],
        [pltpu.VMEM((2, 8 * WIN, 128), F32)],
        (state, cot, token_order(), lane_order(), table) + weights,
    )


def second(last, pieces, table, weights):
    return call(
        second_kernel,
        [pl.BlockSpec(memory_space=pltpu.SMEM)] + [whole(p.shape) for p in pieces]
        + [whole((276, 512)), whole((8, POS))] + weight_specs(1),
        [((112, DIM), F32)] + SENT + GRADS,
        [pltpu.VMEM((2, 8 * WIN, 128), F32), pltpu.VMEM((2, HEADS * WIN, WIN), BF),
         pltpu.VMEM((2, 8 * WIN, 128), F32)],
        (last, *pieces, lane_order(), table) + weights,
    )


def third(saved, pieces, weights):
    return call(
        third_kernel,
        [whole(a.shape) for a in (*saved, *pieces)] + [whole((TOK, TOK)), whole((276, 512))] + weight_specs(0),
        [((2, 6, 24, DIM), F32)] + GRADS,
        [pltpu.VMEM((2, 8 * WIN, 128), F32)],
        (*saved, *pieces, token_order(), lane_order()) + weights,
    )


def body(state, out_cot, qkv_weight, proj_weight, fc1_weight, fc2_weight, norm_gain, bias_table):
    weights = (norm_gain, qkv_weight, proj_weight, fc1_weight, fc2_weight)
    tables = jnp.pad(bias_table[:, 0, 0], ((0, 0), (0, 2), (0, 0)))
    own, *leaving, = first(state, out_cot, tables[0], weights)
    leaving, saved = leaving[:3], leaving[3:]
    arrived = halo(leaving, -1, 0)
    last = (lax.axis_index(LAT) == lax.axis_size(LAT) - 1).astype(jnp.int32).reshape(1)
    mine, *leaving = second(last, (own, *arrived), tables[1], weights)
    leaving, second_grads = leaving[:3], leaving[3:]
    arrived = halo(leaving, 1, 1)
    state_grad, *first_grads = third(saved, (mine, *arrived), weights)
    *summed, table_grad = reduce_all(first_grads[1], second_grads[1], first_grads[0], second_grads[0])
    return (state_grad, *summed, table_grad[:, None, None])


def solution(mesh):
    split = Mesh(mesh.devices.reshape(8, 2, 4, 2, 2), ("lat_0", "lat_1", "lon_0", "lon_1", "lon_2"))
    placed = (
        P(None, LAT, LON, None),
        P(None, LAT, LON, None),
        P(),
        P(),
        P(),
        P(),
        P(),
        P(None, LAT, None, None, None),
    )
    return jax.shard_map(
        body,
        mesh=split,
        in_specs=placed,
        out_specs=(
            P(None, LAT, LON, None),
            P(None, LAT, LON),
            P(None, LAT, LON),
            P(None, LAT, LON),
            P(None, LAT, LON),
            P(),
            P(None, LAT, None, None, LON),
        ),
        check_vma=False,
    )
```

```python
import jax
import jax.numpy as jnp
import ml_dtypes
import numpy as np
from jax import lax
from jax.experimental import pallas as pl
from jax.experimental.pallas import tpu as pltpu
from jax.sharding import Mesh
from jax.sharding import PartitionSpec as P

WZ = 2
WH = 6
WW = 12
LAT = ("lat_0", "lat_1")
LON = ("lon_0", "lon_1", "lon_2")
BF = jnp.bfloat16
F32 = jnp.float32
HEADS = 6
DIM = 192
HEAD = 32
WIN = 144
TOK = 288
HID = 768
POS = 3312
SCALE = HEAD**-0.5


def token_order():
    order = np.zeros((TOK, TOK), np.float32)
    row = 0
    for n in range(2):
        for ih in range(2):
            for w in range(WW):
                for z in range(2):
                    for il in range(3):
                        source = (z * 6 + ih * 3 + il) * 24 + n * WW + w
                        order[row, source] = 1
                        row += 1
    return order.astype(ml_dtypes.bfloat16)


def lane_order():
    order = np.zeros((276, 512), np.float32)
    for a in range(12):
        for d in range(23):
            order[a * 23 + d, (a // 6) * 256 + d * 6 + a % 6] = 1
    return order.astype(ml_dtypes.bfloat16)


def table_offsets(flip):
    offsets = {}
    for b in range(12):
        for a in range(12):
            hk, zk, lk = b // 6, b % 6 // 3, b % 3
            hq, zq, lq = a // 6, a % 6 // 3, a % 3
            if flip:
                hk, zk, hq, zq = 1 - hk, 1 - zk, 1 - hq, 1 - zq
            offsets[b, a] = (zq * 2 + zk) * 828 + ((hq * 3 + lq) * 6 + hk * 3 + lk) * 23
    return offsets


def nn(a, b):
    return lax.dot_general(a, b, (((1,), (0,)), ((), ())), preferred_element_type=F32)


def nt(a, b):
    return lax.dot_general(a, b, (((1,), (1,)), ((), ())), preferred_element_type=F32)


def tn(a, b):
    return lax.dot_general(a, b, (((0,), (0,)), ((), ())), preferred_element_type=F32)


def two_pieces(x):
    high = x.astype(BF)
    return high, (x - high.astype(F32)).astype(BF)


def three_pieces(x):
    high = x.astype(BF)
    rest = x - high.astype(F32)
    middle = rest.astype(BF)
    return high, middle, (rest - middle.astype(F32)).astype(BF)


def expand_bias(table, lanes, flip, bias_ref):
    offsets = table_offsets(flip)
    rows = []
    for b in range(12):
        rows.append(
            jnp.concatenate(
                [table[:, offsets[b, a] : offsets[b, a] + 23] for a in range(12)], axis=1
            )
        )
    stacked = jnp.concatenate(rows, axis=0)
    high, middle, low = three_pieces(stacked)
    spread = nn(high, lanes) + nn(middle, lanes) + nn(low, lanes)
    for b in range(12):
        block = spread[b * 8 : b * 8 + 8]
        for w in range(WW):
            start = (11 - w) * 6
            both = jnp.concatenate(
                (block[:, start : start + 72], block[:, 256 + start : 256 + start + 72]), axis=1
            )
            row = (b // 6) * 72 + w * 6 + b % 6
            right = jnp.concatenate((both[:, 128:], jnp.zeros((8, 112), F32)), axis=1)
            bias_ref[0, pl.ds(row, 8, stride=WIN), :] = both[:, :128]
            bias_ref[1, pl.ds(row, 8, stride=WIN), :] = right


def reduce_bias(grad_ref, lanes, flip):
    offsets = table_offsets(flip)
    rows = []
    for b in range(12):
        left = jnp.zeros((8, 256), F32)
        right = jnp.zeros((8, 256), F32)
        for w in range(WW):
            start = (11 - w) * 6
            row = (b // 6) * 72 + w * 6 + b % 6
            both = jnp.concatenate(
                (
                    grad_ref[0, pl.ds(row, 8, stride=WIN), :],
                    grad_ref[1, pl.ds(row, 8, stride=WIN), :][:, :16],
                ),
                axis=1,
            )
            left = left + jnp.pad(both[:, :72], ((0, 0), (start, 184 - start)))
            right = right + jnp.pad(both[:, 72:], ((0, 0), (start, 184 - start)))
        rows.append(jnp.concatenate((left, right), axis=1))
    stacked = jnp.concatenate(rows, axis=0)
    high, low = two_pieces(stacked)
    packed = nt(high, lanes) + nt(low, lanes)
    places = sorted((start, b, a) for (b, a), start in offsets.items())
    return jnp.concatenate(
        [packed[b * 8 : b * 8 + 8, a * 23 : a * 23 + 23] for _, b, a in places], axis=1
    )


def pack_chunks(qkv, proj, fc1, fc2, table, out_ref):
    table = jnp.concatenate((table, jnp.zeros((8, 256), F32)), axis=1)
    for b in range(16):
        rows = jnp.concatenate(
            [qkv[36 * b : 36 * b + 36], proj[12 * b : 12 * b + 12], fc1[48 * b : 48 * b + 48]]
            + [part[12 * b : 12 * b + 12] for part in fc2],
            axis=0,
        )
        right = rows[:, 128:]
        own = table[:, 207 * b : 207 * b + 207]
        own = jnp.concatenate((own, jnp.zeros((8, 49), F32)), axis=1)
        chunk = jnp.concatenate(
            (
                rows[:, :128],
                jnp.concatenate((right[:72], right[72:]), axis=1),
                own[:, :128],
                own[:, 128:],
                jnp.zeros((8, 128), F32),
            ),
            axis=0,
        )
        y, x, core = b // 4, b // 2 % 2, b % 2
        out_ref[core * 8 + y * 2 + x] = chunk.astype(BF)


def unpack_chunk(chunk):
    right = jnp.concatenate((chunk[144:216, :64], chunk[144:216, 64:]), axis=0)
    return jnp.concatenate((chunk[:144], right), axis=1)


def normed(u):
    mean = jnp.mean(u, -1, keepdims=True)
    centred = u - mean
    scale = lax.rsqrt(jnp.mean(centred * centred, -1, keepdims=True) + 1e-05)
    return centred * scale, scale


def normed_back(grad, unit, scale):
    mean = jnp.mean(grad, -1, keepdims=True)
    product = jnp.mean(grad * unit, -1, keepdims=True)
    return scale * (grad - mean - unit * product)


def head_masks():
    lane = lax.broadcasted_iota(jnp.int32, (1, DIM), 1) // HEAD
    return [(lane == h).astype(F32) for h in range(HEADS)]


def by_head(x, masks):
    return jnp.concatenate([x * m.astype(BF) for m in masks], axis=0)


def from_heads(x, masks):
    total = x[:WIN] * masks[0]
    for h in range(1, HEADS):
        total = total + x[h * WIN : h * WIN + WIN] * masks[h]
    return total


def forward(u, gains, w_qkv, w_proj, w_fc1, w_fc2, bias_ref, allowed, prob_ref):
    masks = head_masks()
    unit, _ = normed(u)
    n1 = (unit * gains[0:1]).astype(BF)
    q, k, v = (
        nn(n1, w_qkv[:, i * DIM : i * DIM + DIM]) for i in range(3)
    )
    joined = []
    for n in range(2):
        part = slice(n * WIN, n * WIN + WIN)
        scores = nt(by_head(k[part].astype(BF), masks), q[part].astype(BF))
        v_t = jnp.transpose(v[part]).astype(BF)
        out_t = []
        for h in range(HEADS):
            rows = slice(h * WIN, h * WIN + WIN)
            bias = jnp.concatenate((bias_ref[0, rows, :], bias_ref[1, rows, :16]), axis=1)
            s = scores[rows] * SCALE + bias
            if allowed is not None:
                s = jnp.where(allowed, s, -1e30)
            e = jnp.exp(s - jnp.max(s, 0, keepdims=True))
            p = (e * (1.0 / jnp.sum(e, 0, keepdims=True))).astype(BF)
            prob_ref[n, rows, :] = p
            out_t.append(nn(v_t[h * HEAD : h * HEAD + HEAD], p))
        joined.append(jnp.transpose(jnp.concatenate(out_t, axis=0)))
    o = jnp.concatenate(joined, axis=0).astype(BF)
    m = u + nn(o, w_proj)
    unit2, _ = normed(m)
    n2 = (unit2 * gains[1:2]).astype(BF)
    e = nn(n2, w_fc1)
    cdf = 0.5 * (1.0 + lax.erf(e * (0.5**0.5)))
    g = (e * cdf).astype(BF)
    slope = cdf + e * jnp.exp(e * e * -0.5) * 0.3989422804014327
    return q.astype(BF), k.astype(BF), v.astype(BF), o, m, g, slope.astype(BF)


def backward(u, q, k, v, o, m, g, slope, cot, gains, w_qkv, w_proj, w_fc1, w_fc2, lanes, flip, prob_ref, grad_ref, gain_ref, chunk_ref,
             meanwhile=None):
    grad_ref[...] = jnp.zeros_like(grad_ref)
    masks = head_masks()
    unit, scale = normed(u)
    n1 = (unit * gains[0:1]).astype(BF)
    unit2, scale2 = normed(m)
    n2 = (unit2 * gains[1:2]).astype(BF)
    y2 = cot.astype(BF)
    fc2 = [tn(y2, g[:, DIM * i : DIM * i + DIM]) for i in range(4)]
    dg = nn(y2, w_fc2).astype(BF).astype(F32)
    y1 = (dg * slope.astype(F32)).astype(BF)
    fc1 = tn(y1, n2)
    dn2 = nt(y1, w_fc1).astype(BF).astype(F32)
    gain_ref[1:2, :] = jnp.sum(dn2 * unit2, 0, keepdims=True)
    dm = cot + normed_back(dn2 * gains[1:2], unit2, scale2)
    yp = dm.astype(BF)
    proj = tn(yp, o)
    do = nt(yp, w_proj).astype(BF)
    if meanwhile is not None:
        meanwhile()
    dqs, dks, dvs = [], [], []
    for n in range(2):
        part = slice(n * WIN, n * WIN + WIN)
        do_n, q_n, k_n, v_n = do[part], q[part], k[part], v[part]
        dp = nt(by_head(v_n, masks), do_n)
        dvs.append(from_heads(nn(prob_ref[n], do_n), masks))
        k_t = jnp.transpose(k_n.astype(F32)).astype(BF)
        ds_all, dq_t = [], []
        for h in range(HEADS):
            rows = slice(h * WIN, h * WIN + WIN)
            p = prob_ref[n, rows, :].astype(F32)
            dp_h = dp[rows].astype(BF).astype(F32)
            ds = p * (dp_h - jnp.sum(p * dp_h, 0, keepdims=True))
            if n == 0:
                grad_ref[0, rows, :] = ds[:, :128]
                grad_ref[1, rows, :16] = ds[:, 128:]
            else:
                grad_ref[0, rows, :] += ds[:, :128]
                grad_ref[1, rows, :16] += ds[:, 128:]
            ds = (ds * SCALE).astype(BF)
            ds_all.append(ds)
            dq_t.append(nn(k_t[h * HEAD : h * HEAD + HEAD], ds))
        dqs.append(jnp.transpose(jnp.concatenate(dq_t, axis=0)))
        dks.append(from_heads(nn(jnp.concatenate(ds_all, axis=0), q_n), masks))
    dn1 = jnp.zeros((TOK, DIM), F32)
    qkv = []
    for i, parts in enumerate((dqs, dks, dvs)):
        d = jnp.concatenate(parts, axis=0).astype(BF)
        qkv.append(tn(d, n1))
        dn1 = dn1 + nt(d, w_qkv[:, i * DIM : i * DIM + DIM])
    dn1 = dn1.astype(BF).astype(F32)
    gain_ref[0:1, :] = jnp.sum(dn1 * unit, 0, keepdims=True)
    table = reduce_bias(grad_ref, lanes, flip)
    pack_chunks(jnp.concatenate(qkv, axis=0), proj, fc1, fc2, table, chunk_ref)
    return dm + normed_back(dn1 * gains[0:1], unit, scale)


def quarters(x):
    return {
        (n, ih, half): x[n * WIN + ih * 72 + half * 36 :][:36]
        for n in range(2)
        for ih in range(2)
        for half in range(2)
    }


def padded(pieces, rows):
    have = sum(p.shape[0] for p in pieces)
    return jnp.concatenate(list(pieces) + [jnp.zeros((rows - have, DIM), F32)], axis=0).astype(BF)


OWN = ((0, 1, 1), (1, 1, 0), (1, 1, 1))
BY_LAT = ((0, 0, 1), (1, 0, 0), (1, 0, 1))
BY_LON = ((0, 1, 0),)
BY_BOTH = ((0, 0, 0),)


def shifted(have):
    order = []
    for n in range(2):
        for ih in range(2):
            order += [(n, ih, 1), ((n + 1) % 2, ih, 0)]
    return jnp.concatenate([have[key] for key in order], axis=0)


def unshifted(x):
    have = {}
    row = 0
    for n in range(2):
        for ih in range(2):
            for key in ((n, ih, 1), ((n + 1) % 2, ih, 0)):
                have[key] = x[row : row + 36]
                row += 36
    return have


def whole_block(have):
    return jnp.concatenate(
        [have[n, ih, half] for n in range(2) for ih in range(2) for half in range(2)], axis=0
    )


def flat_rows(ref):
    return jnp.concatenate([ref[z, i].astype(F32) for z in range(2) for i in range(6)], axis=0)


MESH = pl.DeviceIdType.MESH


def ring(names):
    sizes = [lax.axis_size(name) for name in names]
    me = 0
    for name, size in zip(names, sizes):
        me = me * size + lax.axis_index(name)
    total = 1
    for size in sizes:
        total *= size

    def at(index):
        where = {}
        for name, size in reversed(list(zip(names, sizes))):
            where[name] = lax.rem(index, size)
            index = index // size
        return where

    return me, total, at


def kernel(state_in, cot_in, order_in, lanes_in, table_in, gains_in, w_qkv_in, w_proj_in, w_fc1_in, w_fc2_in,
           du_ref, qkv_ref, proj_ref, fc1_ref, fc2_ref, gain_ref, table_ref,
           state, cot, order, lanes, table, gains, w_qkv, w_proj, w_fc1, w_fc2,
           q_ref, k_ref, v_ref, o_ref, m_ref, g_ref, slope_ref, prob_first, prob_second, bias_ref, grad_ref, mine_ref,
           own_ref, out_lat, out_lon, out_both, in_lat, in_lon, in_both,
           back_lat, back_lon, back_both, home_lat, home_lon, home_both,
           chunk_first, chunk_second, gain_first, gain_second,
           got_a, sum_a, got_b, sum_b, got_c, sent_d, got_d,
           gain_s, gain_a, gain_b, gain_c, gain_d,
           load, send_h, recv_h, send_a, recv_a, send_b, recv_b, send_c, recv_c, send_d, recv_d):
    loads = [
        pltpu.make_async_copy(source, target, load.at[i])
        for i, (source, target) in enumerate(
            (
                (order_in, order),
                (state_in, state),
                (cot_in, cot),
                (table_in, table),
                (lanes_in, lanes),
                (gains_in, gains),
                (w_qkv_in, w_qkv),
                (w_proj_in, w_proj),
                (w_fc1_in, w_fc1),
                (w_fc2_in, w_fc2),
            )
        )
    ]
    for copy in loads:
        copy.start()
    core = lax.axis_index("lon_2")
    side = lax.axis_index("lon_1")
    y, y_count = lax.axis_index("lon_0"), lax.axis_size("lon_0")
    lat_me, lat_count, lat_at = ring(LAT)
    lon_me, lon_count, lon_at = ring(LON)
    core_peer = {"lon_2": 1 - core}
    side_peer = {"lon_1": 1 - side}

    def y_peer(o):
        return lax.rem(y + o, y_count)

    def lat_peer(o):
        return lax.rem(lat_me + o, lat_count)

    def neighbours(way):
        lat = lat_at(lax.rem(lat_me + way + lat_count, lat_count))
        lon = lon_at(lax.rem(lon_me + way + lon_count, lon_count))
        return lat, lon, {**lat, **lon}

    lower, upper = neighbours(-1), neighbours(1)
    peers = (
        [*lower, *upper, core_peer, side_peer]
        + [{"lon_0": y_peer(o)} for o in range(1, y_count)]
        + [lat_at(lat_peer(o)) for o in range(1, lat_count)]
    )
    barrier = pltpu.get_barrier_semaphore()
    for device in peers:
        pl.semaphore_signal(barrier, inc=1, device_id=device, device_id_type=MESH)

    def send(source, target, sems, i, device):
        copy = pltpu.make_async_remote_copy(
            src_ref=source, dst_ref=target, send_sem=sems[0].at[i], recv_sem=sems[1].at[i],
            device_id=device, device_id_type=MESH,
        )
        copy.start()
        return copy

    def table_of(block):
        return jnp.concatenate([table[block, h] for h in range(HEADS)] + [jnp.zeros((2, POS), F32)], axis=0)

    for copy in loads:
        copy.wait()
    perm = order[...]
    x = nn(perm, flat_rows(state).astype(BF))
    cot_rows = nn(perm, flat_rows(cot).astype(BF))
    expand_bias(table_of(0), lanes[...], False, bias_ref)
    first_weights = (w_qkv[0], w_proj[0], w_fc1[0], w_fc2[0])
    q, k, v, o, m, g, slope = forward(x, gains[0], *first_weights, bias_ref, None, prob_first)
    out = quarters(m + nt(g, w_fc2[0]))
    given = quarters(cot_rows)
    for ref, keys in ((own_ref, OWN), (out_lat, BY_LAT), (out_lon, BY_LON), (out_both, BY_BOTH)):
        ref[...] = padded([out[key] for key in keys] + [given[key] for key in keys], ref.shape[0])
    pl.semaphore_wait(barrier, len(peers))
    flights = [
        send(source, target, (send_h, recv_h), i, lower[i])
        for i, (source, target) in enumerate(((out_lat, in_lat), (out_lon, in_lon), (out_both, in_both)))
    ]
    for ref, value in ((q_ref, q), (k_ref, k), (v_ref, v), (o_ref, o), (m_ref, m), (g_ref, g), (slope_ref, slope)):
        ref[...] = value

    expand_bias(table_of(1), lanes[...], True, bias_ref)
    row = lax.broadcasted_iota(jnp.int32, (WIN, WIN), 0)
    lane = lax.broadcasted_iota(jnp.int32, (WIN, WIN), 1)
    same_z = (row % 6 // 3) == (lane % 6 // 3)
    same_h = (row // 72) == (lane // 72)
    allowed = same_z & (same_h | (jnp.full((WIN, WIN), lat_me, jnp.int32) < lat_count - 1))
    for flight in flights:
        flight.wait()
    out, given = {}, {}
    for ref, keys in ((own_ref, OWN), (in_lat, BY_LAT), (in_lon, BY_LON), (in_both, BY_BOTH)):
        rows = ref[...].astype(F32)
        for i, key in enumerate(keys):
            out[key] = rows[36 * i : 36 * i + 36]
            given[key] = rows[36 * (i + len(keys)) :][:36]
    u = shifted(out)
    weights = (w_qkv[1], w_proj[1], w_fc1[1], w_fc2[1])
    saved = forward(u, gains[1], *weights, bias_ref, allowed, prob_second)
    du = backward(
        u, *saved, shifted(given), gains[1], *weights, lanes[...], True, prob_second, grad_ref,
        gain_second, chunk_second,
    )
    have = unshifted(du)
    mine_ref[...] = jnp.concatenate([have[key] for key in OWN] + [jnp.zeros((4, DIM), F32)], axis=0)
    for ref, keys in ((back_lat, BY_LAT), (back_lon, BY_LON), (back_both, BY_BOTH)):
        ref[...] = padded([have[key] for key in keys], ref.shape[0])
    flights = [
        send(source, target, (send_h, recv_h), 3 + i, upper[i])
        for i, (source, target) in enumerate(((back_lat, home_lat), (back_lon, home_lon), (back_both, home_both)))
    ]

    parts = (chunk_second, chunk_first)
    flights_a, flights_b, flights_c = [None] * 3, [None] * 3, [None] * 3

    def start_a(i):
        flights_a[i] = send(parts[i].at[pl.ds((1 - core) * 8, 8)], got_a.at[i], (send_a, recv_a), i, core_peer)

    def start_b(i):
        flights_a[i].wait()
        sum_a[i] = (parts[i][pl.ds(core * 8, 8)].astype(F32) + got_a[i].astype(F32)).astype(BF)
        flights_b[i] = [
            send(sum_a.at[i, pl.ds(y_peer(o) * 2, 2)], got_b.at[i, y], (send_b, recv_b),
                 i * (y_count - 1) + o - 1, {"lon_0": y_peer(o)})
            for o in range(1, y_count)
        ]
        got_b[i, pl.ds(y, 1)] = sum_a[i, pl.ds(y * 2, 2)][None]

    def start_c(i):
        for flight in flights_b[i]:
            flight.wait()
        total = got_b[i, 0].astype(F32)
        for o in range(1, y_count):
            total = total + got_b[i, o].astype(F32)
        sum_b[i] = total.astype(BF)
        flights_c[i] = send(sum_b.at[i, 1 - side], got_c.at[i], (send_c, recv_c), i, side_peer)

    rows_of = [None, None]

    def finish_c(i):
        flights_c[i].wait()
        chunk = sum_b[i, pl.ds(side, 1)][0].astype(F32) + got_c[i].astype(F32)
        sums = jnp.concatenate((chunk[216:224], chunk[224:232]), axis=1)
        for h in range(HEADS):
            table_ref[1 - i, h] = sums[h : h + 1, :207]
        rows_of[1 - i] = unpack_chunk(chunk)

    start_a(0)

    for flight in flights:
        flight.wait()
    have = {}
    for ref, keys in ((mine_ref, OWN), (home_lat, BY_LAT), (home_lon, BY_LON), (home_both, BY_BOTH)):
        rows = ref[...].astype(F32)
        for i, key in enumerate(keys):
            have[key] = rows[36 * i : 36 * i + 36]
    x = nn(order[...], flat_rows(state).astype(BF))
    du = backward(
        x, q_ref[...], k_ref[...], v_ref[...], o_ref[...], m_ref[...], g_ref[...],
        slope_ref[...], whole_block(have), gains[0], *first_weights, lanes[...], False, prob_first, grad_ref,
        gain_first, chunk_first, meanwhile=lambda: start_b(0),
    )
    start_a(1)
    pad = jnp.zeros((2, 64), F32)
    gain_s[0] = jnp.concatenate(
        (
            jnp.concatenate((gain_first[...], pad), axis=1),
            jnp.concatenate((gain_second[...], pad), axis=1),
            jnp.zeros((4, 256), F32),
        ),
        axis=0,
    )
    flights_a[2] = send(gain_s.at[0], gain_a, (send_a, recv_a), 2, core_peer)
    start_c(0)
    start_b(1)
    flights_a[2].wait()
    gain_s[1] = gain_s[0] + gain_a[...]
    flights_b[2] = [
        send(gain_s.at[1], gain_b.at[y], (send_b, recv_b), 2 * (y_count - 1) + o - 1, {"lon_0": y_peer(o)})
        for o in range(1, y_count)
    ]
    gain_b[pl.ds(y, 1)] = gain_s[pl.ds(1, 1)]
    high, low = two_pieces(du)
    flat = tn(order[...], high) + tn(order[...], low)
    for z in range(2):
        for i in range(6):
            start = (z * 6 + i) * 24
            du_ref[z, i] = flat[start : start + 24]
    finish_c(0)
    for flight in flights_b[2]:
        flight.wait()
    total = gain_b[0]
    for o in range(1, y_count):
        total = total + gain_b[o]
    gain_s[2] = total
    flights_c[2] = send(gain_s.at[2], gain_c, (send_c, recv_c), 2, side_peer)
    start_c(1)
    flights_c[2].wait()
    gain_s[3] = gain_s[2] + gain_c[...]
    flights_d = [
        send(gain_s.at[3], gain_d.at[lat_me], (send_d, recv_d), o - 1, lat_at(lat_peer(o)))
        for o in range(1, lat_count)
    ]
    finish_c(1)
    across = jnp.concatenate([jnp.transpose(rows[:96]) for rows in rows_of], axis=1)
    for a in range(16):
        down, right = 96 + 12 * (a // 4), 48 * (a % 4)
        piece = jnp.concatenate(
            [across[12 * a : 12 * a + 12]]
            + [rows[down : down + 12, right : right + 48] for rows in rows_of]
            + [jnp.zeros((12, 96), F32)],
            axis=1,
        )
        sent_d[a] = jnp.concatenate((piece, jnp.zeros((4, 384), F32)), axis=0).astype(BF)
    flights_d += [
        send(sent_d.at[lat_peer(o)], got_d.at[lat_me], (send_d, recv_d), lat_count - 2 + o, lat_at(lat_peer(o)))
        for o in range(1, lat_count)
    ]
    got_d[pl.ds(lat_me, 1)] = sent_d[pl.ds(lat_me, 1)]
    gain_d[pl.ds(lat_me, 1)] = gain_s[pl.ds(3, 1)]
    for flight in flights_d:
        flight.wait()
    total = jnp.sum(got_d[...].astype(F32), axis=0)
    for i in range(2):
        qkv_ref[:, i, :] = total[:12, 96 * i : 96 * i + 36]
        proj_ref[:, i, :] = total[:12, 96 * i + 36 : 96 * i + 48]
        fc1_ref[:, i, :] = total[:12, 96 * i + 48 : 96 * i + 96]
        fc2_ref[:, i, :] = total[:12, 192 + 48 * i : 240 + 48 * i]
    sums = gain_d[0]
    for o in range(1, lat_count):
        sums = sums + gain_d[o]
    for i in range(2):
        gain_ref[i] = sums[2 * i : 2 * i + 2, :DIM]


def body(state, out_cot, qkv_weight, proj_weight, fc1_weight, fc2_weight, norm_gain, bias_table):
    vmem = pl.BlockSpec(memory_space=pltpu.VMEM)
    dma = pltpu.SemaphoreType.DMA
    args = (
        state, out_cot, token_order(), lane_order(), bias_table.reshape(2, HEADS, 1, POS), norm_gain,
        qkv_weight, proj_weight, fc1_weight, jnp.swapaxes(fc2_weight, 1, 2),
    )
    buffers = [(a.shape, a.dtype) for a in args] + [((TOK, DIM), BF)] * 4 + [
        ((TOK, DIM), F32),
        ((TOK, HID), BF),
        ((TOK, HID), BF),
        ((2, HEADS * WIN, WIN), BF),
        ((2, HEADS * WIN, WIN), BF),
        ((2, 8 * WIN, 128), F32),
        ((2, 8 * WIN, 128), F32),
        ((112, DIM), F32),
        ((224, DIM), BF),
        ((224, DIM), BF),
        ((80, DIM), BF),
        ((80, DIM), BF),
        ((224, DIM), BF),
        ((80, DIM), BF),
        ((80, DIM), BF),
        ((112, DIM), BF),
        ((48, DIM), BF),
        ((48, DIM), BF),
        ((112, DIM), BF),
        ((48, DIM), BF),
        ((48, DIM), BF),
        ((16, 240, 128), BF),
        ((16, 240, 128), BF),
        ((2, DIM), F32),
        ((2, DIM), F32),
        ((2, 8, 240, 128), BF),
        ((2, 8, 240, 128), BF),
        ((2, 4, 2, 240, 128), BF),
        ((2, 2, 240, 128), BF),
        ((2, 240, 128), BF),
        ((16, 16, 384), BF),
        ((16, 16, 384), BF),
        ((4, 8, 256), F32),
        ((8, 256), F32),
        ((4, 8, 256), F32),
        ((8, 256), F32),
        ((16, 8, 256), F32),
    ]
    shapes = (
        (2, 6, 24, DIM), (12, 2, 36), (12, 2, 12), (12, 2, 48), (12, 2, 48), (2, 2, DIM), (2, 6, 1, 207)
    )
    outs = pl.pallas_call(
        kernel,
        in_specs=[pl.BlockSpec(memory_space=pltpu.HBM)] * 10,
        out_specs=[vmem] * 7,
        out_shape=[jax.ShapeDtypeStruct(s, F32) for s in shapes],
        scratch_shapes=[pltpu.VMEM(s, d) for s, d in buffers]
        + [dma((10,)), dma((6,)), dma((6,)), dma((3,)), dma((3,)), dma((9,)), dma((9,)), dma((3,)), dma((3,)), dma((30,)), dma((30,))],
        compiler_params=pltpu.CompilerParams(
            collective_id=0, has_side_effects=True, vmem_limit_bytes=60 * 1024 * 1024
        ),
    )(*args)
    state_grad, qkv, proj, fc1, fc2, gain, table = outs
    return (
        state_grad,
        jnp.swapaxes(qkv, 0, 1),
        jnp.swapaxes(proj, 0, 1),
        jnp.swapaxes(fc1, 0, 1),
        jnp.transpose(fc2, (1, 2, 0)),
        gain,
        table.reshape(2, 1, 1, HEADS, 207),
    )


def solution(mesh):
    split = Mesh(mesh.devices.reshape(8, 2, 4, 2, 2), ("lat_0", "lat_1", "lon_0", "lon_1", "lon_2"))
    placed = (
        P(None, LAT, LON, None),
        P(None, LAT, LON, None),
        P(),
        P(),
        P(),
        P(),
        P(),
        P(None, LAT, None, None, None),
    )
    return jax.shard_map(
        body,
        mesh=split,
        in_specs=placed,
        out_specs=(
            P(None, LAT, LON, None),
            P(None, LAT, LON),
            P(None, LAT, LON),
            P(None, LAT, LON),
            P(None, LAT, LON),
            P(),
            P(None, LAT, None, None, LON),
        ),
        check_vma=False,
    )
```

```python
import jax
import jax.numpy as jnp
import ml_dtypes
import numpy as np
from jax import lax
from jax.experimental import pallas as pl
from jax.experimental.pallas import tpu as pltpu
from jax.sharding import Mesh
from jax.sharding import PartitionSpec as P

WZ = 2
WH = 6
WW = 12
LAT = ("lat_0", "lat_1")
LON = ("lon_0", "lon_1", "lon_2")
BF = jnp.bfloat16
F32 = jnp.float32
HEADS = 6
DIM = 192
HEAD = 32
WIN = 144
TOK = 288
HID = 768
POS = 3312
SCALE = HEAD**-0.5


def token_order():
    order = np.zeros((TOK, TOK), np.float32)
    row = 0
    for n in range(2):
        for ih in range(2):
            for w in range(WW):
                for z in range(2):
                    for il in range(3):
                        source = (z * 6 + ih * 3 + il) * 24 + n * WW + w
                        order[row, source] = 1
                        row += 1
    return order.astype(ml_dtypes.bfloat16)


def lane_order():
    order = np.zeros((276, 512), np.float32)
    for a in range(12):
        for d in range(23):
            order[a * 23 + d, (a // 6) * 256 + d * 6 + a % 6] = 1
    return order.astype(ml_dtypes.bfloat16)


def table_offsets(flip):
    offsets = {}
    for b in range(12):
        for a in range(12):
            hk, zk, lk = b // 6, b % 6 // 3, b % 3
            hq, zq, lq = a // 6, a % 6 // 3, a % 3
            if flip:
                hk, zk, hq, zq = 1 - hk, 1 - zk, 1 - hq, 1 - zq
            offsets[b, a] = (zq * 2 + zk) * 828 + ((hq * 3 + lq) * 6 + hk * 3 + lk) * 23
    return offsets


def nn(a, b):
    return lax.dot_general(a, b, (((1,), (0,)), ((), ())), preferred_element_type=F32)


def nt(a, b):
    return lax.dot_general(a, b, (((1,), (1,)), ((), ())), preferred_element_type=F32)


def tn(a, b):
    return lax.dot_general(a, b, (((0,), (0,)), ((), ())), preferred_element_type=F32)


def two_pieces(x):
    high = x.astype(BF)
    return high, (x - high.astype(F32)).astype(BF)


def three_pieces(x):
    high = x.astype(BF)
    rest = x - high.astype(F32)
    middle = rest.astype(BF)
    return high, middle, (rest - middle.astype(F32)).astype(BF)


def expand_bias(table, lanes, flip, bias_ref):
    offsets = table_offsets(flip)
    rows = []
    for b in range(12):
        rows.append(
            jnp.concatenate(
                [table[:, offsets[b, a] : offsets[b, a] + 23] for a in range(12)], axis=1
            )
        )
    stacked = jnp.concatenate(rows, axis=0)
    high, middle, low = three_pieces(stacked)
    spread = nn(high, lanes) + nn(middle, lanes) + nn(low, lanes)
    for b in range(12):
        block = spread[b * 8 : b * 8 + 8]
        for w in range(WW):
            start = (11 - w) * 6
            both = jnp.concatenate(
                (block[:, start : start + 72], block[:, 256 + start : 256 + start + 72]), axis=1
            )
            row = (b // 6) * 72 + w * 6 + b % 6
            right = jnp.concatenate((both[:, 128:], jnp.zeros((8, 112), F32)), axis=1)
            bias_ref[0, pl.ds(row, 8, stride=WIN), :] = both[:, :128]
            bias_ref[1, pl.ds(row, 8, stride=WIN), :] = right


def reduce_bias(grad_ref, lanes, flip):
    offsets = table_offsets(flip)
    rows = []
    for b in range(12):
        left = jnp.zeros((8, 256), F32)
        right = jnp.zeros((8, 256), F32)
        for w in range(WW):
            start = (11 - w) * 6
            row = (b // 6) * 72 + w * 6 + b % 6
            both = jnp.concatenate(
                (
                    grad_ref[0, pl.ds(row, 8, stride=WIN), :],
                    grad_ref[1, pl.ds(row, 8, stride=WIN), :][:, :16],
                ),
                axis=1,
            )
            left = left + jnp.pad(both[:, :72], ((0, 0), (start, 184 - start)))
            right = right + jnp.pad(both[:, 72:], ((0, 0), (start, 184 - start)))
        rows.append(jnp.concatenate((left, right), axis=1))
    stacked = jnp.concatenate(rows, axis=0)
    high, low = two_pieces(stacked)
    packed = nt(high, lanes) + nt(low, lanes)
    places = sorted((start, b, a) for (b, a), start in offsets.items())
    return jnp.concatenate(
        [packed[b * 8 : b * 8 + 8, a * 23 : a * 23 + 23] for _, b, a in places], axis=1
    )


def folded(rows):
    half = rows.shape[0] // 2
    right = rows[:, 128:]
    return jnp.concatenate((rows[:, :128], jnp.concatenate((right[:half], right[half:]), axis=1)), axis=0)


def unfolded(rows):
    count = rows.shape[0] // 3 * 2
    right = jnp.concatenate((rows[count:, :64], rows[count:, 64:]), axis=0)
    return jnp.concatenate((rows[:count], right), axis=1)


def place(b):
    return b % 2 * 8 + b // 4 * 2 + b // 2 % 2


def pack_mlp(fc1, fc2, out_ref):
    for b in range(16):
        rows = [fc1[48 * b : 48 * b + 48]] + [part[12 * b : 12 * b + 12] for part in fc2]
        out_ref[place(b)] = folded(jnp.concatenate(rows, axis=0)).astype(BF)


def pack_attention(qkv, proj, table, gains, out_ref):
    table = jnp.concatenate((table, jnp.zeros((8, 256), F32)), axis=1)
    ends = jnp.concatenate((gains[0][:, 128:], gains[1][:, 128:]), axis=1)
    tail = jnp.concatenate((gains[0][:, :128], gains[1][:, :128], ends, jnp.zeros((5, 128), F32)), axis=0)
    for b in range(16):
        rows = jnp.concatenate((qkv[36 * b : 36 * b + 36], proj[12 * b : 12 * b + 12]), axis=0)
        own = table[:, 207 * b : 207 * b + 207]
        own = jnp.concatenate((own, jnp.zeros((8, 49), F32)), axis=1)
        chunk = jnp.concatenate((folded(rows), own[:, :128], own[:, 128:], tail), axis=0)
        out_ref[place(b)] = chunk.astype(BF)


def normed(u):
    mean = jnp.mean(u, -1, keepdims=True)
    centred = u - mean
    scale = lax.rsqrt(jnp.mean(centred * centred, -1, keepdims=True) + 1e-05)
    return centred * scale, scale


def normed_back(grad, unit, scale):
    mean = jnp.mean(grad, -1, keepdims=True)
    product = jnp.mean(grad * unit, -1, keepdims=True)
    return scale * (grad - mean - unit * product)


def head_masks():
    lane = lax.broadcasted_iota(jnp.int32, (1, DIM), 1) // HEAD
    return [(lane == h).astype(F32) for h in range(HEADS)]


def by_head(x, masks):
    return jnp.concatenate([x * m.astype(BF) for m in masks], axis=0)


def from_heads(x, masks):
    total = x[:WIN] * masks[0]
    for h in range(1, HEADS):
        total = total + x[h * WIN : h * WIN + WIN] * masks[h]
    return total


def forward(u, gains, w_qkv, w_proj, w_fc1, bias_ref, allowed, prob_ref, meanwhile=None):
    masks = head_masks()
    unit, _ = normed(u)
    n1 = (unit * gains[0:1]).astype(BF)
    q, k, v = (
        nn(n1, w_qkv[:, i * DIM : i * DIM + DIM]) for i in range(3)
    )
    joined = []
    for n in range(2):
        part = slice(n * WIN, n * WIN + WIN)
        scores = nt(by_head(k[part].astype(BF), masks), q[part].astype(BF))
        v_t = jnp.transpose(v[part]).astype(BF)
        out_t = []
        for h in range(HEADS):
            rows = slice(h * WIN, h * WIN + WIN)
            bias = jnp.concatenate((bias_ref[0, rows, :], bias_ref[1, rows, :16]), axis=1)
            s = scores[rows] * SCALE + bias
            if allowed is not None:
                s = jnp.where(allowed, s, -1e30)
            e = jnp.exp(s - jnp.max(s, 0, keepdims=True))
            p = (e * (1.0 / jnp.sum(e, 0, keepdims=True))).astype(BF)
            prob_ref[n, rows, :] = p
            out_t.append(nn(v_t[h * HEAD : h * HEAD + HEAD], p))
        joined.append(jnp.transpose(jnp.concatenate(out_t, axis=0)))
    o = jnp.concatenate(joined, axis=0).astype(BF)
    if meanwhile is not None:
        meanwhile()
    m = u + nn(o, w_proj[...])
    unit2, _ = normed(m)
    n2 = (unit2 * gains[1:2]).astype(BF)
    e = nn(n2, w_fc1[...])
    cdf = 0.5 * (1.0 + lax.erf(e * (0.5**0.5)))
    g = (e * cdf).astype(BF)
    slope = cdf + e * jnp.exp(e * e * -0.5) * 0.3989422804014327
    return q.astype(BF), k.astype(BF), v.astype(BF), o, m, g, slope.astype(BF)


def back_mlp(cot, m, slope, w_fc2):
    unit, scale = normed(m)
    y2 = cot.astype(BF)
    dg = nn(y2, w_fc2).astype(BF).astype(F32)
    return y2, (dg * slope.astype(F32)).astype(BF), unit, scale


def back_middle(cot, y1, unit, scale, gain, w_fc1):
    dn = nt(y1, w_fc1).astype(BF).astype(F32)
    return cot + normed_back(dn * gain, unit, scale), jnp.sum(dn * unit, 0, keepdims=True)


def mlp_grads(y2, y1, g, unit, gain):
    n2 = (unit * gain).astype(BF)
    return tn(y1, n2), [tn(y2, g[:, DIM * i : DIM * i + DIM]) for i in range(4)]


def back_attention(do, q, k, v, prob_ref, grad_ref, meanwhile=None):
    masks = head_masks()
    dqs, dks, dvs = [], [], []
    for n in range(2):
        part = slice(n * WIN, n * WIN + WIN)
        do_n, q_n, k_n, v_n = do[part], q[part], k[part], v[part]
        dp = nt(by_head(v_n, masks), do_n)
        dvs.append(from_heads(nn(prob_ref[n], do_n), masks))
        k_t = jnp.transpose(k_n.astype(F32)).astype(BF)
        ds_all, dq_t = [], []
        for h in range(HEADS):
            rows = slice(h * WIN, h * WIN + WIN)
            p = prob_ref[n, rows, :].astype(F32)
            dp_h = dp[rows].astype(BF).astype(F32)
            ds = p * (dp_h - jnp.sum(p * dp_h, 0, keepdims=True))
            if n == 0:
                grad_ref[0, rows, :] = ds[:, :128]
                grad_ref[1, rows, :16] = ds[:, 128:]
            else:
                grad_ref[0, rows, :] += ds[:, :128]
                grad_ref[1, rows, :16] += ds[:, 128:]
            ds = (ds * SCALE).astype(BF)
            ds_all.append(ds)
            dq_t.append(nn(k_t[h * HEAD : h * HEAD + HEAD], ds))
        dqs.append(jnp.transpose(jnp.concatenate(dq_t, axis=0)))
        dks.append(from_heads(nn(jnp.concatenate(ds_all, axis=0), q_n), masks))
        if n == 0 and meanwhile is not None:
            meanwhile()
    return [jnp.concatenate(parts, axis=0).astype(BF) for parts in (dqs, dks, dvs)]


def back_input(dm, d_qkv, unit, scale, gain, w_qkv):
    dn = jnp.zeros((TOK, DIM), F32)
    for i in range(3):
        dn = dn + nt(d_qkv[i], w_qkv[:, i * DIM : i * DIM + DIM])
    dn = dn.astype(BF).astype(F32)
    return dm + normed_back(dn * gain, unit, scale), jnp.sum(dn * unit, 0, keepdims=True)


def qkv_grads(d_qkv, unit, gain):
    n1 = (unit * gain).astype(BF)
    return jnp.concatenate([tn(d, n1) for d in d_qkv], axis=0)


def quarters(x):
    return {
        (n, ih, half): x[n * WIN + ih * 72 + half * 36 :][:36]
        for n in range(2)
        for ih in range(2)
        for half in range(2)
    }


def padded(pieces, rows):
    have = sum(p.shape[0] for p in pieces)
    return jnp.concatenate(list(pieces) + [jnp.zeros((rows - have, DIM), F32)], axis=0).astype(BF)


OWN = ((0, 1, 1), (1, 1, 0), (1, 1, 1))
BY_LAT = ((0, 0, 1), (1, 0, 0), (1, 0, 1))
BY_LON = ((0, 1, 0),)
BY_BOTH = ((0, 0, 0),)


def shifted(have):
    order = []
    for n in range(2):
        for ih in range(2):
            order += [(n, ih, 1), ((n + 1) % 2, ih, 0)]
    return jnp.concatenate([have[key] for key in order], axis=0)


def unshifted(x):
    have = {}
    row = 0
    for n in range(2):
        for ih in range(2):
            for key in ((n, ih, 1), ((n + 1) % 2, ih, 0)):
                have[key] = x[row : row + 36]
                row += 36
    return have


def whole_block(have):
    return jnp.concatenate(
        [have[n, ih, half] for n in range(2) for ih in range(2) for half in range(2)], axis=0
    )


def flat_rows(ref):
    return jnp.concatenate([ref[z, i].astype(F32) for z in range(2) for i in range(6)], axis=0)


MESH = pl.DeviceIdType.MESH


def ring(names):
    sizes = [lax.axis_size(name) for name in names]
    me = 0
    for name, size in zip(names, sizes):
        me = me * size + lax.axis_index(name)
    total = 1
    for size in sizes:
        total *= size

    def at(index):
        where = {}
        for name, size in reversed(list(zip(names, sizes))):
            where[name] = lax.rem(index, size)
            index = index // size
        return where

    return me, total, at


def kernel(state_in, cot_in, order_in, lanes_in, table_in, gains_in, w_qkv_in, w_proj_in, w_fc1_in, w_fc2_in,
           du_ref, qkv_ref, proj_ref, fc1_ref, fc2_ref, gain_ref, table_ref,
           state, cot, order, lanes, table, gains, w_qkv, w_proj, w_fc1, w_fc2,
           q_ref, k_ref, v_ref, o_ref, m_ref, g_ref, slope_ref, prob_first, prob_second, bias_ref, grad_ref,
           mine_ref, own_ref, *rest):
    halos, rest = rest[:18], rest[18:]
    parts, got_a, sum_a, got_b, sum_b, got_c = (rest[4 * i : 4 * i + 4] for i in range(6))
    sent_d, got_d, load, send_h, recv_h, send_a, recv_a, send_b, recv_b, send_c, recv_c, send_d, recv_d = rest[24:]
    loads = [
        pltpu.make_async_copy(source, target, load.at[i])
        for i, (source, target) in enumerate(
            (
                (order_in, order),
                (state_in, state),
                (cot_in, cot),
                (table_in, table),
                (lanes_in, lanes),
                (gains_in, gains),
                (w_qkv_in, w_qkv),
                (w_proj_in, w_proj),
                (w_fc1_in, w_fc1),
                (w_fc2_in, w_fc2),
            )
        )
    ]
    for copy in loads:
        copy.start()
    core = lax.axis_index("lon_2")
    side = lax.axis_index("lon_1")
    y, y_count = lax.axis_index("lon_0"), lax.axis_size("lon_0")
    lat_me, lat_count, lat_at = ring(LAT)
    lon_me, lon_count, lon_at = ring(LON)
    core_peer = {"lon_2": 1 - core}
    side_peer = {"lon_1": 1 - side}

    def y_peer(o):
        return lax.rem(y + o, y_count)

    def lat_peer(o):
        return lax.rem(lat_me + o, lat_count)

    def neighbours(way):
        lat = lat_at(lax.rem(lat_me + way + lat_count, lat_count))
        lon = lon_at(lax.rem(lon_me + way + lon_count, lon_count))
        return lat, lon, {**lat, **lon}

    lower, upper = neighbours(-1), neighbours(1)
    peers = (
        [*lower, *upper, core_peer, side_peer]
        + [{"lon_0": y_peer(o)} for o in range(1, y_count)]
        + [lat_at(lat_peer(o)) for o in range(1, lat_count)]
    )
    barrier = pltpu.get_barrier_semaphore()
    for device in peers:
        pl.semaphore_signal(barrier, inc=1, device_id=device, device_id_type=MESH)

    def send(source, target, sems, i, device):
        copy = pltpu.make_async_remote_copy(
            src_ref=source, dst_ref=target, send_sem=sems[0].at[i], recv_sem=sems[1].at[i],
            device_id=device, device_id_type=MESH,
        )
        copy.start()
        return copy

    def table_of(block):
        return jnp.concatenate([table[block, h] for h in range(HEADS)] + [jnp.zeros((2, POS), F32)], axis=0)

    def exchange(step, targets):
        return [
            send(halos[6 * step + i], halos[6 * step + 3 + i], (send_h, recv_h), 3 * step + i, targets[i])
            for i in range(3)
        ]

    def fill(step, have):
        for i, keys in enumerate((BY_LAT, BY_LON, BY_BOTH)):
            ref = halos[6 * step + i]
            ref[...] = padded([have[key] for key in keys], ref.shape[0])

    def arrived(step, own):
        have = {}
        for ref, keys in zip((own, *halos[6 * step + 3 : 6 * step + 6]), (OWN, BY_LAT, BY_LON, BY_BOTH)):
            rows = ref[...].astype(F32)
            for i, key in enumerate(keys):
                have[key] = rows[36 * i : 36 * i + 36]
        return have

    for copy in loads[:5]:
        copy.wait()
    perm = order[...]
    x = nn(perm, flat_rows(state).astype(BF))
    given = quarters(nn(perm, flat_rows(cot).astype(BF)))
    fill(0, given)
    expand_bias(table_of(0), lanes[...], False, bias_ref)
    for copy in loads[5:7]:
        copy.wait()
    first_gains, second_gains = gains[0], gains[1]
    early = []

    def open_halo():
        for copy in loads[7:]:
            copy.wait()
        pl.semaphore_wait(barrier, len(peers))
        early.extend(exchange(0, lower))

    q, k, v, o, m, g, slope = forward(
        x, first_gains, w_qkv[0], w_proj.at[0], w_fc1.at[0], bias_ref, None, prob_first, open_halo
    )
    out = quarters(m + nt(g, w_fc2[0]))
    fill(1, out)
    flights = early + exchange(1, lower)
    own_ref[0] = padded([out[key] for key in OWN], 112)
    own_ref[1] = padded([given[key] for key in OWN], 112)
    for ref, value in ((q_ref, q), (k_ref, k), (v_ref, v), (o_ref, o), (m_ref, m), (g_ref, g), (slope_ref, slope)):
        ref[...] = value

    expand_bias(table_of(1), lanes[...], True, bias_ref)
    row = lax.broadcasted_iota(jnp.int32, (WIN, WIN), 0)
    lane = lax.broadcasted_iota(jnp.int32, (WIN, WIN), 1)
    same_z = (row % 6 // 3) == (lane % 6 // 3)
    same_h = (row // 72) == (lane // 72)
    allowed = same_z & (same_h | (jnp.full((WIN, WIN), lat_me, jnp.int32) < lat_count - 1))
    grad_ref[...] = jnp.zeros_like(grad_ref)
    for flight in flights:
        flight.wait()
    u = shifted(arrived(1, own_ref.at[0]))
    cot_u = shifted(arrived(0, own_ref.at[1]))
    q, k, v, o, m, g, slope = forward(
        u, second_gains, w_qkv[1], w_proj.at[1], w_fc1.at[1], bias_ref, allowed, prob_second
    )
    y2, y1, unit2, scale2 = back_mlp(cot_u, m, slope, w_fc2[1])
    dm, gain2 = back_middle(cot_u, y1, unit2, scale2, second_gains[1:2], w_fc1[1])
    yp = dm.astype(BF)
    d_qkv = back_attention(nt(yp, w_proj[1]).astype(BF), q, k, v, prob_second, grad_ref)
    unit1, scale1 = normed(u)
    du, gain1 = back_input(dm, d_qkv, unit1, scale1, second_gains[0:1], w_qkv[1])
    have = unshifted(du)
    fill(2, have)
    flights = exchange(2, upper)
    mine_ref[...] = jnp.concatenate([have[key] for key in OWN] + [jnp.zeros((4, DIM), F32)], axis=0)

    flights_a, flights_b, flights_c, done = [None] * 4, [None] * 4, [None] * 4, [None] * 4

    def start_a(i):
        flights_a[i] = send(parts[i].at[pl.ds((1 - core) * 8, 8)], got_a[i], (send_a, recv_a), i, core_peer)

    def start_b(i):
        flights_a[i].wait()
        sum_a[i][...] = (parts[i][pl.ds(core * 8, 8)].astype(F32) + got_a[i][...].astype(F32)).astype(BF)
        flights_b[i] = [
            send(sum_a[i].at[pl.ds(y_peer(o) * 2, 2)], got_b[i].at[y], (send_b, recv_b),
                 i * (y_count - 1) + o - 1, {"lon_0": y_peer(o)})
            for o in range(1, y_count)
        ]
        got_b[i][pl.ds(y, 1)] = sum_a[i][pl.ds(y * 2, 2)][None]

    def start_c(i):
        for flight in flights_b[i]:
            flight.wait()
        total = got_b[i][0].astype(F32)
        for o in range(1, y_count):
            total = total + got_b[i][o].astype(F32)
        sum_b[i][...] = total.astype(BF)
        flights_c[i] = send(sum_b[i].at[1 - side], got_c[i], (send_c, recv_c), i, side_peer)

    def finish_c(i):
        flights_c[i].wait()
        chunk = sum_b[i][pl.ds(side, 1)][0].astype(F32) + got_c[i][...].astype(F32)
        if i % 2 == 0:
            rows = unfolded(chunk)
            done[i] = (jnp.transpose(rows[:48]), rows[48:])
        else:
            sums = jnp.concatenate((chunk[72:80], chunk[80:88]), axis=1)
            for h in range(HEADS):
                table_ref[1 - i // 2, h] = sums[h : h + 1, :207]
            gain = jnp.concatenate(
                (
                    jnp.concatenate((chunk[88:89], chunk[90:91, :64]), axis=1),
                    jnp.concatenate((chunk[89:90], chunk[90:91, 64:]), axis=1),
                ),
                axis=0,
            )
            done[i] = (jnp.transpose(unfolded(chunk[:72])), gain)

    pack_mlp(*mlp_grads(y2, y1, g, unit2, second_gains[1:2]), parts[0])
    start_a(0)
    pack_attention(
        qkv_grads(d_qkv, unit1, second_gains[0:1]), tn(yp, o), reduce_bias(grad_ref, lanes[...], True),
        (gain1, gain2), parts[1],
    )
    start_a(1)

    for flight in flights:
        flight.wait()
    cot_x = whole_block(arrived(2, mine_ref))
    y2, y1, unit2, scale2 = back_mlp(cot_x, m_ref[...], slope_ref[...], w_fc2[0])
    start_b(0)
    pack_mlp(*mlp_grads(y2, y1, g_ref[...], unit2, first_gains[1:2]), parts[2])
    start_a(2)
    start_b(1)
    dm, gain2 = back_middle(cot_x, y1, unit2, scale2, first_gains[1:2], w_fc1[0])
    yp = dm.astype(BF)
    do = nt(yp, w_proj[0]).astype(BF)
    d_qkv = back_attention(
        do, q_ref[...], k_ref[...], v_ref[...], prob_first, grad_ref, lambda: start_b(2)
    )
    start_c(0)
    unit1, scale1 = normed(nn(order[...], flat_rows(state).astype(BF)))
    du, gain1 = back_input(dm, d_qkv, unit1, scale1, first_gains[0:1], w_qkv[0])
    pack_attention(
        qkv_grads(d_qkv, unit1, first_gains[0:1]), tn(yp, o_ref[...]), reduce_bias(grad_ref, lanes[...], False),
        (gain1, gain2), parts[3],
    )
    start_a(3)
    start_c(1)
    high, low = two_pieces(du)
    flat = tn(order[...], high) + tn(order[...], low)
    start_b(3)
    for z in range(2):
        for i in range(6):
            start = (z * 6 + i) * 24
            du_ref[z, i] = flat[start : start + 24]
    finish_c(0)
    start_c(2)
    finish_c(1)
    finish_c(2)
    start_c(3)
    finish_c(3)
    across = jnp.concatenate([done[i][0] for i in (3, 1, 2, 0)], axis=1)
    gain = jnp.concatenate((done[3][1], done[1][1]), axis=0)
    gain = jnp.concatenate((gain, jnp.zeros((4, DIM), F32)), axis=1)
    for a in range(16):
        down, right = 12 * (a // 4), 48 * (a % 4)
        piece = jnp.concatenate(
            [across[12 * a : 12 * a + 12]]
            + [done[i][1][down : down + 12, right : right + 48] for i in (2, 0)]
            + [jnp.zeros((12, 96), F32)],
            axis=1,
        )
        sent_d[a] = jnp.concatenate((piece, gain), axis=0).astype(BF)
    flights_d = [
        send(sent_d.at[lat_peer(o)], got_d.at[lat_me], (send_d, recv_d), o - 1, lat_at(lat_peer(o)))
        for o in range(1, lat_count)
    ]
    got_d[pl.ds(lat_me, 1)] = sent_d[pl.ds(lat_me, 1)]
    for flight in flights_d:
        flight.wait()
    total = got_d[0].astype(F32)
    for o in range(1, lat_count):
        total = total + got_d[o].astype(F32)
    for i in range(2):
        qkv_ref[:, i, :] = total[:12, 48 * i : 48 * i + 36]
        proj_ref[:, i, :] = total[:12, 48 * i + 36 : 48 * i + 48]
        fc1_ref[:, i, :] = total[:12, 96 + 48 * i : 144 + 48 * i]
        fc2_ref[:, i, :] = total[:12, 192 + 48 * i : 240 + 48 * i]
        gain_ref[i] = total[12 + 2 * i : 14 + 2 * i, :DIM]


def hand_over(*refs):
    count = len(refs) // 2
    sems = refs[-1]
    copies = [pltpu.make_async_copy(refs[i], refs[count + i], sems.at[i]) for i in range(count)]
    for copy in copies:
        copy.start()
    for copy in copies:
        copy.wait()


def body(state, out_cot, qkv_weight, proj_weight, fc1_weight, fc2_weight, norm_gain, bias_table):
    vmem = pl.BlockSpec(memory_space=pltpu.VMEM)
    dma = pltpu.SemaphoreType.DMA
    args = (
        state, out_cot, token_order(), lane_order(), bias_table.reshape(2, HEADS, 1, POS), norm_gain,
        qkv_weight, proj_weight, fc1_weight, jnp.swapaxes(fc2_weight, 1, 2),
    )
    buffers = [(a.shape, a.dtype) for a in args] + [((TOK, DIM), BF)] * 4 + [
        ((TOK, DIM), F32),
        ((TOK, HID), BF),
        ((TOK, HID), BF),
        ((2, HEADS * WIN, WIN), BF),
        ((2, HEADS * WIN, WIN), BF),
        ((2, 8 * WIN, 128), F32),
        ((2, 8 * WIN, 128), F32),
        ((112, DIM), F32),
        ((2, 112, DIM), BF),
    ]
    buffers += [((112, DIM), BF), ((48, DIM), BF), ((48, DIM), BF)] * 6
    rows = (144, 96, 144, 96)
    for lead in ((16,), (8,), (8,), (4, 2), (2,), ()):
        buffers += [(lead + (r, 128), BF) for r in rows]
    buffers += [((16, 16, 384), BF), ((16, 16, 384), BF)]
    shapes = (
        (2, 6, 24, DIM), (12, 2, 36), (12, 2, 12), (12, 2, 48), (12, 2, 48), (2, 2, DIM), (2, 6, 1, 207)
    )
    outs = pl.pallas_call(
        kernel,
        in_specs=[pl.BlockSpec(memory_space=pltpu.HBM)] * 10,
        out_specs=[vmem] * 7,
        out_shape=[jax.ShapeDtypeStruct(s, F32) for s in shapes],
        scratch_shapes=[pltpu.VMEM(s, d) for s, d in buffers]
        + [dma((n,)) for n in (10, 9, 9, 4, 4, 12, 12, 4, 4, 15, 15)],
        compiler_params=pltpu.CompilerParams(
            collective_id=0, has_side_effects=True, vmem_limit_bytes=60 * 1024 * 1024
        ),
    )(*args)
    hbm = pl.BlockSpec(memory_space=pltpu.HBM)
    outs = pl.pallas_call(
        hand_over,
        in_specs=[hbm] * 7,
        out_specs=[hbm] * 7,
        out_shape=[jax.ShapeDtypeStruct(s, F32) for s in shapes],
        scratch_shapes=[dma((7,))],
        compiler_params=pltpu.CompilerParams(vmem_limit_bytes=60 * 1024 * 1024),
    )(*outs)
    state_grad, qkv, proj, fc1, fc2, gain, table = outs
    return (
        state_grad,
        jnp.swapaxes(qkv, 0, 1),
        jnp.swapaxes(proj, 0, 1),
        jnp.swapaxes(fc1, 0, 1),
        jnp.transpose(fc2, (1, 2, 0)),
        gain,
        table.reshape(2, 1, 1, HEADS, 207),
    )


def solution(mesh):
    split = Mesh(mesh.devices.reshape(8, 2, 4, 2, 2), ("lat_0", "lat_1", "lon_0", "lon_1", "lon_2"))
    placed = (
        P(None, LAT, LON, None),
        P(None, LAT, LON, None),
        P(),
        P(),
        P(),
        P(),
        P(),
        P(None, LAT, None, None, None),
    )
    return jax.shard_map(
        body,
        mesh=split,
        in_specs=placed,
        out_specs=(
            P(None, LAT, LON, None),
            P(None, LAT, LON),
            P(None, LAT, LON),
            P(None, LAT, LON),
            P(None, LAT, LON),
            P(),
            P(None, LAT, None, None, LON),
        ),
        check_vma=False,
    )
```

```python
import jax
import jax.numpy as jnp
import ml_dtypes
import numpy as np
from jax import lax
from jax.experimental import pallas as pl
from jax.experimental.pallas import tpu as pltpu
from jax.sharding import Mesh
from jax.sharding import PartitionSpec as P

WZ = 2
WH = 6
WW = 12
LAT = ("lat_0", "lat_1")
LON = ("lon_0", "lon_1", "lon_2")
BF = jnp.bfloat16
F32 = jnp.float32
HEADS = 6
DIM = 192
HEAD = 32
WIN = 144
TOK = 288
HID = 768
POS = 3312
SCALE = HEAD**-0.5


def token_order():
    order = np.zeros((TOK, TOK), np.float32)
    row = 0
    for n in range(2):
        for ih in range(2):
            for w in range(WW):
                for z in range(2):
                    for il in range(3):
                        source = (z * 6 + ih * 3 + il) * 24 + n * WW + w
                        order[row, source] = 1
                        row += 1
    return order.astype(ml_dtypes.bfloat16)


def lane_order():
    order = np.zeros((276, 512), np.float32)
    for a in range(12):
        for d in range(23):
            order[a * 23 + d, (a // 6) * 256 + d * 6 + a % 6] = 1
    return order.astype(ml_dtypes.bfloat16)


def table_offsets(flip):
    offsets = {}
    for b in range(12):
        for a in range(12):
            hk, zk, lk = b // 6, b % 6 // 3, b % 3
            hq, zq, lq = a // 6, a % 6 // 3, a % 3
            if flip:
                hk, zk, hq, zq = 1 - hk, 1 - zk, 1 - hq, 1 - zq
            offsets[b, a] = (zq * 2 + zk) * 828 + ((hq * 3 + lq) * 6 + hk * 3 + lk) * 23
    return offsets


def nn(a, b):
    return lax.dot_general(a, b, (((1,), (0,)), ((), ())), preferred_element_type=F32)


def nt(a, b):
    return lax.dot_general(a, b, (((1,), (1,)), ((), ())), preferred_element_type=F32)


def tn(a, b):
    return lax.dot_general(a, b, (((0,), (0,)), ((), ())), preferred_element_type=F32)


def two_pieces(x):
    high = x.astype(BF)
    return high, (x - high.astype(F32)).astype(BF)


def three_pieces(x):
    high = x.astype(BF)
    rest = x - high.astype(F32)
    middle = rest.astype(BF)
    return high, middle, (rest - middle.astype(F32)).astype(BF)


def expand_bias(table, lanes, flip, bias_ref):
    offsets = table_offsets(flip)
    rows = []
    for b in range(12):
        rows.append(
            jnp.concatenate(
                [table[:, offsets[b, a] : offsets[b, a] + 23] for a in range(12)], axis=1
            )
        )
    stacked = jnp.concatenate(rows, axis=0)
    high, middle, low = three_pieces(stacked)
    spread = nn(high, lanes) + nn(middle, lanes) + nn(low, lanes)
    for b in range(12):
        block = spread[b * 8 : b * 8 + 8]
        for w in range(WW):
            start = (11 - w) * 6
            both = jnp.concatenate(
                (block[:, start : start + 72], block[:, 256 + start : 256 + start + 72]), axis=1
            )
            row = (b // 6) * 72 + w * 6 + b % 6
            right = jnp.concatenate((both[:, 128:], jnp.zeros((8, 112), F32)), axis=1)
            bias_ref[0, pl.ds(row, 8, stride=WIN), :] = both[:, :128]
            bias_ref[1, pl.ds(row, 8, stride=WIN), :] = right


def reduce_bias(grad_ref, lanes, flip):
    offsets = table_offsets(flip)
    rows = []
    for b in range(12):
        left = jnp.zeros((8, 256), F32)
        right = jnp.zeros((8, 256), F32)
        for w in range(WW):
            start = (11 - w) * 6
            row = (b // 6) * 72 + w * 6 + b % 6
            both = jnp.concatenate(
                (
                    grad_ref[0, pl.ds(row, 8, stride=WIN), :],
                    grad_ref[1, pl.ds(row, 8, stride=WIN), :][:, :16],
                ),
                axis=1,
            )
            left = left + jnp.pad(both[:, :72], ((0, 0), (start, 184 - start)))
            right = right + jnp.pad(both[:, 72:], ((0, 0), (start, 184 - start)))
        rows.append(jnp.concatenate((left, right), axis=1))
    stacked = jnp.concatenate(rows, axis=0)
    high, low = two_pieces(stacked)
    packed = nt(high, lanes) + nt(low, lanes)
    places = sorted((start, b, a) for (b, a), start in offsets.items())
    return jnp.concatenate(
        [packed[b * 8 : b * 8 + 8, a * 23 : a * 23 + 23] for _, b, a in places], axis=1
    )


def folded(rows):
    half = rows.shape[0] // 2
    right = rows[:, 128:]
    return jnp.concatenate((rows[:, :128], jnp.concatenate((right[:half], right[half:]), axis=1)), axis=0)


def unfolded(rows):
    count = rows.shape[0] // 3 * 2
    right = jnp.concatenate((rows[count:, :64], rows[count:, 64:]), axis=0)
    return jnp.concatenate((rows[:count], right), axis=1)


def place(b):
    return b % 2 * 8 + b // 4 * 2 + b // 2 % 2


def pack_mlp(fc1, fc2, out_ref):
    for b in range(16):
        rows = [fc1[48 * b : 48 * b + 48]] + [part[12 * b : 12 * b + 12] for part in fc2]
        out_ref[place(b)] = folded(jnp.concatenate(rows, axis=0)).astype(BF)


def pack_attention(qkv, proj, table, out_ref):
    table = jnp.concatenate((table, jnp.zeros((8, 256), F32)), axis=1)
    tail = jnp.zeros((8, 128), F32)
    for b in range(16):
        rows = jnp.concatenate((qkv[36 * b : 36 * b + 36], proj[12 * b : 12 * b + 12]), axis=0)
        own = table[:, 207 * b : 207 * b + 207]
        own = jnp.concatenate((own, jnp.zeros((8, 49), F32)), axis=1)
        chunk = jnp.concatenate((folded(rows), own[:, :128], own[:, 128:], tail), axis=0)
        out_ref[place(b)] = chunk.astype(BF)


def normed(u):
    mean = jnp.mean(u, -1, keepdims=True)
    centred = u - mean
    scale = lax.rsqrt(jnp.mean(centred * centred, -1, keepdims=True) + 1e-05)
    return centred * scale, scale


def normed_back(grad, unit, scale):
    mean = jnp.mean(grad, -1, keepdims=True)
    product = jnp.mean(grad * unit, -1, keepdims=True)
    return scale * (grad - mean - unit * product)


def head_masks():
    lane = lax.broadcasted_iota(jnp.int32, (1, DIM), 1) // HEAD
    return [(lane == h).astype(F32) for h in range(HEADS)]


def by_head(x, masks):
    return jnp.concatenate([x * m.astype(BF) for m in masks], axis=0)


def from_heads(x, masks):
    total = x[:WIN] * masks[0]
    for h in range(1, HEADS):
        total = total + x[h * WIN : h * WIN + WIN] * masks[h]
    return total


def forward(u, gains, w_qkv, w_proj, w_fc1, bias_ref, allowed, prob_ref, meanwhile=None):
    masks = head_masks()
    unit, _ = normed(u)
    n1 = (unit * gains[0:1]).astype(BF)
    q, k, v = (
        nn(n1, w_qkv[:, i * DIM : i * DIM + DIM]) for i in range(3)
    )
    joined = []
    for n in range(2):
        part = slice(n * WIN, n * WIN + WIN)
        scores = nt(by_head(k[part].astype(BF), masks), q[part].astype(BF))
        v_t = jnp.transpose(v[part]).astype(BF)
        out_t = []
        for h in range(HEADS):
            rows = slice(h * WIN, h * WIN + WIN)
            bias = jnp.concatenate((bias_ref[0, rows, :], bias_ref[1, rows, :16]), axis=1)
            s = scores[rows] * SCALE + bias
            if allowed is not None:
                s = jnp.where(allowed, s, -1e30)
            e = jnp.exp(s - jnp.max(s, 0, keepdims=True))
            p = (e * (1.0 / jnp.sum(e, 0, keepdims=True))).astype(BF)
            prob_ref[n, rows, :] = p
            out_t.append(nn(v_t[h * HEAD : h * HEAD + HEAD], p))
        joined.append(jnp.transpose(jnp.concatenate(out_t, axis=0)))
    o = jnp.concatenate(joined, axis=0).astype(BF)
    if meanwhile is not None:
        meanwhile()
    m = u + nn(o, w_proj[...])
    unit2, _ = normed(m)
    n2 = (unit2 * gains[1:2]).astype(BF)
    e = nn(n2, w_fc1[...])
    cdf = 0.5 * (1.0 + lax.erf(e * (0.5**0.5)))
    g = (e * cdf).astype(BF)
    slope = cdf + e * jnp.exp(e * e * -0.5) * 0.3989422804014327
    return q.astype(BF), k.astype(BF), v.astype(BF), o, m, g, slope.astype(BF)


def back_mlp(cot, m, slope, w_fc2):
    unit, scale = normed(m)
    y2 = cot.astype(BF)
    dg = nn(y2, w_fc2).astype(BF).astype(F32)
    return y2, (dg * slope.astype(F32)).astype(BF), unit, scale


def back_middle(cot, y1, unit, scale, gain, w_fc1):
    dn = nt(y1, w_fc1).astype(BF).astype(F32)
    return cot + normed_back(dn * gain, unit, scale), jnp.sum(dn * unit, 0, keepdims=True)


def mlp_grads(y2, y1, g, unit, gain):
    n2 = (unit * gain).astype(BF)
    return tn(y1, n2), [tn(y2, g[:, DIM * i : DIM * i + DIM]) for i in range(4)]


def back_attention(do, q, k, v, prob_ref, grad_ref, meanwhile=None):
    masks = head_masks()
    dqs, dks, dvs = [], [], []
    for n in range(2):
        part = slice(n * WIN, n * WIN + WIN)
        do_n, q_n, k_n, v_n = do[part], q[part], k[part], v[part]
        dp = nt(by_head(v_n, masks), do_n)
        dvs.append(from_heads(nn(prob_ref[n], do_n), masks))
        k_t = jnp.transpose(k_n.astype(F32)).astype(BF)
        ds_all, dq_t = [], []
        for h in range(HEADS):
            rows = slice(h * WIN, h * WIN + WIN)
            p = prob_ref[n, rows, :].astype(F32)
            dp_h = dp[rows].astype(BF).astype(F32)
            ds = p * (dp_h - jnp.sum(p * dp_h, 0, keepdims=True))
            if n == 0:
                grad_ref[0, rows, :] = ds[:, :128]
                grad_ref[1, rows, :16] = ds[:, 128:]
            else:
                grad_ref[0, rows, :] += ds[:, :128]
                grad_ref[1, rows, :16] += ds[:, 128:]
            ds = (ds * SCALE).astype(BF)
            ds_all.append(ds)
            dq_t.append(nn(k_t[h * HEAD : h * HEAD + HEAD], ds))
        dqs.append(jnp.transpose(jnp.concatenate(dq_t, axis=0)))
        dks.append(from_heads(nn(jnp.concatenate(ds_all, axis=0), q_n), masks))
        if n == 0 and meanwhile is not None:
            meanwhile()
    return [jnp.concatenate(parts, axis=0).astype(BF) for parts in (dqs, dks, dvs)]


def back_input(dm, d_qkv, unit, scale, gain, w_qkv):
    dn = jnp.zeros((TOK, DIM), F32)
    for i in range(3):
        dn = dn + nt(d_qkv[i], w_qkv[:, i * DIM : i * DIM + DIM])
    dn = dn.astype(BF).astype(F32)
    return dm + normed_back(dn * gain, unit, scale), jnp.sum(dn * unit, 0, keepdims=True)


def qkv_grads(d_qkv, unit, gain):
    n1 = (unit * gain).astype(BF)
    return jnp.concatenate([tn(d, n1) for d in d_qkv], axis=0)


def quarters(x):
    return {
        (n, ih, half): x[n * WIN + ih * 72 + half * 36 :][:36]
        for n in range(2)
        for ih in range(2)
        for half in range(2)
    }


def padded(pieces, rows):
    have = sum(p.shape[0] for p in pieces)
    return jnp.concatenate(list(pieces) + [jnp.zeros((rows - have, DIM), F32)], axis=0).astype(BF)


OWN = ((0, 1, 1), (1, 1, 0), (1, 1, 1))
BY_LAT = ((0, 0, 1), (1, 0, 0), (1, 0, 1))
BY_LON = ((0, 1, 0),)
BY_BOTH = ((0, 0, 0),)


def shifted(have):
    order = []
    for n in range(2):
        for ih in range(2):
            order += [(n, ih, 1), ((n + 1) % 2, ih, 0)]
    return jnp.concatenate([have[key] for key in order], axis=0)


def unshifted(x):
    have = {}
    row = 0
    for n in range(2):
        for ih in range(2):
            for key in ((n, ih, 1), ((n + 1) % 2, ih, 0)):
                have[key] = x[row : row + 36]
                row += 36
    return have


def whole_block(have):
    return jnp.concatenate(
        [have[n, ih, half] for n in range(2) for ih in range(2) for half in range(2)], axis=0
    )


def flat_rows(ref):
    return jnp.concatenate([ref[z, i].astype(F32) for z in range(2) for i in range(6)], axis=0)


MESH = pl.DeviceIdType.MESH


def ring(names):
    sizes = [lax.axis_size(name) for name in names]
    me = 0
    for name, size in zip(names, sizes):
        me = me * size + lax.axis_index(name)
    total = 1
    for size in sizes:
        total *= size

    def at(index):
        where = {}
        for name, size in reversed(list(zip(names, sizes))):
            where[name] = lax.rem(index, size)
            index = index // size
        return where

    return me, total, at


def kernel(state_in, cot_in, order_in, lanes_in, table_in, gains_in, w_qkv_in, w_proj_in, w_fc1_in, w_fc2_in,
           du_ref, qkv_ref, proj_ref, fc1_ref, fc2_ref, gain_ref, table_ref,
           state, cot, order, lanes, table, gains, w_qkv, w_proj, w_fc1, w_fc2,
           q_ref, k_ref, v_ref, o_ref, m_ref, g_ref, slope_ref, prob_first, prob_second, bias_ref, grad_ref,
           mine_ref, own_ref, *rest):
    halos, rest = rest[:18], rest[18:]
    parts, got_a, sum_a, relay, passed, got_b, sum_b, got_c = (rest[4 * i : 4 * i + 4] for i in range(8))
    rest = rest[32:]
    sent_d, got_d, sent_e, got_e, gain_s, gain_a, gain_b, gain_c = rest[:8]
    load, send_h, recv_h, send_a, recv_a, send_b, recv_b, send_c, recv_c, send_d, recv_d = rest[8:]
    loads = [
        pltpu.make_async_copy(source, target, load.at[i])
        for i, (source, target) in enumerate(
            (
                (order_in, order),
                (state_in, state),
                (cot_in, cot),
                (table_in, table),
                (lanes_in, lanes),
                (gains_in, gains),
                (w_qkv_in, w_qkv),
                (w_proj_in, w_proj),
                (w_fc1_in, w_fc1),
                (w_fc2_in, w_fc2),
            )
        )
    ]
    for copy in loads:
        copy.start()
    core = lax.axis_index("lon_2")
    side = lax.axis_index("lon_1")
    y, y_count = lax.axis_index("lon_0"), lax.axis_size("lon_0")
    lat_me, lat_count, lat_at = ring(LAT)
    lon_me, lon_count, lon_at = ring(LON)
    core_peer = {"lon_2": 1 - core}
    side_peer = {"lon_1": 1 - side}

    def y_peer(o):
        return lax.rem(y + o, y_count)

    def lat_peer(o):
        return lax.rem(lat_me + o, lat_count)

    def neighbours(way):
        lat = lat_at(lax.rem(lat_me + way + lat_count, lat_count))
        lon = lon_at(lax.rem(lon_me + way + lon_count, lon_count))
        return lat, lon, {**lat, **lon}

    lower, upper = neighbours(-1), neighbours(1)
    peers = (
        [*lower, *upper, core_peer, side_peer]
        + [{"lon_0": y_peer(o)} for o in range(1, y_count)]
        + [lat_at(lat_peer(o)) for o in range(1, lat_count)]
    )
    barrier = pltpu.get_barrier_semaphore()
    for device in peers:
        pl.semaphore_signal(barrier, inc=1, device_id=device, device_id_type=MESH)

    def send(source, target, sems, i, device):
        copy = pltpu.make_async_remote_copy(
            src_ref=source, dst_ref=target, send_sem=sems[0].at[i], recv_sem=sems[1].at[i],
            device_id=device, device_id_type=MESH,
        )
        copy.start()
        return copy

    def table_of(block):
        return jnp.concatenate([table[block, h] for h in range(HEADS)] + [jnp.zeros((2, POS), F32)], axis=0)

    def exchange(step, targets):
        return [
            send(halos[6 * step + i], halos[6 * step + 3 + i], (send_h, recv_h), 3 * step + i, targets[i])
            for i in range(3)
        ]

    def fill(step, have):
        for i, keys in enumerate((BY_LAT, BY_LON, BY_BOTH)):
            ref = halos[6 * step + i]
            ref[...] = padded([have[key] for key in keys], ref.shape[0])

    def arrived(step, own):
        have = {}
        for ref, keys in zip((own, *halos[6 * step + 3 : 6 * step + 6]), (OWN, BY_LAT, BY_LON, BY_BOTH)):
            rows = ref[...].astype(F32)
            for i, key in enumerate(keys):
                have[key] = rows[36 * i : 36 * i + 36]
        return have

    for copy in loads[:5]:
        copy.wait()
    perm = order[...]
    x = nn(perm, flat_rows(state).astype(BF))
    given = quarters(nn(perm, flat_rows(cot).astype(BF)))
    fill(0, given)
    expand_bias(table_of(0), lanes[...], False, bias_ref)
    for copy in loads[5:7]:
        copy.wait()
    first_gains, second_gains = gains[0], gains[1]
    early = []

    def open_halo():
        for copy in loads[7:]:
            copy.wait()
        pl.semaphore_wait(barrier, len(peers))
        early.extend(exchange(0, lower))

    q, k, v, o, m, g, slope = forward(
        x, first_gains, w_qkv[0], w_proj.at[0], w_fc1.at[0], bias_ref, None, prob_first, open_halo
    )
    out = quarters(m + nt(g, w_fc2[0]))
    fill(1, out)
    flights = early + exchange(1, lower)
    own_ref[0] = padded([out[key] for key in OWN], 112)
    own_ref[1] = padded([given[key] for key in OWN], 112)
    for ref, value in ((q_ref, q), (k_ref, k), (v_ref, v), (o_ref, o), (m_ref, m), (g_ref, g), (slope_ref, slope)):
        ref[...] = value

    expand_bias(table_of(1), lanes[...], True, bias_ref)
    row = lax.broadcasted_iota(jnp.int32, (WIN, WIN), 0)
    lane = lax.broadcasted_iota(jnp.int32, (WIN, WIN), 1)
    same_z = (row % 6 // 3) == (lane % 6 // 3)
    same_h = (row // 72) == (lane // 72)
    allowed = same_z & (same_h | (jnp.full((WIN, WIN), lat_me, jnp.int32) < lat_count - 1))
    grad_ref[...] = jnp.zeros_like(grad_ref)
    for flight in flights:
        flight.wait()
    u = shifted(arrived(1, own_ref.at[0]))
    cot_u = shifted(arrived(0, own_ref.at[1]))
    q, k, v, o, m, g, slope = forward(
        u, second_gains, w_qkv[1], w_proj.at[1], w_fc1.at[1], bias_ref, allowed, prob_second
    )
    y2, y1, unit2, scale2 = back_mlp(cot_u, m, slope, w_fc2[1])
    dm, gain2 = back_middle(cot_u, y1, unit2, scale2, second_gains[1:2], w_fc1[1])
    yp = dm.astype(BF)
    d_qkv = back_attention(nt(yp, w_proj[1]).astype(BF), q, k, v, prob_second, grad_ref)
    unit1, scale1 = normed(u)
    du, gain1 = back_input(dm, d_qkv, unit1, scale1, second_gains[0:1], w_qkv[1])
    have = unshifted(du)
    fill(2, have)
    flights = exchange(2, upper)
    mine_ref[...] = jnp.concatenate([have[key] for key in OWN] + [jnp.zeros((4, DIM), F32)], axis=0)

    flights_a, flights_r, flights_b, flights_c, done = ([None] * 4 for _ in range(5))
    up, down, far = y_peer(1), y_peer(y_count - 1), y_peer(2)

    def start_a(i):
        flights_a[i] = send(parts[i].at[pl.ds((1 - core) * 8, 8)], got_a[i], (send_a, recv_a), i, core_peer)

    def send_y(i, j, source, target, peer):
        return send(source, target, (send_b, recv_b), 6 * i + j, {"lon_0": peer})

    def start_b(i):
        flights_a[i].wait()
        sum_a[i][...] = (parts[i][pl.ds(core * 8, 8)].astype(F32) + got_a[i][...].astype(F32)).astype(BF)
        flights_r[i] = [
            send_y(i, 0, sum_a[i].at[far * 2], relay[i].at[0], up),
            send_y(i, 1, sum_a[i].at[far * 2 + 1], relay[i].at[1], down),
        ]
        flights_b[i] = [
            send_y(i, 2, sum_a[i].at[up * 2 + 1], got_b[i].at[0, 1], up),
            send_y(i, 3, sum_a[i].at[down * 2], got_b[i].at[1, 0], down),
        ]

    def pass_b(i):
        for flight in flights_r[i]:
            flight.wait()
        passed[i][0] = (sum_a[i][pl.ds(up * 2, 1)][0].astype(F32) + relay[i][0].astype(F32)).astype(BF)
        passed[i][1] = (sum_a[i][pl.ds(down * 2 + 1, 1)][0].astype(F32) + relay[i][1].astype(F32)).astype(BF)
        flights_b[i] += [
            send_y(i, 4, passed[i].at[0], got_b[i].at[0, 0], up),
            send_y(i, 5, passed[i].at[1], got_b[i].at[1, 1], down),
        ]

    def start_c(i):
        for flight in flights_b[i]:
            flight.wait()
        total = sum_a[i][pl.ds(y * 2, 2)].astype(F32) + got_b[i][0].astype(F32) + got_b[i][1].astype(F32)
        sum_b[i][...] = total.astype(BF)
        flights_c[i] = send(sum_b[i].at[1 - side], got_c[i], (send_c, recv_c), i, side_peer)

    def finish_c(i):
        flights_c[i].wait()
        chunk = sum_b[i][pl.ds(side, 1)][0].astype(F32) + got_c[i][...].astype(F32)
        if i % 2 == 0:
            rows = unfolded(chunk)
            done[i] = (jnp.transpose(rows[:48]), rows[48:])
        else:
            sums = jnp.concatenate((chunk[72:80], chunk[80:88]), axis=1)
            for h in range(HEADS):
                table_ref[1 - i // 2, h] = sums[h : h + 1, :207]
            done[i] = jnp.transpose(unfolded(chunk[:72]))

    first_of_gains = (gain1, gain2)
    pack_mlp(*mlp_grads(y2, y1, g, unit2, second_gains[1:2]), parts[0])
    start_a(0)
    pack_attention(
        qkv_grads(d_qkv, unit1, second_gains[0:1]), tn(yp, o), reduce_bias(grad_ref, lanes[...], True), parts[1]
    )
    start_a(1)

    for flight in flights:
        flight.wait()
    cot_x = whole_block(arrived(2, mine_ref))
    y2, y1, unit2, scale2 = back_mlp(cot_x, m_ref[...], slope_ref[...], w_fc2[0])
    start_b(0)
    pack_mlp(*mlp_grads(y2, y1, g_ref[...], unit2, first_gains[1:2]), parts[2])
    start_a(2)
    start_b(1)
    dm, gain2 = back_middle(cot_x, y1, unit2, scale2, first_gains[1:2], w_fc1[0])
    yp = dm.astype(BF)
    do = nt(yp, w_proj[0]).astype(BF)
    pass_b(0)

    def halfway():
        start_b(2)
        pass_b(1)

    d_qkv = back_attention(do, q_ref[...], k_ref[...], v_ref[...], prob_first, grad_ref, halfway)
    start_c(0)
    pass_b(2)
    unit1, scale1 = normed(nn(order[...], flat_rows(state).astype(BF)))
    pack_attention(
        qkv_grads(d_qkv, unit1, first_gains[0:1]), tn(yp, o_ref[...]), reduce_bias(grad_ref, lanes[...], False),
        parts[3],
    )
    start_a(3)
    du, gain1 = back_input(dm, d_qkv, unit1, scale1, first_gains[0:1], w_qkv[0])
    gain_s[0] = jnp.concatenate(
        [jnp.concatenate((row, jnp.zeros((1, 64), F32)), axis=1) for row in (gain1, gain2, *first_of_gains)]
        + [jnp.zeros((4, 256), F32)],
        axis=0,
    )
    gain_flight = send(gain_s.at[0], gain_a, (send_a, recv_a), 4, core_peer)
    start_c(1)
    start_b(3)
    gain_flight.wait()
    gain_s[1] = gain_s[0] + gain_a[...]
    gain_flights = [
        send(gain_s.at[1], gain_b.at[y], (send_b, recv_b), 23 + o, {"lon_0": y_peer(o)})
        for o in range(1, y_count)
    ]
    gain_b[pl.ds(y, 1)] = gain_s[pl.ds(1, 1)]
    start_c(2)
    finish_c(0)
    finish_c(1)
    pass_b(3)
    high, low = two_pieces(du)
    flat = tn(order[...], high) + tn(order[...], low)
    for z in range(2):
        for i in range(6):
            start = (z * 6 + i) * 24
            du_ref[z, i] = flat[start : start + 24]
    finish_c(2)
    across = jnp.concatenate([done[1], done[2][0], done[0][0]], axis=1)
    for a in range(16):
        low_row, right = 12 * (a // 4), 48 * (a % 4)
        piece = jnp.concatenate(
            [across[12 * a : 12 * a + 12]]
            + [done[i][1][low_row : low_row + 12, right : right + 48] for i in (2, 0)]
            + [jnp.zeros((12, 16), F32)],
            axis=1,
        )
        sent_d[a] = jnp.concatenate((piece, jnp.zeros((4, 256), F32)), axis=0).astype(BF)

    def to_latitudes(source, target, first_sem):
        return [
            send(source.at[lat_peer(o)], target.at[lat_me], (send_d, recv_d), first_sem + o - 1, lat_at(lat_peer(o)))
            for o in range(1, lat_count)
        ]

    start_c(3)
    flights_d = to_latitudes(sent_d, got_d, 0)
    got_d[pl.ds(lat_me, 1)] = sent_d[pl.ds(lat_me, 1)]
    for flight in gain_flights:
        flight.wait()
    total = gain_b[0]
    for o in range(1, y_count):
        total = total + gain_b[o]
    gain_s[2] = total
    gain_flight = send(gain_s.at[2], gain_c, (send_c, recv_c), 4, side_peer)
    finish_c(3)
    gain_flight.wait()
    total = gain_s[2] + gain_c[...]
    gain = jnp.concatenate([total[r : r + 1, 64 * c : 64 * c + 64] for r in range(4) for c in range(3)], axis=0)
    for a in range(16):
        piece = jnp.concatenate((done[3][12 * a : 12 * a + 12], gain, jnp.zeros((12, 16), F32)), axis=1)
        sent_e[a] = jnp.concatenate((piece, jnp.zeros((4, 128), F32)), axis=0).astype(BF)
    flights_e = to_latitudes(sent_e, got_e, lat_count - 1)
    got_e[pl.ds(lat_me, 1)] = sent_e[pl.ds(lat_me, 1)]
    for flight in flights_d:
        flight.wait()

    def summed(ref):
        total = ref[0].astype(F32)
        for o in range(1, lat_count):
            total = total + ref[o].astype(F32)
        return total

    total = summed(got_d)
    qkv_ref[:, 1, :] = total[:12, :36]
    proj_ref[:, 1, :] = total[:12, 36:48]
    for i in range(2):
        fc1_ref[:, i, :] = total[:12, 48 + 48 * i : 96 + 48 * i]
        fc2_ref[:, i, :] = total[:12, 144 + 48 * i : 192 + 48 * i]
    for flight in flights_e:
        flight.wait()
    total = summed(got_e)
    qkv_ref[:, 0, :] = total[:12, :36]
    proj_ref[:, 0, :] = total[:12, 36:48]
    for r in range(4):
        gain_ref[r // 2, r % 2 : r % 2 + 1] = jnp.concatenate(
            [total[3 * r + c : 3 * r + c + 1, 48:112] for c in range(3)], axis=1
        )


def hand_over(*refs):
    for source, target in zip(refs[:7], refs[7:]):
        target[...] = source[...]


def body(state, out_cot, qkv_weight, proj_weight, fc1_weight, fc2_weight, norm_gain, bias_table):
    vmem = pl.BlockSpec(memory_space=pltpu.VMEM)
    dma = pltpu.SemaphoreType.DMA
    args = (
        state, out_cot, token_order(), lane_order(), bias_table.reshape(2, HEADS, 1, POS), norm_gain,
        qkv_weight, proj_weight, fc1_weight, jnp.swapaxes(fc2_weight, 1, 2),
    )
    buffers = [(a.shape, a.dtype) for a in args] + [((TOK, DIM), BF)] * 4 + [
        ((TOK, DIM), F32),
        ((TOK, HID), BF),
        ((TOK, HID), BF),
        ((2, HEADS * WIN, WIN), BF),
        ((2, HEADS * WIN, WIN), BF),
        ((2, 8 * WIN, 128), F32),
        ((2, 8 * WIN, 128), F32),
        ((112, DIM), F32),
        ((2, 112, DIM), BF),
    ]
    buffers += [((112, DIM), BF), ((48, DIM), BF), ((48, DIM), BF)] * 6
    rows = (144, 96, 144, 96)
    for lead in ((16,), (8,), (8,), (2,), (2,), (2, 2), (2,), ()):
        buffers += [(lead + (r, 128), BF) for r in rows]
    buffers += [((16, 16, 256), BF), ((16, 16, 256), BF), ((16, 16, 128), BF), ((16, 16, 128), BF)]
    buffers += [((3, 8, 256), F32), ((8, 256), F32), ((4, 8, 256), F32), ((8, 256), F32)]
    shapes = (
        (2, 6, 24, DIM), (12, 2, 36), (12, 2, 12), (12, 2, 48), (12, 2, 48), (2, 2, DIM), (2, 6, 1, 207)
    )
    outs = pl.pallas_call(
        kernel,
        in_specs=[pl.BlockSpec(memory_space=pltpu.HBM)] * 10,
        out_specs=[vmem] * 7,
        out_shape=[jax.ShapeDtypeStruct(s, F32) for s in shapes],
        scratch_shapes=[pltpu.VMEM(s, d) for s, d in buffers]
        + [dma((n,)) for n in (10, 9, 9, 5, 5, 27, 27, 5, 5, 30, 30)],
        compiler_params=pltpu.CompilerParams(
            collective_id=0, has_side_effects=True, vmem_limit_bytes=60 * 1024 * 1024
        ),
    )(*args)
    outs = pl.pallas_call(
        hand_over,
        in_specs=[vmem] * 7,
        out_specs=[vmem] * 7,
        out_shape=[jax.ShapeDtypeStruct(s, F32) for s in shapes],
        compiler_params=pltpu.CompilerParams(vmem_limit_bytes=60 * 1024 * 1024),
    )(*outs)
    state_grad, qkv, proj, fc1, fc2, gain, table = outs
    return (
        state_grad,
        jnp.swapaxes(qkv, 0, 1),
        jnp.swapaxes(proj, 0, 1),
        jnp.swapaxes(fc1, 0, 1),
        jnp.transpose(fc2, (1, 2, 0)),
        gain,
        table.reshape(2, 1, 1, HEADS, 207),
    )


def solution(mesh):
    split = Mesh(mesh.devices.reshape(8, 2, 4, 2, 2), ("lat_0", "lat_1", "lon_0", "lon_1", "lon_2"))
    placed = (
        P(None, LAT, LON, None),
        P(None, LAT, LON, None),
        P(),
        P(),
        P(),
        P(),
        P(),
        P(None, LAT, None, None, None),
    )
    return jax.shard_map(
        body,
        mesh=split,
        in_specs=placed,
        out_specs=(
            P(None, LAT, LON, None),
            P(None, LAT, LON),
            P(None, LAT, LON),
            P(None, LAT, LON),
            P(None, LAT, LON),
            P(),
            P(None, LAT, None, None, LON),
        ),
        check_vma=False,
    )
```

```python
import jax
import jax.numpy as jnp
import ml_dtypes
import numpy as np
from jax import lax
from jax.experimental import pallas as pl
from jax.experimental.pallas import tpu as pltpu
from jax.sharding import Mesh
from jax.sharding import PartitionSpec as P

WZ = 2
WH = 6
WW = 12
LAT = ("lat_0", "lat_1")
LON = ("lon_0", "lon_1", "lon_2")
BF = jnp.bfloat16
F32 = jnp.float32
HEADS = 6
DIM = 192
HEAD = 32
WIN = 144
TOK = 288
HID = 768
POS = 3312
SCALE = HEAD**-0.5


def token_order():
    order = np.zeros((TOK, TOK), np.float32)
    row = 0
    for n in range(2):
        for ih in range(2):
            for w in range(WW):
                for z in range(2):
                    for il in range(3):
                        source = (z * 6 + ih * 3 + il) * 24 + n * WW + w
                        order[row, source] = 1
                        row += 1
    return order.astype(ml_dtypes.bfloat16)


def lane_order():
    order = np.zeros((276, 512), np.float32)
    for a in range(12):
        for d in range(23):
            order[a * 23 + d, (a // 6) * 256 + d * 6 + a % 6] = 1
    return order.astype(ml_dtypes.bfloat16)


def table_offsets(flip):
    offsets = {}
    for b in range(12):
        for a in range(12):
            hk, zk, lk = b // 6, b % 6 // 3, b % 3
            hq, zq, lq = a // 6, a % 6 // 3, a % 3
            if flip:
                hk, zk, hq, zq = 1 - hk, 1 - zk, 1 - hq, 1 - zq
            offsets[b, a] = (zq * 2 + zk) * 828 + ((hq * 3 + lq) * 6 + hk * 3 + lk) * 23
    return offsets


def nn(a, b):
    return lax.dot_general(a, b, (((1,), (0,)), ((), ())), preferred_element_type=F32)


def nt(a, b):
    return lax.dot_general(a, b, (((1,), (1,)), ((), ())), preferred_element_type=F32)


def tn(a, b):
    return lax.dot_general(a, b, (((0,), (0,)), ((), ())), preferred_element_type=F32)


def two_pieces(x):
    high = x.astype(BF)
    return high, (x - high.astype(F32)).astype(BF)


def three_pieces(x):
    high = x.astype(BF)
    rest = x - high.astype(F32)
    middle = rest.astype(BF)
    return high, middle, (rest - middle.astype(F32)).astype(BF)


def expand_bias(table, lanes, flip, bias_ref):
    offsets = table_offsets(flip)
    rows = []
    for b in range(12):
        rows.append(
            jnp.concatenate(
                [table[:, offsets[b, a] : offsets[b, a] + 23] for a in range(12)], axis=1
            )
        )
    stacked = jnp.concatenate(rows, axis=0)
    high, middle, low = three_pieces(stacked)
    spread = nn(high, lanes) + nn(middle, lanes) + nn(low, lanes)
    for b in range(12):
        block = spread[b * 8 : b * 8 + 8]
        for w in range(WW):
            start = (11 - w) * 6
            both = jnp.concatenate(
                (block[:, start : start + 72], block[:, 256 + start : 256 + start + 72]), axis=1
            )
            row = (b // 6) * 72 + w * 6 + b % 6
            right = jnp.concatenate((both[:, 128:], jnp.zeros((8, 112), F32)), axis=1)
            bias_ref[0, pl.ds(row, 8, stride=WIN), :] = both[:, :128]
            bias_ref[1, pl.ds(row, 8, stride=WIN), :] = right


def reduce_bias(grad_ref, lanes, flip):
    offsets = table_offsets(flip)
    rows = []
    for b in range(12):
        left = jnp.zeros((8, 256), F32)
        right = jnp.zeros((8, 256), F32)
        for w in range(WW):
            start = (11 - w) * 6
            row = (b // 6) * 72 + w * 6 + b % 6
            both = jnp.concatenate(
                (
                    grad_ref[0, pl.ds(row, 8, stride=WIN), :],
                    grad_ref[1, pl.ds(row, 8, stride=WIN), :][:, :16],
                ),
                axis=1,
            )
            left = left + jnp.pad(both[:, :72], ((0, 0), (start, 184 - start)))
            right = right + jnp.pad(both[:, 72:], ((0, 0), (start, 184 - start)))
        rows.append(jnp.concatenate((left, right), axis=1))
    stacked = jnp.concatenate(rows, axis=0)
    high, low = two_pieces(stacked)
    packed = nt(high, lanes) + nt(low, lanes)
    places = sorted((start, b, a) for (b, a), start in offsets.items())
    return jnp.concatenate(
        [packed[b * 8 : b * 8 + 8, a * 23 : a * 23 + 23] for _, b, a in places], axis=1
    )


def folded(rows):
    half = rows.shape[0] // 2
    right = rows[:, 128:]
    return jnp.concatenate((rows[:, :128], jnp.concatenate((right[:half], right[half:]), axis=1)), axis=0)


def unfolded(rows):
    count = rows.shape[0] // 3 * 2
    right = jnp.concatenate((rows[count:, :64], rows[count:, 64:]), axis=0)
    return jnp.concatenate((rows[:count], right), axis=1)


def place(b):
    return b % 2 * 8 + b // 4 * 2 + b // 2 % 2


def pack_mlp(fc1, fc2, out_ref):
    for b in range(16):
        rows = [fc1[48 * b : 48 * b + 48]] + [part[12 * b : 12 * b + 12] for part in fc2]
        out_ref[place(b)] = folded(jnp.concatenate(rows, axis=0)).astype(BF)


def pack_attention(qkv, proj, table, gains, out_ref):
    table = jnp.concatenate((table, jnp.zeros((8, 256), F32)), axis=1)
    ends = jnp.concatenate((gains[0][:, 128:], gains[1][:, 128:]), axis=1)
    tail = jnp.concatenate((gains[0][:, :128], gains[1][:, :128], ends, jnp.zeros((5, 128), F32)), axis=0)
    for b in range(16):
        rows = jnp.concatenate((qkv[36 * b : 36 * b + 36], proj[12 * b : 12 * b + 12]), axis=0)
        own = table[:, 207 * b : 207 * b + 207]
        own = jnp.concatenate((own, jnp.zeros((8, 49), F32)), axis=1)
        chunk = jnp.concatenate((folded(rows), own[:, :128], own[:, 128:], tail), axis=0)
        out_ref[place(b)] = chunk.astype(BF)


def normed(u):
    mean = jnp.mean(u, -1, keepdims=True)
    centred = u - mean
    scale = lax.rsqrt(jnp.mean(centred * centred, -1, keepdims=True) + 1e-05)
    return centred * scale, scale


def normed_back(grad, unit, scale):
    mean = jnp.mean(grad, -1, keepdims=True)
    product = jnp.mean(grad * unit, -1, keepdims=True)
    return scale * (grad - mean - unit * product)


def head_masks():
    lane = lax.broadcasted_iota(jnp.int32, (1, DIM), 1) // HEAD
    return [(lane == h).astype(F32) for h in range(HEADS)]


def by_head(x, masks):
    return jnp.concatenate([x * m.astype(BF) for m in masks], axis=0)


def from_heads(x, masks):
    total = x[:WIN] * masks[0]
    for h in range(1, HEADS):
        total = total + x[h * WIN : h * WIN + WIN] * masks[h]
    return total


def forward(u, gains, w_qkv, w_proj, w_fc1, bias_ref, allowed, prob_ref, meanwhile=None):
    masks = head_masks()
    unit, _ = normed(u)
    n1 = (unit * gains[0:1]).astype(BF)
    q, k, v = (
        nn(n1, w_qkv[:, i * DIM : i * DIM + DIM]) for i in range(3)
    )
    joined = []
    for n in range(2):
        part = slice(n * WIN, n * WIN + WIN)
        scores = nt(by_head(k[part].astype(BF), masks), q[part].astype(BF))
        v_t = jnp.transpose(v[part]).astype(BF)
        out_t = []
        for h in range(HEADS):
            rows = slice(h * WIN, h * WIN + WIN)
            bias = jnp.concatenate((bias_ref[0, rows, :], bias_ref[1, rows, :16]), axis=1)
            s = scores[rows] * SCALE + bias
            if allowed is not None:
                s = jnp.where(allowed, s, -1e30)
            e = jnp.exp(s - jnp.max(s, 0, keepdims=True))
            p = (e * (1.0 / jnp.sum(e, 0, keepdims=True))).astype(BF)
            prob_ref[n, rows, :] = p
            out_t.append(nn(v_t[h * HEAD : h * HEAD + HEAD], p))
        joined.append(jnp.transpose(jnp.concatenate(out_t, axis=0)))
    o = jnp.concatenate(joined, axis=0).astype(BF)
    if meanwhile is not None:
        meanwhile()
    m = u + nn(o, w_proj[...])
    unit2, _ = normed(m)
    n2 = (unit2 * gains[1:2]).astype(BF)
    e = nn(n2, w_fc1[...])
    cdf = 0.5 * (1.0 + lax.erf(e * (0.5**0.5)))
    g = (e * cdf).astype(BF)
    slope = cdf + e * jnp.exp(e * e * -0.5) * 0.3989422804014327
    return q.astype(BF), k.astype(BF), v.astype(BF), o, m, g, slope.astype(BF)


def back_mlp(cot, m, slope, w_fc2):
    unit, scale = normed(m)
    y2 = cot.astype(BF)
    dg = nn(y2, w_fc2).astype(BF).astype(F32)
    return y2, (dg * slope.astype(F32)).astype(BF), unit, scale


def back_middle(cot, y1, unit, scale, gain, w_fc1):
    dn = nt(y1, w_fc1).astype(BF).astype(F32)
    return cot + normed_back(dn * gain, unit, scale), jnp.sum(dn * unit, 0, keepdims=True)


def mlp_grads(y2, y1, g, unit, gain):
    n2 = (unit * gain).astype(BF)
    return tn(y1, n2), [tn(y2, g[:, DIM * i : DIM * i + DIM]) for i in range(4)]


def back_attention(do, q, k, v, prob_ref, grad_ref, meanwhile=None):
    masks = head_masks()
    dqs, dks, dvs = [], [], []
    for n in range(2):
        part = slice(n * WIN, n * WIN + WIN)
        do_n, q_n, k_n, v_n = do[part], q[part], k[part], v[part]
        dp = nt(by_head(v_n, masks), do_n)
        dvs.append(from_heads(nn(prob_ref[n], do_n), masks))
        k_t = jnp.transpose(k_n.astype(F32)).astype(BF)
        ds_all, dq_t = [], []
        for h in range(HEADS):
            rows = slice(h * WIN, h * WIN + WIN)
            p = prob_ref[n, rows, :].astype(F32)
            dp_h = dp[rows].astype(BF).astype(F32)
            ds = p * (dp_h - jnp.sum(p * dp_h, 0, keepdims=True))
            if n == 0:
                grad_ref[0, rows, :] = ds[:, :128]
                grad_ref[1, rows, :16] = ds[:, 128:]
            else:
                grad_ref[0, rows, :] += ds[:, :128]
                grad_ref[1, rows, :16] += ds[:, 128:]
            ds = (ds * SCALE).astype(BF)
            ds_all.append(ds)
            dq_t.append(nn(k_t[h * HEAD : h * HEAD + HEAD], ds))
        dqs.append(jnp.transpose(jnp.concatenate(dq_t, axis=0)))
        dks.append(from_heads(nn(jnp.concatenate(ds_all, axis=0), q_n), masks))
        if n == 0 and meanwhile is not None:
            meanwhile()
    return [jnp.concatenate(parts, axis=0).astype(BF) for parts in (dqs, dks, dvs)]


def back_input(dm, d_qkv, unit, scale, gain, w_qkv):
    dn = jnp.zeros((TOK, DIM), F32)
    for i in range(3):
        dn = dn + nt(d_qkv[i], w_qkv[:, i * DIM : i * DIM + DIM])
    dn = dn.astype(BF).astype(F32)
    return dm + normed_back(dn * gain, unit, scale), jnp.sum(dn * unit, 0, keepdims=True)


def qkv_grads(d_qkv, unit, gain):
    n1 = (unit * gain).astype(BF)
    return jnp.concatenate([tn(d, n1) for d in d_qkv], axis=0)


def quarters(x):
    return {
        (n, ih, half): x[n * WIN + ih * 72 + half * 36 :][:36]
        for n in range(2)
        for ih in range(2)
        for half in range(2)
    }


def padded(pieces, rows):
    have = sum(p.shape[0] for p in pieces)
    return jnp.concatenate(list(pieces) + [jnp.zeros((rows - have, DIM), F32)], axis=0).astype(BF)


OWN = ((0, 1, 1), (1, 1, 0), (1, 1, 1))
BY_LAT = ((0, 0, 1), (1, 0, 0), (1, 0, 1))
BY_LON = ((0, 1, 0),)
BY_BOTH = ((0, 0, 0),)


def shifted(have):
    order = []
    for n in range(2):
        for ih in range(2):
            order += [(n, ih, 1), ((n + 1) % 2, ih, 0)]
    return jnp.concatenate([have[key] for key in order], axis=0)


def unshifted(x):
    have = {}
    row = 0
    for n in range(2):
        for ih in range(2):
            for key in ((n, ih, 1), ((n + 1) % 2, ih, 0)):
                have[key] = x[row : row + 36]
                row += 36
    return have


def whole_block(have):
    return jnp.concatenate(
        [have[n, ih, half] for n in range(2) for ih in range(2) for half in range(2)], axis=0
    )


def flat_rows(ref):
    return jnp.concatenate([ref[z, i].astype(F32) for z in range(2) for i in range(6)], axis=0)


MESH = pl.DeviceIdType.MESH


def ring(names):
    sizes = [lax.axis_size(name) for name in names]
    me = 0
    for name, size in zip(names, sizes):
        me = me * size + lax.axis_index(name)
    total = 1
    for size in sizes:
        total *= size

    def at(index):
        where = {}
        for name, size in reversed(list(zip(names, sizes))):
            where[name] = lax.rem(index, size)
            index = index // size
        return where

    return me, total, at


def kernel(state_in, cot_in, order_in, lanes_in, table_in, gains_in, w_qkv_in, w_proj_in, w_fc1_in, w_fc2_in,
           du_ref, qkv_ref, proj_ref, fc1_ref, fc2_ref, gain_ref, table_ref,
           state, cot, order, lanes, table, gains, w_qkv, w_proj, w_fc1, w_fc2,
           q_ref, k_ref, v_ref, o_ref, m_ref, g_ref, slope_ref, prob_first, prob_second, bias_ref, grad_ref,
           mine_ref, own_ref, *rest):
    halos, rest = rest[:18], rest[18:]
    parts, got_a, sum_a, got_b = (rest[4 * i : 4 * i + 4] for i in range(4))
    rest = rest[16:]
    sent_d, got_d, sent_e, got_e, load, send_h, recv_h, send_a, recv_a, send_b, recv_b, send_d, recv_d = rest
    loads = [
        pltpu.make_async_copy(source, target, load.at[i])
        for i, (source, target) in enumerate(
            (
                (order_in, order),
                (state_in, state),
                (cot_in, cot),
                (table_in, table),
                (lanes_in, lanes),
                (gains_in, gains),
                (w_qkv_in, w_qkv),
                (w_proj_in, w_proj),
                (w_fc1_in, w_fc1),
                (w_fc2_in, w_fc2),
            )
        )
    ]
    for copy in loads:
        copy.start()
    core = lax.axis_index("lon_2")
    chip, chip_count, chip_at = ring(LON[:2])
    lat_me, lat_count, lat_at = ring(LAT)
    lon_me, lon_count, lon_at = ring(LON)
    core_peer = {"lon_2": 1 - core}

    def chip_peer(o):
        return lax.rem(chip + o, chip_count)

    def lat_peer(o):
        return lax.rem(lat_me + o, lat_count)

    def neighbours(way):
        lat = lat_at(lax.rem(lat_me + way + lat_count, lat_count))
        lon = lon_at(lax.rem(lon_me + way + lon_count, lon_count))
        return lat, lon, {**lat, **lon}

    lower, upper = neighbours(-1), neighbours(1)
    peers = (
        [*lower, *upper, core_peer]
        + [chip_at(chip_peer(o)) for o in range(1, chip_count)]
        + [lat_at(lat_peer(o)) for o in range(1, lat_count)]
    )
    barrier = pltpu.get_barrier_semaphore()
    for device in peers:
        pl.semaphore_signal(barrier, inc=1, device_id=device, device_id_type=MESH)

    def send(source, target, sems, i, device):
        copy = pltpu.make_async_remote_copy(
            src_ref=source, dst_ref=target, send_sem=sems[0].at[i], recv_sem=sems[1].at[i],
            device_id=device, device_id_type=MESH,
        )
        copy.start()
        return copy

    def table_of(block):
        return jnp.concatenate([table[block, h] for h in range(HEADS)] + [jnp.zeros((2, POS), F32)], axis=0)

    def exchange(step, targets):
        return [
            send(halos[6 * step + i], halos[6 * step + 3 + i], (send_h, recv_h), 3 * step + i, targets[i])
            for i in range(3)
        ]

    def fill(step, have):
        for i, keys in enumerate((BY_LAT, BY_LON, BY_BOTH)):
            ref = halos[6 * step + i]
            ref[...] = padded([have[key] for key in keys], ref.shape[0])

    def arrived(step, own):
        have = {}
        for ref, keys in zip((own, *halos[6 * step + 3 : 6 * step + 6]), (OWN, BY_LAT, BY_LON, BY_BOTH)):
            rows = ref[...].astype(F32)
            for i, key in enumerate(keys):
                have[key] = rows[36 * i : 36 * i + 36]
        return have

    for copy in loads[:5]:
        copy.wait()
    perm = order[...]
    x = nn(perm, flat_rows(state).astype(BF))
    given = quarters(nn(perm, flat_rows(cot).astype(BF)))
    fill(0, given)
    expand_bias(table_of(0), lanes[...], False, bias_ref)
    for copy in loads[5:7]:
        copy.wait()
    first_gains, second_gains = gains[0], gains[1]
    early = []

    def open_halo():
        for copy in loads[7:]:
            copy.wait()
        pl.semaphore_wait(barrier, len(peers))
        early.extend(exchange(0, lower))

    q, k, v, o, m, g, slope = forward(
        x, first_gains, w_qkv[0], w_proj.at[0], w_fc1.at[0], bias_ref, None, prob_first, open_halo
    )
    out = quarters(m + nt(g, w_fc2[0]))
    fill(1, out)
    flights = early + exchange(1, lower)
    own_ref[0] = padded([out[key] for key in OWN], 112)
    own_ref[1] = padded([given[key] for key in OWN], 112)
    for ref, value in ((q_ref, q), (k_ref, k), (v_ref, v), (o_ref, o), (m_ref, m), (g_ref, g), (slope_ref, slope)):
        ref[...] = value

    expand_bias(table_of(1), lanes[...], True, bias_ref)
    row = lax.broadcasted_iota(jnp.int32, (WIN, WIN), 0)
    lane = lax.broadcasted_iota(jnp.int32, (WIN, WIN), 1)
    same_z = (row % 6 // 3) == (lane % 6 // 3)
    same_h = (row // 72) == (lane // 72)
    allowed = same_z & (same_h | (jnp.full((WIN, WIN), lat_me, jnp.int32) < lat_count - 1))
    grad_ref[...] = jnp.zeros_like(grad_ref)
    for flight in flights:
        flight.wait()
    u = shifted(arrived(1, own_ref.at[0]))
    cot_u = shifted(arrived(0, own_ref.at[1]))
    q, k, v, o, m, g, slope = forward(
        u, second_gains, w_qkv[1], w_proj.at[1], w_fc1.at[1], bias_ref, allowed, prob_second
    )
    y2, y1, unit2, scale2 = back_mlp(cot_u, m, slope, w_fc2[1])
    dm, gain2 = back_middle(cot_u, y1, unit2, scale2, second_gains[1:2], w_fc1[1])
    yp = dm.astype(BF)
    d_qkv = back_attention(nt(yp, w_proj[1]).astype(BF), q, k, v, prob_second, grad_ref)
    unit1, scale1 = normed(u)
    du, gain1 = back_input(dm, d_qkv, unit1, scale1, second_gains[0:1], w_qkv[1])
    have = unshifted(du)
    fill(2, have)
    flights = exchange(2, upper)
    mine_ref[...] = jnp.concatenate([have[key] for key in OWN] + [jnp.zeros((4, DIM), F32)], axis=0)

    flights_a, flights_b, done = [None] * 4, [None] * 4, [None] * 4

    def start_a(i):
        flights_a[i] = send(parts[i].at[pl.ds((1 - core) * 8, 8)], got_a[i], (send_a, recv_a), i, core_peer)

    def start_b(i):
        flights_a[i].wait()
        sum_a[i][...] = (parts[i][pl.ds(core * 8, 8)].astype(F32) + got_a[i][...].astype(F32)).astype(BF)
        flights_b[i] = [
            send(sum_a[i].at[chip_peer(o)], got_b[i].at[chip], (send_b, recv_b),
                 i * (chip_count - 1) + o - 1, chip_at(chip_peer(o)))
            for o in range(1, chip_count)
        ]
        got_b[i][pl.ds(chip, 1)] = sum_a[i][pl.ds(chip, 1)]

    def finish_b(i):
        for flight in flights_b[i]:
            flight.wait()
        chunk = got_b[i][0].astype(F32)
        for o in range(1, chip_count):
            chunk = chunk + got_b[i][o].astype(F32)
        if i % 2 == 0:
            rows = unfolded(chunk)
            done[i] = (jnp.transpose(rows[:48]), rows[48:])
        else:
            sums = jnp.concatenate((chunk[72:80], chunk[80:88]), axis=1)
            for h in range(HEADS):
                table_ref[1 - i // 2, h] = sums[h : h + 1, :207]
            pieces = [chunk[88 + r : 89 + r, 64 * c : 64 * c + 64] for r in range(2) for c in range(2)]
            ends = [chunk[90:91, :64], chunk[90:91, 64:]]
            gain = jnp.concatenate(pieces[:2] + ends[:1] + pieces[2:] + ends[1:], axis=0)
            done[i] = (jnp.transpose(unfolded(chunk[:72])), gain)

    pack_mlp(*mlp_grads(y2, y1, g, unit2, second_gains[1:2]), parts[0])
    start_a(0)
    pack_attention(
        qkv_grads(d_qkv, unit1, second_gains[0:1]), tn(yp, o), reduce_bias(grad_ref, lanes[...], True),
        (gain1, gain2), parts[1],
    )
    start_a(1)

    for flight in flights:
        flight.wait()
    cot_x = whole_block(arrived(2, mine_ref))
    y2, y1, unit2, scale2 = back_mlp(cot_x, m_ref[...], slope_ref[...], w_fc2[0])
    start_b(0)
    pack_mlp(*mlp_grads(y2, y1, g_ref[...], unit2, first_gains[1:2]), parts[2])
    start_a(2)
    start_b(1)
    dm, gain2 = back_middle(cot_x, y1, unit2, scale2, first_gains[1:2], w_fc1[0])
    yp = dm.astype(BF)
    do = nt(yp, w_proj[0]).astype(BF)
    d_qkv = back_attention(do, q_ref[...], k_ref[...], v_ref[...], prob_first, grad_ref, lambda: start_b(2))
    unit1, scale1 = normed(nn(order[...], flat_rows(state).astype(BF)))
    du, gain1 = back_input(dm, d_qkv, unit1, scale1, first_gains[0:1], w_qkv[0])
    pack_attention(
        qkv_grads(d_qkv, unit1, first_gains[0:1]), tn(yp, o_ref[...]), reduce_bias(grad_ref, lanes[...], False),
        (gain1, gain2), parts[3],
    )
    start_a(3)
    finish_b(0)
    finish_b(1)
    start_b(3)
    finish_b(2)
    across = jnp.concatenate([done[1][0], done[2][0], done[0][0]], axis=1)
    for a in range(16):
        low_row, right = 12 * (a // 4), 48 * (a % 4)
        piece = jnp.concatenate(
            [across[12 * a : 12 * a + 12]]
            + [done[i][1][low_row : low_row + 12, right : right + 48] for i in (2, 0)]
            + [jnp.zeros((12, 16), F32)],
            axis=1,
        )
        sent_d[a] = jnp.concatenate((piece, jnp.zeros((4, 256), F32)), axis=0).astype(BF)

    def to_latitudes(source, target, first_sem):
        return [
            send(source.at[lat_peer(o)], target.at[lat_me], (send_d, recv_d), first_sem + o - 1, lat_at(lat_peer(o)))
            for o in range(1, lat_count)
        ]

    flights_d = to_latitudes(sent_d, got_d, 0)
    got_d[pl.ds(lat_me, 1)] = sent_d[pl.ds(lat_me, 1)]
    high, low = two_pieces(du)
    flat = tn(order[...], high) + tn(order[...], low)
    for z in range(2):
        for i in range(6):
            start = (z * 6 + i) * 24
            du_ref[z, i] = flat[start : start + 24]
    finish_b(3)
    gain = jnp.concatenate((done[3][1], done[1][1]), axis=0)
    for a in range(16):
        piece = jnp.concatenate((done[3][0][12 * a : 12 * a + 12], gain, jnp.zeros((12, 16), F32)), axis=1)
        sent_e[a] = jnp.concatenate((piece, jnp.zeros((4, 128), F32)), axis=0).astype(BF)
    flights_e = to_latitudes(sent_e, got_e, lat_count - 1)
    got_e[pl.ds(lat_me, 1)] = sent_e[pl.ds(lat_me, 1)]
    for flight in flights_d:
        flight.wait()

    def summed(ref):
        total = ref[0].astype(F32)
        for o in range(1, lat_count):
            total = total + ref[o].astype(F32)
        return total

    total = summed(got_d)
    qkv_ref[:, 1, :] = total[:12, :36]
    proj_ref[:, 1, :] = total[:12, 36:48]
    for i in range(2):
        fc1_ref[:, i, :] = total[:12, 48 + 48 * i : 96 + 48 * i]
        fc2_ref[:, i, :] = total[:12, 144 + 48 * i : 192 + 48 * i]
    for flight in flights_e:
        flight.wait()
    total = summed(got_e)
    qkv_ref[:, 0, :] = total[:12, :36]
    proj_ref[:, 0, :] = total[:12, 36:48]
    for r in range(4):
        gain_ref[r // 2, r % 2 : r % 2 + 1] = jnp.concatenate(
            [total[3 * r + c : 3 * r + c + 1, 48:112] for c in range(3)], axis=1
        )


def hand_over(*refs):
    for source, target in zip(refs[:7], refs[7:]):
        target[...] = source[...]


def body(state, out_cot, qkv_weight, proj_weight, fc1_weight, fc2_weight, norm_gain, bias_table):
    vmem = pl.BlockSpec(memory_space=pltpu.VMEM)
    dma = pltpu.SemaphoreType.DMA
    args = (
        state, out_cot, token_order(), lane_order(), bias_table.reshape(2, HEADS, 1, POS), norm_gain,
        qkv_weight, proj_weight, fc1_weight, jnp.swapaxes(fc2_weight, 1, 2),
    )
    buffers = [(a.shape, a.dtype) for a in args] + [((TOK, DIM), BF)] * 4 + [
        ((TOK, DIM), F32),
        ((TOK, HID), BF),
        ((TOK, HID), BF),
        ((2, HEADS * WIN, WIN), BF),
        ((2, HEADS * WIN, WIN), BF),
        ((2, 8 * WIN, 128), F32),
        ((2, 8 * WIN, 128), F32),
        ((112, DIM), F32),
        ((2, 112, DIM), BF),
    ]
    buffers += [((112, DIM), BF), ((48, DIM), BF), ((48, DIM), BF)] * 6
    rows = (144, 96, 144, 96)
    for lead in (16, 8, 8, 8):
        buffers += [((lead, r, 128), BF) for r in rows]
    buffers += [((16, 16, 256), BF), ((16, 16, 256), BF), ((16, 16, 128), BF), ((16, 16, 128), BF)]
    shapes = (
        (2, 6, 24, DIM), (12, 2, 36), (12, 2, 12), (12, 2, 48), (12, 2, 48), (2, 2, DIM), (2, 6, 1, 207)
    )
    outs = pl.pallas_call(
        kernel,
        in_specs=[pl.BlockSpec(memory_space=pltpu.HBM)] * 10,
        out_specs=[vmem] * 7,
        out_shape=[jax.ShapeDtypeStruct(s, F32) for s in shapes],
        scratch_shapes=[pltpu.VMEM(s, d) for s, d in buffers]
        + [dma((n,)) for n in (10, 9, 9, 4, 4, 28, 28, 30, 30)],
        compiler_params=pltpu.CompilerParams(
            collective_id=0, has_side_effects=True, vmem_limit_bytes=60 * 1024 * 1024
        ),
    )(*args)
    outs = pl.pallas_call(
        hand_over,
        in_specs=[vmem] * 7,
        out_specs=[vmem] * 7,
        out_shape=[jax.ShapeDtypeStruct(s, F32) for s in shapes],
        compiler_params=pltpu.CompilerParams(vmem_limit_bytes=60 * 1024 * 1024),
    )(*outs)
    state_grad, qkv, proj, fc1, fc2, gain, table = outs
    return (
        state_grad,
        jnp.swapaxes(qkv, 0, 1),
        jnp.swapaxes(proj, 0, 1),
        jnp.swapaxes(fc1, 0, 1),
        jnp.transpose(fc2, (1, 2, 0)),
        gain,
        table.reshape(2, 1, 1, HEADS, 207),
    )


def solution(mesh):
    split = Mesh(mesh.devices.reshape(8, 2, 4, 2, 2), ("lat_0", "lat_1", "lon_0", "lon_1", "lon_2"))
    placed = (
        P(None, LAT, LON, None),
        P(None, LAT, LON, None),
        P(),
        P(),
        P(),
        P(),
        P(),
        P(None, LAT, None, None, None),
    )
    return jax.shard_map(
        body,
        mesh=split,
        in_specs=placed,
        out_specs=(
            P(None, LAT, LON, None),
            P(None, LAT, LON),
            P(None, LAT, LON),
            P(None, LAT, LON),
            P(None, LAT, LON),
            P(),
            P(None, LAT, None, None, LON),
        ),
        check_vma=False,
    )
```

```python
import jax
import jax.numpy as jnp
import ml_dtypes
import numpy as np
from jax import lax
from jax.experimental import pallas as pl
from jax.experimental.pallas import tpu as pltpu
from jax.sharding import Mesh
from jax.sharding import PartitionSpec as P

WZ = 2
WH = 6
WW = 12
LAT = ("lat_0", "lat_1")
LON = ("lon_0", "lon_1", "lon_2")
BF = jnp.bfloat16
F32 = jnp.float32
HEADS = 6
DIM = 192
HEAD = 32
WIN = 144
TOK = 288
HID = 768
POS = 3312
SCALE = HEAD**-0.5


def token_order():
    order = np.zeros((TOK, TOK), np.float32)
    row = 0
    for n in range(2):
        for ih in range(2):
            for w in range(WW):
                for z in range(2):
                    for il in range(3):
                        source = (z * 6 + ih * 3 + il) * 24 + n * WW + w
                        order[row, source] = 1
                        row += 1
    return order.astype(ml_dtypes.bfloat16)


def lane_order():
    order = np.zeros((276, 512), np.float32)
    for a in range(12):
        for d in range(23):
            order[a * 23 + d, (a // 6) * 256 + d * 6 + a % 6] = 1
    return order.astype(ml_dtypes.bfloat16)


def table_offsets(flip):
    offsets = {}
    for b in range(12):
        for a in range(12):
            hk, zk, lk = b // 6, b % 6 // 3, b % 3
            hq, zq, lq = a // 6, a % 6 // 3, a % 3
            if flip:
                hk, zk, hq, zq = 1 - hk, 1 - zk, 1 - hq, 1 - zq
            offsets[b, a] = (zq * 2 + zk) * 828 + ((hq * 3 + lq) * 6 + hk * 3 + lk) * 23
    return offsets


def nn(a, b):
    return lax.dot_general(a, b, (((1,), (0,)), ((), ())), preferred_element_type=F32)


def nt(a, b):
    return lax.dot_general(a, b, (((1,), (1,)), ((), ())), preferred_element_type=F32)


def tn(a, b):
    return lax.dot_general(a, b, (((0,), (0,)), ((), ())), preferred_element_type=F32)


def two_pieces(x):
    high = x.astype(BF)
    return high, (x - high.astype(F32)).astype(BF)


def three_pieces(x):
    high = x.astype(BF)
    rest = x - high.astype(F32)
    middle = rest.astype(BF)
    return high, middle, (rest - middle.astype(F32)).astype(BF)


def expand_bias(table, lanes, flip, bias_ref):
    offsets = table_offsets(flip)
    rows = []
    for b in range(12):
        rows.append(
            jnp.concatenate(
                [table[:, offsets[b, a] : offsets[b, a] + 23] for a in range(12)], axis=1
            )
        )
    stacked = jnp.concatenate(rows, axis=0)
    high, middle, low = three_pieces(stacked)
    spread = nn(high, lanes) + nn(middle, lanes) + nn(low, lanes)
    for b in range(12):
        block = spread[b * 8 : b * 8 + 8]
        for w in range(WW):
            start = (11 - w) * 6
            both = jnp.concatenate(
                (block[:, start : start + 72], block[:, 256 + start : 256 + start + 72]), axis=1
            )
            row = (b // 6) * 72 + w * 6 + b % 6
            right = jnp.concatenate((both[:, 128:], jnp.zeros((8, 112), F32)), axis=1)
            bias_ref[0, pl.ds(row, 8, stride=WIN), :] = both[:, :128]
            bias_ref[1, pl.ds(row, 8, stride=WIN), :] = right


def reduce_bias(grad_ref, lanes, flip):
    offsets = table_offsets(flip)
    rows = []
    for b in range(12):
        left = jnp.zeros((8, 256), F32)
        right = jnp.zeros((8, 256), F32)
        for w in range(WW):
            start = (11 - w) * 6
            row = (b // 6) * 72 + w * 6 + b % 6
            both = jnp.concatenate(
                (
                    grad_ref[0, pl.ds(row, 8, stride=WIN), :],
                    grad_ref[1, pl.ds(row, 8, stride=WIN), :][:, :16],
                ),
                axis=1,
            )
            left = left + jnp.pad(both[:, :72], ((0, 0), (start, 184 - start)))
            right = right + jnp.pad(both[:, 72:], ((0, 0), (start, 184 - start)))
        rows.append(jnp.concatenate((left, right), axis=1))
    stacked = jnp.concatenate(rows, axis=0)
    high, low = two_pieces(stacked)
    packed = nt(high, lanes) + nt(low, lanes)
    places = sorted((start, b, a) for (b, a), start in offsets.items())
    return jnp.concatenate(
        [packed[b * 8 : b * 8 + 8, a * 23 : a * 23 + 23] for _, b, a in places], axis=1
    )


def folded(rows):
    half = rows.shape[0] // 2
    right = rows[:, 128:]
    return jnp.concatenate((rows[:, :128], jnp.concatenate((right[:half], right[half:]), axis=1)), axis=0)


def unfolded(rows):
    count = rows.shape[0] // 3 * 2
    right = jnp.concatenate((rows[count:, :64], rows[count:, 64:]), axis=0)
    return jnp.concatenate((rows[:count], right), axis=1)


def place(b):
    return b % 2 * 8 + b // 4 * 2 + b // 2 % 2


def pack_mlp(fc1, fc2, out_ref):
    for b in range(16):
        rows = [fc1[48 * b : 48 * b + 48]] + [part[12 * b : 12 * b + 12] for part in fc2]
        out_ref[place(b)] = folded(jnp.concatenate(rows, axis=0)).astype(BF)


def pack_attention(qkv, proj, table, gains, out_ref):
    table = jnp.concatenate((table, jnp.zeros((8, 256), F32)), axis=1)
    ends = jnp.concatenate((gains[0][:, 128:], gains[1][:, 128:]), axis=1)
    tail = jnp.concatenate((gains[0][:, :128], gains[1][:, :128], ends, jnp.zeros((5, 128), F32)), axis=0)
    for b in range(16):
        rows = jnp.concatenate((qkv[36 * b : 36 * b + 36], proj[12 * b : 12 * b + 12]), axis=0)
        own = table[:, 207 * b : 207 * b + 207]
        own = jnp.concatenate((own, jnp.zeros((8, 49), F32)), axis=1)
        chunk = jnp.concatenate((folded(rows), own[:, :128], own[:, 128:], tail), axis=0)
        out_ref[place(b)] = chunk.astype(BF)


def normed(u):
    mean = jnp.mean(u, -1, keepdims=True)
    centred = u - mean
    scale = lax.rsqrt(jnp.mean(centred * centred, -1, keepdims=True) + 1e-05)
    return centred * scale, scale


def normed_back(grad, unit, scale):
    mean = jnp.mean(grad, -1, keepdims=True)
    product = jnp.mean(grad * unit, -1, keepdims=True)
    return scale * (grad - mean - unit * product)


def head_masks():
    lane = lax.broadcasted_iota(jnp.int32, (1, DIM), 1) // HEAD
    return [(lane == h).astype(F32) for h in range(HEADS)]


def by_head(x, masks):
    return jnp.concatenate([x * m.astype(BF) for m in masks], axis=0)


def from_heads(x, masks):
    total = x[:WIN] * masks[0]
    for h in range(1, HEADS):
        total = total + x[h * WIN : h * WIN + WIN] * masks[h]
    return total


def forward(u, gains, w_qkv, w_proj, w_fc1, bias_ref, allowed, prob_ref, meanwhile=None):
    masks = head_masks()
    unit, _ = normed(u)
    n1 = (unit * gains[0:1]).astype(BF)
    q, k, v = (
        nn(n1, w_qkv[:, i * DIM : i * DIM + DIM]) for i in range(3)
    )
    joined = []
    for n in range(2):
        part = slice(n * WIN, n * WIN + WIN)
        scores = nt(by_head(k[part].astype(BF), masks), q[part].astype(BF))
        v_t = jnp.transpose(v[part]).astype(BF)
        out_t = []
        for h in range(HEADS):
            rows = slice(h * WIN, h * WIN + WIN)
            bias = jnp.concatenate((bias_ref[0, rows, :], bias_ref[1, rows, :16]), axis=1)
            s = scores[rows] * SCALE + bias
            if allowed is not None:
                s = jnp.where(allowed, s, -1e30)
            e = jnp.exp(s - jnp.max(s, 0, keepdims=True))
            p = (e * (1.0 / jnp.sum(e, 0, keepdims=True))).astype(BF)
            prob_ref[n, rows, :] = p
            out_t.append(nn(v_t[h * HEAD : h * HEAD + HEAD], p))
        joined.append(jnp.transpose(jnp.concatenate(out_t, axis=0)))
    o = jnp.concatenate(joined, axis=0).astype(BF)
    if meanwhile is not None:
        meanwhile()
    m = u + nn(o, w_proj[...])
    unit2, _ = normed(m)
    n2 = (unit2 * gains[1:2]).astype(BF)
    e = nn(n2, w_fc1[...])
    cdf = 0.5 * (1.0 + lax.erf(e * (0.5**0.5)))
    g = (e * cdf).astype(BF)

    def slope():
        return (cdf + e * jnp.exp(e * e * -0.5) * 0.3989422804014327).astype(BF)

    return q.astype(BF), k.astype(BF), v.astype(BF), o, m, g, slope


def back_mlp(cot, m, slope, w_fc2):
    unit, scale = normed(m)
    y2 = cot.astype(BF)
    dg = nn(y2, w_fc2).astype(BF).astype(F32)
    return y2, (dg * slope.astype(F32)).astype(BF), unit, scale


def back_middle(cot, y1, unit, scale, gain, w_fc1):
    dn = nt(y1, w_fc1).astype(BF).astype(F32)
    return cot + normed_back(dn * gain, unit, scale), jnp.sum(dn * unit, 0, keepdims=True)


def mlp_grads(y2, y1, g, unit, gain):
    n2 = (unit * gain).astype(BF)
    return tn(y1, n2), [tn(y2, g[:, DIM * i : DIM * i + DIM]) for i in range(4)]


def back_attention(do, q, k, v, prob_ref, grad_ref, meanwhile=None):
    masks = head_masks()
    dqs, dks, dvs = [], [], []
    for n in range(2):
        part = slice(n * WIN, n * WIN + WIN)
        do_n, q_n, k_n, v_n = do[part], q[part], k[part], v[part]
        dp = nt(by_head(v_n, masks), do_n)
        dvs.append(from_heads(nn(prob_ref[n], do_n), masks))
        k_t = jnp.transpose(k_n.astype(F32)).astype(BF)
        ds_all, dq_t = [], []
        for h in range(HEADS):
            rows = slice(h * WIN, h * WIN + WIN)
            p = prob_ref[n, rows, :].astype(F32)
            dp_h = dp[rows].astype(BF).astype(F32)
            ds = p * (dp_h - jnp.sum(p * dp_h, 0, keepdims=True))
            if n == 0:
                grad_ref[0, rows, :] = ds[:, :128]
                grad_ref[1, rows, :16] = ds[:, 128:]
            else:
                grad_ref[0, rows, :] += ds[:, :128]
                grad_ref[1, rows, :16] += ds[:, 128:]
            ds = (ds * SCALE).astype(BF)
            ds_all.append(ds)
            dq_t.append(nn(k_t[h * HEAD : h * HEAD + HEAD], ds))
            if n == 0 and h == 2 and meanwhile is not None:
                meanwhile()
        dqs.append(jnp.transpose(jnp.concatenate(dq_t, axis=0)))
        dks.append(from_heads(nn(jnp.concatenate(ds_all, axis=0), q_n), masks))
    return [jnp.concatenate(parts, axis=0).astype(BF) for parts in (dqs, dks, dvs)]


def back_input(dm, d_qkv, unit, scale, gain, w_qkv):
    dn = jnp.zeros((TOK, DIM), F32)
    for i in range(3):
        dn = dn + nt(d_qkv[i], w_qkv[:, i * DIM : i * DIM + DIM])
    dn = dn.astype(BF).astype(F32)
    return dm + normed_back(dn * gain, unit, scale), jnp.sum(dn * unit, 0, keepdims=True)


def qkv_grads(d_qkv, unit, gain):
    n1 = (unit * gain).astype(BF)
    return jnp.concatenate([tn(d, n1) for d in d_qkv], axis=0)


def quarters(x):
    return {
        (n, ih, half): x[n * WIN + ih * 72 + half * 36 :][:36]
        for n in range(2)
        for ih in range(2)
        for half in range(2)
    }


def padded(pieces, rows):
    have = sum(p.shape[0] for p in pieces)
    return jnp.concatenate(list(pieces) + [jnp.zeros((rows - have, DIM), F32)], axis=0).astype(BF)


OWN = ((0, 1, 1), (1, 1, 0), (1, 1, 1))
BY_LAT = ((0, 0, 1), (1, 0, 0), (1, 0, 1))
BY_LON = ((0, 1, 0),)
BY_BOTH = ((0, 0, 0),)


def shifted(have):
    order = []
    for n in range(2):
        for ih in range(2):
            order += [(n, ih, 1), ((n + 1) % 2, ih, 0)]
    return jnp.concatenate([have[key] for key in order], axis=0)


def unshifted(x):
    have = {}
    row = 0
    for n in range(2):
        for ih in range(2):
            for key in ((n, ih, 1), ((n + 1) % 2, ih, 0)):
                have[key] = x[row : row + 36]
                row += 36
    return have


def whole_block(have):
    return jnp.concatenate(
        [have[n, ih, half] for n in range(2) for ih in range(2) for half in range(2)], axis=0
    )


def flat_rows(ref):
    return jnp.concatenate([ref[z, i].astype(F32) for z in range(2) for i in range(6)], axis=0)


MESH = pl.DeviceIdType.MESH


def ring(names):
    sizes = [lax.axis_size(name) for name in names]
    me = 0
    for name, size in zip(names, sizes):
        me = me * size + lax.axis_index(name)
    total = 1
    for size in sizes:
        total *= size

    def at(index):
        where = {}
        for name, size in reversed(list(zip(names, sizes))):
            where[name] = lax.rem(index, size)
            index = index // size
        return where

    return me, total, at


def farthest_first(count):
    return sorted(range(1, count), key=lambda o: -min(o, count - o))


def kernel(state_in, cot_in, order_in, lanes_in, table_in, gains_in, w_qkv_in, w_proj_in, w_fc1_in, w_fc2_in,
           du_ref, qkv_ref, proj_ref, fc1_ref, fc2_ref, gain_ref, table_ref,
           state, cot, order, lanes, table, gains, w_qkv, w_proj, w_fc1, w_fc2,
           q_ref, k_ref, v_ref, o_ref, m_ref, g_ref, slope_ref, prob_first, prob_second, bias_ref, grad_ref,
           mine_ref, own_ref, *rest):
    halos, rest = rest[:18], rest[18:]
    parts, got_a, sum_a, got_b = (rest[4 * i : 4 * i + 4] for i in range(4))
    rest = rest[16:]
    sent_d, got_d, sent_e, got_e, load, send_h, recv_h, send_a, recv_a, send_b, recv_b, send_d, recv_d = rest
    loads = [
        pltpu.make_async_copy(source, target, load.at[i])
        for i, (source, target) in enumerate(
            (
                (order_in, order),
                (state_in, state),
                (cot_in, cot),
                (table_in, table),
                (lanes_in, lanes),
                (gains_in, gains),
                (w_qkv_in, w_qkv),
                (w_proj_in, w_proj),
                (w_fc1_in, w_fc1),
                (w_fc2_in, w_fc2),
            )
        )
    ]
    for copy in loads:
        copy.start()
    core = lax.axis_index("lon_2")
    chip, chip_count, chip_at = ring(LON[:2])
    lat_me, lat_count, lat_at = ring(LAT)
    lon_me, lon_count, lon_at = ring(LON)
    core_peer = {"lon_2": 1 - core}

    def chip_peer(o):
        return lax.rem(chip + o, chip_count)

    def lat_peer(o):
        return lax.rem(lat_me + o, lat_count)

    def neighbours(way):
        lat = lat_at(lax.rem(lat_me + way + lat_count, lat_count))
        lon = lon_at(lax.rem(lon_me + way + lon_count, lon_count))
        return lat, lon, {**lat, **lon}

    lower, upper = neighbours(-1), neighbours(1)
    peers = (
        [*lower, *upper, core_peer]
        + [chip_at(chip_peer(o)) for o in range(1, chip_count)]
        + [lat_at(lat_peer(o)) for o in range(1, lat_count)]
    )
    barrier = pltpu.get_barrier_semaphore()
    for device in peers:
        pl.semaphore_signal(barrier, inc=1, device_id=device, device_id_type=MESH)

    def send(source, target, sems, i, device):
        copy = pltpu.make_async_remote_copy(
            src_ref=source, dst_ref=target, send_sem=sems[0].at[i], recv_sem=sems[1].at[i],
            device_id=device, device_id_type=MESH,
        )
        copy.start()
        return copy

    def table_of(block):
        return jnp.concatenate([table[block, h] for h in range(HEADS)] + [jnp.zeros((2, POS), F32)], axis=0)

    def exchange(step, targets):
        return [
            send(halos[6 * step + i], halos[6 * step + 3 + i], (send_h, recv_h), 3 * step + i, targets[i])
            for i in (2, 1, 0)
        ]

    def fill(step, have):
        for i, keys in enumerate((BY_LAT, BY_LON, BY_BOTH)):
            ref = halos[6 * step + i]
            ref[...] = padded([have[key] for key in keys], ref.shape[0])

    def arrived(step, own):
        have = {}
        for ref, keys in zip((own, *halos[6 * step + 3 : 6 * step + 6]), (OWN, BY_LAT, BY_LON, BY_BOTH)):
            rows = ref[...].astype(F32)
            for i, key in enumerate(keys):
                have[key] = rows[36 * i : 36 * i + 36]
        return have

    for copy in loads[:2]:
        copy.wait()
    perm = order[...]
    x = nn(perm, flat_rows(state).astype(BF))
    loads[2].wait()
    given = quarters(nn(perm, flat_rows(cot).astype(BF)))
    fill(0, given)
    for copy in loads[3:5]:
        copy.wait()
    expand_bias(table_of(0), lanes[...], False, bias_ref)
    for copy in loads[5:7]:
        copy.wait()
    first_gains, second_gains = gains[0], gains[1]
    early = []

    def open_halo():
        for copy in loads[7:]:
            copy.wait()
        pl.semaphore_wait(barrier, len(peers))
        early.extend(exchange(0, lower))

    q, k, v, o, m, g, slope = forward(
        x, first_gains, w_qkv[0], w_proj.at[0], w_fc1.at[0], bias_ref, None, prob_first, open_halo
    )
    out = quarters(m + nt(g, w_fc2[0]))
    fill(1, out)
    flights = early + exchange(1, lower)
    own_ref[0] = padded([out[key] for key in OWN], 112)
    own_ref[1] = padded([given[key] for key in OWN], 112)
    for ref, value in ((q_ref, q), (k_ref, k), (v_ref, v), (o_ref, o), (m_ref, m), (g_ref, g), (slope_ref, slope())):
        ref[...] = value

    expand_bias(table_of(1), lanes[...], True, bias_ref)
    row = lax.broadcasted_iota(jnp.int32, (WIN, WIN), 0)
    lane = lax.broadcasted_iota(jnp.int32, (WIN, WIN), 1)
    same_z = (row % 6 // 3) == (lane % 6 // 3)
    same_h = (row // 72) == (lane // 72)
    allowed = same_z & (same_h | (jnp.full((WIN, WIN), lat_me, jnp.int32) < lat_count - 1))
    grad_ref[...] = jnp.zeros_like(grad_ref)
    for flight in flights:
        flight.wait()
    u = shifted(arrived(1, own_ref.at[0]))
    cot_u = shifted(arrived(0, own_ref.at[1]))
    q, k, v, o, m, g, slope = forward(
        u, second_gains, w_qkv[1], w_proj.at[1], w_fc1.at[1], bias_ref, allowed, prob_second
    )
    y2, y1, unit2, scale2 = back_mlp(cot_u, m, slope(), w_fc2[1])
    dm, gain2 = back_middle(cot_u, y1, unit2, scale2, second_gains[1:2], w_fc1[1])
    yp = dm.astype(BF)
    d_qkv = back_attention(nt(yp, w_proj[1]).astype(BF), q, k, v, prob_second, grad_ref)
    unit1, scale1 = normed(u)
    du, gain1 = back_input(dm, d_qkv, unit1, scale1, second_gains[0:1], w_qkv[1])
    have = unshifted(du)
    fill(2, have)
    flights = exchange(2, upper)
    mine_ref[...] = jnp.concatenate([have[key] for key in OWN] + [jnp.zeros((4, DIM), F32)], axis=0)

    flights_a, flights_b, done = [None] * 4, [None] * 4, [None] * 4

    def start_a(i):
        flights_a[i] = send(parts[i].at[pl.ds((1 - core) * 8, 8)], got_a[i], (send_a, recv_a), i, core_peer)

    def start_b(i):
        flights_a[i].wait()
        sum_a[i][...] = (parts[i][pl.ds(core * 8, 8)].astype(F32) + got_a[i][...].astype(F32)).astype(BF)
        flights_b[i] = [
            send(sum_a[i].at[chip_peer(o)], got_b[i].at[chip], (send_b, recv_b),
                 i * (chip_count - 1) + o - 1, chip_at(chip_peer(o)))
            for o in farthest_first(chip_count)
        ]
        got_b[i][pl.ds(chip, 1)] = sum_a[i][pl.ds(chip, 1)]

    def finish_b(i):
        for flight in flights_b[i]:
            flight.wait()
        chunk = got_b[i][0].astype(F32)
        for o in range(1, chip_count):
            chunk = chunk + got_b[i][o].astype(F32)
        if i % 2 == 0:
            rows = unfolded(chunk)
            done[i] = (jnp.transpose(rows[:48]), rows[48:])
        else:
            sums = jnp.concatenate((chunk[72:80], chunk[80:88]), axis=1)
            for h in range(HEADS):
                table_ref[1 - i // 2, h] = sums[h : h + 1, :207]
            pieces = [chunk[88 + r : 89 + r, 64 * c : 64 * c + 64] for r in range(2) for c in range(2)]
            ends = [chunk[90:91, :64], chunk[90:91, 64:]]
            gain = jnp.concatenate(pieces[:2] + ends[:1] + pieces[2:] + ends[1:], axis=0)
            done[i] = (jnp.transpose(unfolded(chunk[:72])), gain)

    pack_mlp(*mlp_grads(y2, y1, g, unit2, second_gains[1:2]), parts[0])
    start_a(0)
    pack_attention(
        qkv_grads(d_qkv, unit1, second_gains[0:1]), tn(yp, o), reduce_bias(grad_ref, lanes[...], True),
        (gain1, gain2), parts[1],
    )
    start_a(1)

    start_b(0)
    for flight in flights:
        flight.wait()
    start_b(1)
    cot_x = whole_block(arrived(2, mine_ref))
    y2, y1, unit2, scale2 = back_mlp(cot_x, m_ref[...], slope_ref[...], w_fc2[0])
    pack_mlp(*mlp_grads(y2, y1, g_ref[...], unit2, first_gains[1:2]), parts[2])
    start_a(2)
    dm, gain2 = back_middle(cot_x, y1, unit2, scale2, first_gains[1:2], w_fc1[0])
    yp = dm.astype(BF)
    do = nt(yp, w_proj[0]).astype(BF)
    d_qkv = back_attention(do, q_ref[...], k_ref[...], v_ref[...], prob_first, grad_ref, lambda: start_b(2))
    unit1, scale1 = normed(nn(order[...], flat_rows(state).astype(BF)))
    du, gain1 = back_input(dm, d_qkv, unit1, scale1, first_gains[0:1], w_qkv[0])
    pack_attention(
        qkv_grads(d_qkv, unit1, first_gains[0:1]), tn(yp, o_ref[...]), reduce_bias(grad_ref, lanes[...], False),
        (gain1, gain2), parts[3],
    )
    start_a(3)
    finish_b(0)
    finish_b(1)
    start_b(3)
    finish_b(2)
    across = jnp.concatenate([done[1][0], done[2][0], done[0][0]], axis=1)
    for a in range(16):
        low_row, right = 12 * (a // 4), 48 * (a % 4)
        piece = jnp.concatenate(
            [across[12 * a : 12 * a + 12]]
            + [done[i][1][low_row : low_row + 12, right : right + 48] for i in (2, 0)]
            + [jnp.zeros((12, 16), F32)],
            axis=1,
        )
        sent_d[a] = jnp.concatenate((piece, jnp.zeros((4, 256), F32)), axis=0).astype(BF)

    def to_latitudes(source, target, first_sem):
        return [
            send(source.at[lat_peer(o)], target.at[lat_me], (send_d, recv_d), first_sem + o - 1, lat_at(lat_peer(o)))
            for o in farthest_first(lat_count)
        ]

    flights_d = to_latitudes(sent_d, got_d, 0)
    got_d[pl.ds(lat_me, 1)] = sent_d[pl.ds(lat_me, 1)]
    high, low = two_pieces(du)
    flat = tn(order[...], high) + tn(order[...], low)
    for z in range(2):
        for i in range(6):
            start = (z * 6 + i) * 24
            du_ref[z, i] = flat[start : start + 24]
    finish_b(3)
    gain = jnp.concatenate((done[3][1], done[1][1]), axis=0)
    for a in range(16):
        piece = jnp.concatenate((done[3][0][12 * a : 12 * a + 12], gain, jnp.zeros((12, 16), F32)), axis=1)
        sent_e[a] = jnp.concatenate((piece, jnp.zeros((4, 128), F32)), axis=0).astype(BF)
    flights_e = to_latitudes(sent_e, got_e, lat_count - 1)
    got_e[pl.ds(lat_me, 1)] = sent_e[pl.ds(lat_me, 1)]
    for flight in flights_d:
        flight.wait()

    def summed(ref):
        total = ref[0].astype(F32)
        for o in range(1, lat_count):
            total = total + ref[o].astype(F32)
        return total

    total = summed(got_d)
    qkv_ref[:, 1, :] = total[:12, :36]
    proj_ref[:, 1, :] = total[:12, 36:48]
    for i in range(2):
        fc1_ref[:, i, :] = total[:12, 48 + 48 * i : 96 + 48 * i]
        fc2_ref[:, i, :] = total[:12, 144 + 48 * i : 192 + 48 * i]
    for flight in flights_e:
        flight.wait()
    total = summed(got_e)
    qkv_ref[:, 0, :] = total[:12, :36]
    proj_ref[:, 0, :] = total[:12, 36:48]
    for r in range(4):
        gain_ref[r // 2, r % 2 : r % 2 + 1] = jnp.concatenate(
            [total[3 * r + c : 3 * r + c + 1, 48:112] for c in range(3)], axis=1
        )


def hand_over(*refs):
    for source, target in zip(refs[:7], refs[7:]):
        target[...] = source[...]


def body(state, out_cot, qkv_weight, proj_weight, fc1_weight, fc2_weight, norm_gain, bias_table):
    vmem = pl.BlockSpec(memory_space=pltpu.VMEM)
    dma = pltpu.SemaphoreType.DMA
    args = (
        state, out_cot, token_order(), lane_order(), bias_table.reshape(2, HEADS, 1, POS), norm_gain,
        qkv_weight, proj_weight, fc1_weight, jnp.swapaxes(fc2_weight, 1, 2),
    )
    buffers = [(a.shape, a.dtype) for a in args] + [((TOK, DIM), BF)] * 4 + [
        ((TOK, DIM), F32),
        ((TOK, HID), BF),
        ((TOK, HID), BF),
        ((2, HEADS * WIN, WIN), BF),
        ((2, HEADS * WIN, WIN), BF),
        ((2, 8 * WIN, 128), F32),
        ((2, 8 * WIN, 128), F32),
        ((112, DIM), F32),
        ((2, 112, DIM), BF),
    ]
    buffers += [((112, DIM), BF), ((48, DIM), BF), ((48, DIM), BF)] * 6
    rows = (144, 96, 144, 96)
    for lead in (16, 8, 8, 8):
        buffers += [((lead, r, 128), BF) for r in rows]
    buffers += [((16, 16, 256), BF), ((16, 16, 256), BF), ((16, 16, 128), BF), ((16, 16, 128), BF)]
    shapes = (
        (2, 6, 24, DIM), (12, 2, 36), (12, 2, 12), (12, 2, 48), (12, 2, 48), (2, 2, DIM), (2, 6, 1, 207)
    )
    outs = pl.pallas_call(
        kernel,
        in_specs=[pl.BlockSpec(memory_space=pltpu.HBM)] * 10,
        out_specs=[vmem] * 7,
        out_shape=[jax.ShapeDtypeStruct(s, F32) for s in shapes],
        scratch_shapes=[pltpu.VMEM(s, d) for s, d in buffers]
        + [dma((n,)) for n in (10, 9, 9, 4, 4, 28, 28, 30, 30)],
        compiler_params=pltpu.CompilerParams(
            collective_id=0, has_side_effects=True, vmem_limit_bytes=60 * 1024 * 1024
        ),
    )(*args)
    outs = pl.pallas_call(
        hand_over,
        in_specs=[vmem] * 7,
        out_specs=[vmem] * 7,
        out_shape=[jax.ShapeDtypeStruct(s, F32) for s in shapes],
        compiler_params=pltpu.CompilerParams(vmem_limit_bytes=60 * 1024 * 1024),
    )(*outs)
    state_grad, qkv, proj, fc1, fc2, gain, table = outs
    return (
        state_grad,
        jnp.swapaxes(qkv, 0, 1),
        jnp.swapaxes(proj, 0, 1),
        jnp.swapaxes(fc1, 0, 1),
        jnp.transpose(fc2, (1, 2, 0)),
        gain,
        table.reshape(2, 1, 1, HEADS, 207),
    )


def solution(mesh):
    split = Mesh(mesh.devices.reshape(8, 2, 4, 2, 2), ("lat_0", "lat_1", "lon_0", "lon_1", "lon_2"))
    placed = (
        P(None, LAT, LON, None),
        P(None, LAT, LON, None),
        P(),
        P(),
        P(),
        P(),
        P(),
        P(None, LAT, None, None, None),
    )
    return jax.shard_map(
        body,
        mesh=split,
        in_specs=placed,
        out_specs=(
            P(None, LAT, LON, None),
            P(None, LAT, LON),
            P(None, LAT, LON),
            P(None, LAT, LON),
            P(None, LAT, LON),
            P(),
            P(None, LAT, None, None, LON),
        ),
        check_vma=False,
    )
```

```python
import jax
import jax.numpy as jnp
import ml_dtypes
import numpy as np
from jax import lax
from jax.experimental import pallas as pl
from jax.experimental.pallas import tpu as pltpu
from jax.sharding import Mesh
from jax.sharding import PartitionSpec as P

WZ = 2
WH = 6
WW = 12
LAT = ("lat_0", "lat_1")
LON = ("lon_0", "lon_1", "lon_2")
BF = jnp.bfloat16
F32 = jnp.float32
HEADS = 6
DIM = 192
HEAD = 32
WIN = 144
TOK = 288
HID = 768
POS = 3312
SCALE = HEAD**-0.5


def token_order():
    order = np.zeros((TOK, TOK), np.float32)
    row = 0
    for n in range(2):
        for ih in range(2):
            for w in range(WW):
                for z in range(2):
                    for il in range(3):
                        source = (z * 6 + ih * 3 + il) * 24 + n * WW + w
                        order[row, source] = 1
                        row += 1
    return order.astype(ml_dtypes.bfloat16)


def lane_order():
    order = np.zeros((276, 512), np.float32)
    for a in range(12):
        for d in range(23):
            order[a * 23 + d, (a // 6) * 256 + d * 6 + a % 6] = 1
    return order.astype(ml_dtypes.bfloat16)


def table_offsets(flip):
    offsets = {}
    for b in range(12):
        for a in range(12):
            hk, zk, lk = b // 6, b % 6 // 3, b % 3
            hq, zq, lq = a // 6, a % 6 // 3, a % 3
            if flip:
                hk, zk, hq, zq = 1 - hk, 1 - zk, 1 - hq, 1 - zq
            offsets[b, a] = (zq * 2 + zk) * 828 + ((hq * 3 + lq) * 6 + hk * 3 + lk) * 23
    return offsets


def nn(a, b):
    return lax.dot_general(a, b, (((1,), (0,)), ((), ())), preferred_element_type=F32)


def nt(a, b):
    return lax.dot_general(a, b, (((1,), (1,)), ((), ())), preferred_element_type=F32)


def tn(a, b):
    return lax.dot_general(a, b, (((0,), (0,)), ((), ())), preferred_element_type=F32)


def two_pieces(x):
    high = x.astype(BF)
    return high, (x - high.astype(F32)).astype(BF)


def three_pieces(x):
    high = x.astype(BF)
    rest = x - high.astype(F32)
    middle = rest.astype(BF)
    return high, middle, (rest - middle.astype(F32)).astype(BF)


def expand_bias(table, lanes, flip, bias_ref):
    offsets = table_offsets(flip)
    rows = []
    for b in range(12):
        rows.append(
            jnp.concatenate(
                [table[:, offsets[b, a] : offsets[b, a] + 23] for a in range(12)], axis=1
            )
        )
    stacked = jnp.concatenate(rows, axis=0)
    high, middle, low = three_pieces(stacked)
    spread = nn(high, lanes) + nn(middle, lanes) + nn(low, lanes)
    for b in range(12):
        block = spread[b * 8 : b * 8 + 8]
        for w in range(WW):
            start = (11 - w) * 6
            both = jnp.concatenate(
                (block[:, start : start + 72], block[:, 256 + start : 256 + start + 72]), axis=1
            )
            row = (b // 6) * 72 + w * 6 + b % 6
            right = jnp.concatenate((both[:, 128:], jnp.zeros((8, 112), F32)), axis=1)
            bias_ref[0, pl.ds(row, 8, stride=WIN), :] = both[:, :128]
            bias_ref[1, pl.ds(row, 8, stride=WIN), :] = right


def reduce_bias(grad_ref, lanes, flip):
    offsets = table_offsets(flip)
    rows = []
    for b in range(12):
        left = jnp.zeros((8, 256), F32)
        right = jnp.zeros((8, 256), F32)
        for w in range(WW):
            start = (11 - w) * 6
            row = (b // 6) * 72 + w * 6 + b % 6
            both = jnp.concatenate(
                (
                    grad_ref[0, pl.ds(row, 8, stride=WIN), :],
                    grad_ref[1, pl.ds(row, 8, stride=WIN), :][:, :16],
                ),
                axis=1,
            )
            left = left + jnp.pad(both[:, :72], ((0, 0), (start, 184 - start)))
            right = right + jnp.pad(both[:, 72:], ((0, 0), (start, 184 - start)))
        rows.append(jnp.concatenate((left, right), axis=1))
    stacked = jnp.concatenate(rows, axis=0)
    high, low = two_pieces(stacked)
    packed = nt(high, lanes) + nt(low, lanes)
    places = sorted((start, b, a) for (b, a), start in offsets.items())
    return jnp.concatenate(
        [packed[b * 8 : b * 8 + 8, a * 23 : a * 23 + 23] for _, b, a in places], axis=1
    )


def folded(rows):
    half = rows.shape[0] // 2
    right = rows[:, 128:]
    return jnp.concatenate((rows[:, :128], jnp.concatenate((right[:half], right[half:]), axis=1)), axis=0)


def unfolded(rows):
    count = rows.shape[0] // 3 * 2
    right = jnp.concatenate((rows[count:, :64], rows[count:, 64:]), axis=0)
    return jnp.concatenate((rows[:count], right), axis=1)


def place(b):
    return b % 2 * 8 + b // 4 * 2 + b // 2 % 2


def pack_mlp(fc1, fc2, out_ref):
    for b in range(16):
        rows = [fc1[48 * b : 48 * b + 48]] + [part[12 * b : 12 * b + 12] for part in fc2]
        out_ref[place(b)] = folded(jnp.concatenate(rows, axis=0)).astype(BF)


def pack_attention(qkv, proj, table, gains, out_ref):
    table = jnp.concatenate((table, jnp.zeros((8, 256), F32)), axis=1)
    ends = jnp.concatenate((gains[0][:, 128:], gains[1][:, 128:]), axis=1)
    tail = jnp.concatenate((gains[0][:, :128], gains[1][:, :128], ends, jnp.zeros((5, 128), F32)), axis=0)
    for b in range(16):
        rows = jnp.concatenate((qkv[36 * b : 36 * b + 36], proj[12 * b : 12 * b + 12]), axis=0)
        own = table[:, 207 * b : 207 * b + 207]
        own = jnp.concatenate((own, jnp.zeros((8, 49), F32)), axis=1)
        chunk = jnp.concatenate((folded(rows), own[:, :128], own[:, 128:], tail), axis=0)
        out_ref[place(b)] = chunk.astype(BF)


def normed(u):
    mean = jnp.mean(u, -1, keepdims=True)
    centred = u - mean
    scale = lax.rsqrt(jnp.mean(centred * centred, -1, keepdims=True) + 1e-05)
    return centred * scale, scale


def normed_back(grad, unit, scale):
    mean = jnp.mean(grad, -1, keepdims=True)
    product = jnp.mean(grad * unit, -1, keepdims=True)
    return scale * (grad - mean - unit * product)


def head_masks():
    lane = lax.broadcasted_iota(jnp.int32, (1, DIM), 1) // HEAD
    return [(lane == h).astype(F32) for h in range(HEADS)]


def by_head(x, masks):
    return jnp.concatenate([x * m.astype(BF) for m in masks], axis=0)


def from_heads(x, masks):
    total = x[:WIN] * masks[0]
    for h in range(1, HEADS):
        total = total + x[h * WIN : h * WIN + WIN] * masks[h]
    return total


def forward(u, gains, w_qkv, w_proj, w_fc1, bias_ref, allowed, prob_ref, meanwhile=None):
    masks = head_masks()
    unit, _ = normed(u)
    n1 = (unit * gains[0:1]).astype(BF)
    q, k, v = (
        nn(n1, w_qkv[:, i * DIM : i * DIM + DIM]) for i in range(3)
    )
    joined = []
    for n in range(2):
        part = slice(n * WIN, n * WIN + WIN)
        scores = nt(by_head(k[part].astype(BF), masks), q[part].astype(BF))
        v_t = jnp.transpose(v[part]).astype(BF)
        out_t = []
        for h in range(HEADS):
            rows = slice(h * WIN, h * WIN + WIN)
            bias = jnp.concatenate((bias_ref[0, rows, :], bias_ref[1, rows, :16]), axis=1)
            s = scores[rows] * SCALE + bias
            if allowed is not None:
                s = jnp.where(allowed, s, -1e30)
            e = jnp.exp(s - jnp.max(s, 0, keepdims=True))
            p = (e * (1.0 / jnp.sum(e, 0, keepdims=True))).astype(BF)
            prob_ref[n, rows, :] = p
            out_t.append(nn(v_t[h * HEAD : h * HEAD + HEAD], p))
        joined.append(jnp.transpose(jnp.concatenate(out_t, axis=0)))
    o = jnp.concatenate(joined, axis=0).astype(BF)
    if meanwhile is not None:
        meanwhile()
    m = u + nn(o, w_proj[...])
    unit2, _ = normed(m)
    n2 = (unit2 * gains[1:2]).astype(BF)
    e = nn(n2, w_fc1[...])
    cdf = 0.5 * (1.0 + lax.erf(e * (0.5**0.5)))
    g = (e * cdf).astype(BF)

    def slope():
        return (cdf + e * jnp.exp(e * e * -0.5) * 0.3989422804014327).astype(BF)

    return q.astype(BF), k.astype(BF), v.astype(BF), o, m, g, slope


def back_mlp(cot, m, slope, w_fc2):
    unit, scale = normed(m)
    y2 = cot.astype(BF)
    dg = nn(y2, w_fc2).astype(BF).astype(F32)
    return y2, (dg * slope.astype(F32)).astype(BF), unit, scale


def back_middle(cot, y1, unit, scale, gain, w_fc1):
    dn = nt(y1, w_fc1).astype(BF).astype(F32)
    return cot + normed_back(dn * gain, unit, scale), jnp.sum(dn * unit, 0, keepdims=True)


def mlp_grads(y2, y1, g, unit, gain):
    n2 = (unit * gain).astype(BF)
    return tn(y1, n2), [tn(y2, g[:, DIM * i : DIM * i + DIM]) for i in range(4)]


def back_attention(do, q, k, v, prob_ref, grad_ref, meanwhile=None):
    masks = head_masks()
    dqs, dks, dvs = [], [], []
    for n in range(2):
        part = slice(n * WIN, n * WIN + WIN)
        do_n, q_n, k_n, v_n = do[part], q[part], k[part], v[part]
        dp = nt(by_head(v_n, masks), do_n)
        dvs.append(from_heads(nn(prob_ref[n], do_n), masks))
        k_t = jnp.transpose(k_n.astype(F32)).astype(BF)
        ds_all, dq_t = [], []
        for h in range(HEADS):
            rows = slice(h * WIN, h * WIN + WIN)
            p = prob_ref[n, rows, :].astype(F32)
            dp_h = dp[rows].astype(BF).astype(F32)
            ds = p * (dp_h - jnp.sum(p * dp_h, 0, keepdims=True))
            if n == 0:
                grad_ref[0, rows, :] = ds[:, :128]
                grad_ref[1, rows, :16] = ds[:, 128:]
            else:
                grad_ref[0, rows, :] += ds[:, :128]
                grad_ref[1, rows, :16] += ds[:, 128:]
            ds = (ds * SCALE).astype(BF)
            ds_all.append(ds)
            dq_t.append(nn(k_t[h * HEAD : h * HEAD + HEAD], ds))
            if n == 0 and h == 2 and meanwhile is not None:
                meanwhile()
        dqs.append(jnp.transpose(jnp.concatenate(dq_t, axis=0)))
        dks.append(from_heads(nn(jnp.concatenate(ds_all, axis=0), q_n), masks))
    return [jnp.concatenate(parts, axis=0).astype(BF) for parts in (dqs, dks, dvs)]


def back_input(dm, d_qkv, unit, scale, gain, w_qkv):
    dn = jnp.zeros((TOK, DIM), F32)
    for i in range(3):
        dn = dn + nt(d_qkv[i], w_qkv[:, i * DIM : i * DIM + DIM])
    dn = dn.astype(BF).astype(F32)
    return dm + normed_back(dn * gain, unit, scale), jnp.sum(dn * unit, 0, keepdims=True)


def qkv_grads(d_qkv, unit, gain):
    n1 = (unit * gain).astype(BF)
    return jnp.concatenate([tn(d, n1) for d in d_qkv], axis=0)


def quarters(x):
    return {
        (n, ih, half): x[n * WIN + ih * 72 + half * 36 :][:36]
        for n in range(2)
        for ih in range(2)
        for half in range(2)
    }


def padded(pieces, rows):
    have = sum(p.shape[0] for p in pieces)
    return jnp.concatenate(list(pieces) + [jnp.zeros((rows - have, DIM), F32)], axis=0).astype(BF)


OWN = ((0, 1, 1), (1, 1, 0), (1, 1, 1))
BY_LAT = ((0, 0, 1), (1, 0, 0), (1, 0, 1))
BY_LON = ((0, 1, 0),)
BY_BOTH = ((0, 0, 0),)


def shifted(have):
    order = []
    for n in range(2):
        for ih in range(2):
            order += [(n, ih, 1), ((n + 1) % 2, ih, 0)]
    return jnp.concatenate([have[key] for key in order], axis=0)


def unshifted(x):
    have = {}
    row = 0
    for n in range(2):
        for ih in range(2):
            for key in ((n, ih, 1), ((n + 1) % 2, ih, 0)):
                have[key] = x[row : row + 36]
                row += 36
    return have


def whole_block(have):
    return jnp.concatenate(
        [have[n, ih, half] for n in range(2) for ih in range(2) for half in range(2)], axis=0
    )


def flat_rows(ref):
    return jnp.concatenate([ref[z, i].astype(F32) for z in range(2) for i in range(6)], axis=0)


MESH = pl.DeviceIdType.MESH


def ring(names):
    sizes = [lax.axis_size(name) for name in names]
    me = 0
    for name, size in zip(names, sizes):
        me = me * size + lax.axis_index(name)
    total = 1
    for size in sizes:
        total *= size

    def at(index):
        where = {}
        for name, size in reversed(list(zip(names, sizes))):
            where[name] = lax.rem(index, size)
            index = index // size
        return where

    return me, total, at


def farthest_first(count):
    return sorted(range(1, count), key=lambda o: -min(o, count - o))


def kernel(state_in, cot_in, order_in, lanes_in, table_in, gains_in, w_qkv_in, w_proj_in, w_fc1_in, w_fc2_in,
           du_ref, qkv_ref, proj_ref, fc1_ref, fc2_ref, gain_ref, table_ref,
           state, cot, order, lanes, table, gains, w_qkv, w_proj, w_fc1, w_fc2,
           q_ref, k_ref, v_ref, o_ref, m_ref, g_ref, slope_ref, prob_first, prob_second, bias_ref, grad_ref,
           mine_ref, own_ref, *rest):
    halos, rest = rest[:18], rest[18:]
    parts, got_a, sum_a, got_b = (rest[4 * i : 4 * i + 4] for i in range(4))
    rest = rest[16:]
    sent_d, got_d, sent_e, got_e, load, send_h, recv_h, send_a, recv_a, send_b, recv_b, send_d, recv_d = rest
    core = lax.axis_index("lon_2")
    chip, chip_count, chip_at = ring(LON[:2])
    lat_me, lat_count, lat_at = ring(LAT)
    lon_me, lon_count, lon_at = ring(LON)
    core_peer = {"lon_2": 1 - core}

    def chip_peer(o):
        return lax.rem(chip + o, chip_count)

    def lat_peer(o):
        return lax.rem(lat_me + o, lat_count)

    def neighbours(way):
        lat = lat_at(lax.rem(lat_me + way + lat_count, lat_count))
        lon = lon_at(lax.rem(lon_me + way + lon_count, lon_count))
        return lat, lon, {**lat, **lon}

    lower, upper = neighbours(-1), neighbours(1)
    peers = (
        [lat_at(lat_peer(o)) for o in farthest_first(lat_count)]
        + [chip_at(chip_peer(o)) for o in farthest_first(chip_count)]
        + [*reversed(lower), *reversed(upper), core_peer]
    )
    barrier = pltpu.get_barrier_semaphore()
    for device in peers:
        pl.semaphore_signal(barrier, inc=1, device_id=device, device_id_type=MESH)
    loads = [
        pltpu.make_async_copy(source, target, load.at[i])
        for i, (source, target) in enumerate(
            (
                (order_in, order),
                (state_in, state),
                (cot_in, cot),
                (table_in, table),
                (lanes_in, lanes),
                (gains_in, gains),
                (w_qkv_in, w_qkv),
                (w_proj_in, w_proj),
                (w_fc1_in, w_fc1),
                (w_fc2_in, w_fc2),
            )
        )
    ]
    for copy in loads:
        copy.start()

    def send(source, target, sems, i, device):
        copy = pltpu.make_async_remote_copy(
            src_ref=source, dst_ref=target, send_sem=sems[0].at[i], recv_sem=sems[1].at[i],
            device_id=device, device_id_type=MESH,
        )
        copy.start()
        return copy

    def table_of(block):
        return jnp.concatenate([table[block, h] for h in range(HEADS)] + [jnp.zeros((2, POS), F32)], axis=0)

    def exchange(step, targets):
        return [
            send(halos[6 * step + i], halos[6 * step + 3 + i], (send_h, recv_h), 3 * step + i, targets[i])
            for i in (2, 1, 0)
        ]

    def fill(step, have):
        for i, keys in enumerate((BY_LAT, BY_LON, BY_BOTH)):
            ref = halos[6 * step + i]
            ref[...] = padded([have[key] for key in keys], ref.shape[0])

    def arrived(step, own):
        have = {}
        for ref, keys in zip((own, *halos[6 * step + 3 : 6 * step + 6]), (OWN, BY_LAT, BY_LON, BY_BOTH)):
            rows = ref[...].astype(F32)
            for i, key in enumerate(keys):
                have[key] = rows[36 * i : 36 * i + 36]
        return have

    for copy in loads[:2]:
        copy.wait()
    perm = order[...]
    x = nn(perm, flat_rows(state).astype(BF))
    loads[2].wait()
    given = quarters(nn(perm, flat_rows(cot).astype(BF)))
    fill(0, given)
    for copy in loads[3:5]:
        copy.wait()
    expand_bias(table_of(0), lanes[...], False, bias_ref)
    for copy in loads[5:7]:
        copy.wait()
    first_gains, second_gains = gains[0], gains[1]

    def rest_of_loads():
        for copy in loads[7:]:
            copy.wait()

    q, k, v, o, m, g, slope = forward(
        x, first_gains, w_qkv[0], w_proj.at[0], w_fc1.at[0], bias_ref, None, prob_first, rest_of_loads
    )
    out = quarters(m + nt(g, w_fc2[0]))
    fill(1, out)
    pl.semaphore_wait(barrier, len(peers))
    flights = exchange(1, lower)
    later_flights = exchange(0, lower)
    own_ref[0] = padded([out[key] for key in OWN], 112)
    own_ref[1] = padded([given[key] for key in OWN], 112)
    for ref, value in ((q_ref, q), (k_ref, k), (v_ref, v), (o_ref, o), (m_ref, m), (g_ref, g), (slope_ref, slope())):
        ref[...] = value

    expand_bias(table_of(1), lanes[...], True, bias_ref)
    row = lax.broadcasted_iota(jnp.int32, (WIN, WIN), 0)
    lane = lax.broadcasted_iota(jnp.int32, (WIN, WIN), 1)
    same_z = (row % 6 // 3) == (lane % 6 // 3)
    same_h = (row // 72) == (lane // 72)
    allowed = same_z & (same_h | (jnp.full((WIN, WIN), lat_me, jnp.int32) < lat_count - 1))
    grad_ref[...] = jnp.zeros_like(grad_ref)
    for flight in flights:
        flight.wait()
    u = shifted(arrived(1, own_ref.at[0]))
    q, k, v, o, m, g, slope = forward(
        u, second_gains, w_qkv[1], w_proj.at[1], w_fc1.at[1], bias_ref, allowed, prob_second
    )
    for flight in later_flights:
        flight.wait()
    cot_u = shifted(arrived(0, own_ref.at[1]))
    y2, y1, unit2, scale2 = back_mlp(cot_u, m, slope(), w_fc2[1])
    dm, gain2 = back_middle(cot_u, y1, unit2, scale2, second_gains[1:2], w_fc1[1])
    yp = dm.astype(BF)
    d_qkv = back_attention(nt(yp, w_proj[1]).astype(BF), q, k, v, prob_second, grad_ref)
    unit1, scale1 = normed(u)
    du, gain1 = back_input(dm, d_qkv, unit1, scale1, second_gains[0:1], w_qkv[1])
    have = unshifted(du)
    fill(2, have)
    flights = exchange(2, upper)
    mine_ref[...] = jnp.concatenate([have[key] for key in OWN] + [jnp.zeros((4, DIM), F32)], axis=0)

    flights_a, flights_b, done = [None] * 4, [None] * 4, [None] * 4

    def start_a(i):
        flights_a[i] = send(parts[i].at[pl.ds((1 - core) * 8, 8)], got_a[i], (send_a, recv_a), i, core_peer)

    def start_b(i):
        flights_a[i].wait()
        sum_a[i][...] = (parts[i][pl.ds(core * 8, 8)].astype(F32) + got_a[i][...].astype(F32)).astype(BF)
        flights_b[i] = [
            send(sum_a[i].at[chip_peer(o)], got_b[i].at[chip], (send_b, recv_b),
                 i * (chip_count - 1) + o - 1, chip_at(chip_peer(o)))
            for o in farthest_first(chip_count)
        ]
        got_b[i][pl.ds(chip, 1)] = sum_a[i][pl.ds(chip, 1)]

    def finish_b(i):
        for flight in flights_b[i]:
            flight.wait()
        chunk = got_b[i][0].astype(F32)
        for o in range(1, chip_count):
            chunk = chunk + got_b[i][o].astype(F32)
        if i % 2 == 0:
            rows = unfolded(chunk)
            done[i] = (jnp.transpose(rows[:48]), rows[48:])
        else:
            sums = jnp.concatenate((chunk[72:80], chunk[80:88]), axis=1)
            for h in range(HEADS):
                table_ref[1 - i // 2, h] = sums[h : h + 1, :207]
            pieces = [chunk[88 + r : 89 + r, 64 * c : 64 * c + 64] for r in range(2) for c in range(2)]
            ends = [chunk[90:91, :64], chunk[90:91, 64:]]
            gain = jnp.concatenate(pieces[:2] + ends[:1] + pieces[2:] + ends[1:], axis=0)
            done[i] = (jnp.transpose(unfolded(chunk[:72])), gain)

    pack_mlp(*mlp_grads(y2, y1, g, unit2, second_gains[1:2]), parts[0])
    start_a(0)
    pack_attention(
        qkv_grads(d_qkv, unit1, second_gains[0:1]), tn(yp, o), reduce_bias(grad_ref, lanes[...], True),
        (gain1, gain2), parts[1],
    )
    start_a(1)

    start_b(0)
    for flight in flights:
        flight.wait()
    start_b(1)
    cot_x = whole_block(arrived(2, mine_ref))
    y2, y1, unit2, scale2 = back_mlp(cot_x, m_ref[...], slope_ref[...], w_fc2[0])
    pack_mlp(*mlp_grads(y2, y1, g_ref[...], unit2, first_gains[1:2]), parts[2])
    start_a(2)
    dm, gain2 = back_middle(cot_x, y1, unit2, scale2, first_gains[1:2], w_fc1[0])
    yp = dm.astype(BF)
    do = nt(yp, w_proj[0]).astype(BF)
    d_qkv = back_attention(do, q_ref[...], k_ref[...], v_ref[...], prob_first, grad_ref, lambda: start_b(2))
    unit1, scale1 = normed(nn(order[...], flat_rows(state).astype(BF)))
    du, gain1 = back_input(dm, d_qkv, unit1, scale1, first_gains[0:1], w_qkv[0])
    pack_attention(
        qkv_grads(d_qkv, unit1, first_gains[0:1]), tn(yp, o_ref[...]), reduce_bias(grad_ref, lanes[...], False),
        (gain1, gain2), parts[3],
    )
    start_a(3)
    finish_b(0)
    finish_b(1)
    start_b(3)
    finish_b(2)
    across = jnp.concatenate([done[1][0], done[2][0], done[0][0]], axis=1)
    for a in range(16):
        low_row, right = 12 * (a // 4), 48 * (a % 4)
        piece = jnp.concatenate(
            [across[12 * a : 12 * a + 12]]
            + [done[i][1][low_row : low_row + 12, right : right + 48] for i in (2, 0)]
            + [jnp.zeros((12, 16), F32)],
            axis=1,
        )
        sent_d[a] = jnp.concatenate((piece, jnp.zeros((4, 256), F32)), axis=0).astype(BF)

    def to_latitudes(source, target, first_sem):
        return [
            send(source.at[lat_peer(o)], target.at[lat_me], (send_d, recv_d), first_sem + o - 1, lat_at(lat_peer(o)))
            for o in farthest_first(lat_count)
        ]

    flights_d = to_latitudes(sent_d, got_d, 0)
    got_d[pl.ds(lat_me, 1)] = sent_d[pl.ds(lat_me, 1)]
    high, low = two_pieces(du)
    flat = tn(order[...], high) + tn(order[...], low)
    for z in range(2):
        for i in range(6):
            start = (z * 6 + i) * 24
            du_ref[z, i] = flat[start : start + 24]
    finish_b(3)
    gain = jnp.concatenate((done[3][1], done[1][1]), axis=0)
    for a in range(16):
        piece = jnp.concatenate((done[3][0][12 * a : 12 * a + 12], gain, jnp.zeros((12, 16), F32)), axis=1)
        sent_e[a] = jnp.concatenate((piece, jnp.zeros((4, 128), F32)), axis=0).astype(BF)
    flights_e = to_latitudes(sent_e, got_e, lat_count - 1)
    got_e[pl.ds(lat_me, 1)] = sent_e[pl.ds(lat_me, 1)]
    for flight in flights_d:
        flight.wait()

    def summed(ref):
        total = ref[0].astype(F32)
        for o in range(1, lat_count):
            total = total + ref[o].astype(F32)
        return total

    total = summed(got_d)
    qkv_ref[:, 1, :] = total[:12, :36]
    proj_ref[:, 1, :] = total[:12, 36:48]
    for i in range(2):
        fc1_ref[:, i, :] = total[:12, 48 + 48 * i : 96 + 48 * i]
        fc2_ref[:, i, :] = total[:12, 144 + 48 * i : 192 + 48 * i]
    for flight in flights_e:
        flight.wait()
    total = summed(got_e)
    qkv_ref[:, 0, :] = total[:12, :36]
    proj_ref[:, 0, :] = total[:12, 36:48]
    for r in range(4):
        gain_ref[r // 2, r % 2 : r % 2 + 1] = jnp.concatenate(
            [total[3 * r + c : 3 * r + c + 1, 48:112] for c in range(3)], axis=1
        )


def hand_over(*refs):
    for source, target in zip(refs[:7], refs[7:]):
        target[...] = source[...]


def body(state, out_cot, qkv_weight, proj_weight, fc1_weight, fc2_weight, norm_gain, bias_table):
    vmem = pl.BlockSpec(memory_space=pltpu.VMEM)
    dma = pltpu.SemaphoreType.DMA
    args = (
        state, out_cot, token_order(), lane_order(), bias_table.reshape(2, HEADS, 1, POS), norm_gain,
        qkv_weight, proj_weight, fc1_weight, jnp.swapaxes(fc2_weight, 1, 2),
    )
    buffers = [(a.shape, a.dtype) for a in args] + [((TOK, DIM), BF)] * 4 + [
        ((TOK, DIM), F32),
        ((TOK, HID), BF),
        ((TOK, HID), BF),
        ((2, HEADS * WIN, WIN), BF),
        ((2, HEADS * WIN, WIN), BF),
        ((2, 8 * WIN, 128), F32),
        ((2, 8 * WIN, 128), F32),
        ((112, DIM), F32),
        ((2, 112, DIM), BF),
    ]
    buffers += [((112, DIM), BF), ((48, DIM), BF), ((48, DIM), BF)] * 6
    rows = (144, 96, 144, 96)
    for lead in (16, 8, 8, 8):
        buffers += [((lead, r, 128), BF) for r in rows]
    buffers += [((16, 16, 256), BF), ((16, 16, 256), BF), ((16, 16, 128), BF), ((16, 16, 128), BF)]
    shapes = (
        (2, 6, 24, DIM), (12, 2, 36), (12, 2, 12), (12, 2, 48), (12, 2, 48), (2, 2, DIM), (2, 6, 1, 207)
    )
    outs = pl.pallas_call(
        kernel,
        in_specs=[pl.BlockSpec(memory_space=pltpu.HBM)] * 10,
        out_specs=[vmem] * 7,
        out_shape=[jax.ShapeDtypeStruct(s, F32) for s in shapes],
        scratch_shapes=[pltpu.VMEM(s, d) for s, d in buffers]
        + [dma((n,)) for n in (10, 9, 9, 4, 4, 28, 28, 30, 30)],
        compiler_params=pltpu.CompilerParams(
            collective_id=0, has_side_effects=True, vmem_limit_bytes=60 * 1024 * 1024
        ),
    )(*args)
    outs = pl.pallas_call(
        hand_over,
        in_specs=[vmem] * 7,
        out_specs=[vmem] * 7,
        out_shape=[jax.ShapeDtypeStruct(s, F32) for s in shapes],
        compiler_params=pltpu.CompilerParams(vmem_limit_bytes=60 * 1024 * 1024),
    )(*outs)
    state_grad, qkv, proj, fc1, fc2, gain, table = outs
    return (
        state_grad,
        jnp.swapaxes(qkv, 0, 1),
        jnp.swapaxes(proj, 0, 1),
        jnp.swapaxes(fc1, 0, 1),
        jnp.transpose(fc2, (1, 2, 0)),
        gain,
        table.reshape(2, 1, 1, HEADS, 207),
    )


def solution(mesh):
    split = Mesh(mesh.devices.reshape(8, 2, 4, 2, 2), ("lat_0", "lat_1", "lon_0", "lon_1", "lon_2"))
    placed = (
        P(None, LAT, LON, None),
        P(None, LAT, LON, None),
        P(),
        P(),
        P(),
        P(),
        P(),
        P(None, LAT, None, None, None),
    )
    return jax.shard_map(
        body,
        mesh=split,
        in_specs=placed,
        out_specs=(
            P(None, LAT, LON, None),
            P(None, LAT, LON),
            P(None, LAT, LON),
            P(None, LAT, LON),
            P(None, LAT, LON),
            P(),
            P(None, LAT, None, None, LON),
        ),
        check_vma=False,
    )
```

```python
import jax
import jax.numpy as jnp
import ml_dtypes
import numpy as np
from jax import lax
from jax.experimental import pallas as pl
from jax.experimental.pallas import tpu as pltpu
from jax.sharding import Mesh
from jax.sharding import PartitionSpec as P

WZ = 2
WH = 6
WW = 12
LAT = ("lat_0", "lat_1")
LON = ("lon_0", "lon_1", "lon_2")
BF = jnp.bfloat16
F32 = jnp.float32
HEADS = 6
DIM = 192
HEAD = 32
WIN = 144
TOK = 288
HID = 768
POS = 3312
SCALE = HEAD**-0.5


def token_order():
    order = np.zeros((TOK, TOK), np.float32)
    row = 0
    for n in range(2):
        for ih in range(2):
            for w in range(WW):
                for z in range(2):
                    for il in range(3):
                        source = (z * 6 + ih * 3 + il) * 24 + n * WW + w
                        order[row, source] = 1
                        row += 1
    return order.astype(ml_dtypes.bfloat16)


def lane_order():
    order = np.zeros((276, 512), np.float32)
    for a in range(12):
        for d in range(23):
            order[a * 23 + d, (a // 6) * 256 + d * 6 + a % 6] = 1
    return order.astype(ml_dtypes.bfloat16)


def table_offsets(flip):
    offsets = {}
    for b in range(12):
        for a in range(12):
            hk, zk, lk = b // 6, b % 6 // 3, b % 3
            hq, zq, lq = a // 6, a % 6 // 3, a % 3
            if flip:
                hk, zk, hq, zq = 1 - hk, 1 - zk, 1 - hq, 1 - zq
            offsets[b, a] = (zq * 2 + zk) * 828 + ((hq * 3 + lq) * 6 + hk * 3 + lk) * 23
    return offsets


def nn(a, b):
    return lax.dot_general(a, b, (((1,), (0,)), ((), ())), preferred_element_type=F32)


def nt(a, b):
    return lax.dot_general(a, b, (((1,), (1,)), ((), ())), preferred_element_type=F32)


def tn(a, b):
    return lax.dot_general(a, b, (((0,), (0,)), ((), ())), preferred_element_type=F32)


def two_pieces(x):
    high = x.astype(BF)
    return high, (x - high.astype(F32)).astype(BF)


def three_pieces(x):
    high = x.astype(BF)
    rest = x - high.astype(F32)
    middle = rest.astype(BF)
    return high, middle, (rest - middle.astype(F32)).astype(BF)


def expand_bias(table, lanes, flip, bias_ref):
    offsets = table_offsets(flip)
    rows = []
    for b in range(12):
        rows.append(
            jnp.concatenate(
                [table[:, offsets[b, a] : offsets[b, a] + 23] for a in range(12)], axis=1
            )
        )
    stacked = jnp.concatenate(rows, axis=0)
    high, middle, low = three_pieces(stacked)
    spread = nn(high, lanes) + nn(middle, lanes) + nn(low, lanes)
    for b in range(12):
        block = spread[b * 8 : b * 8 + 8]
        for w in range(WW):
            start = (11 - w) * 6
            both = jnp.concatenate(
                (block[:, start : start + 72], block[:, 256 + start : 256 + start + 72]), axis=1
            )
            row = (b // 6) * 72 + w * 6 + b % 6
            right = jnp.concatenate((both[:, 128:], jnp.zeros((8, 112), F32)), axis=1)
            bias_ref[0, pl.ds(row, 8, stride=WIN), :] = both[:, :128]
            bias_ref[1, pl.ds(row, 8, stride=WIN), :] = right


def reduce_bias(grad_ref, lanes, flip):
    offsets = table_offsets(flip)
    rows = []
    for b in range(12):
        left = jnp.zeros((8, 256), F32)
        right = jnp.zeros((8, 256), F32)
        for w in range(WW):
            start = (11 - w) * 6
            row = (b // 6) * 72 + w * 6 + b % 6
            both = jnp.concatenate(
                (
                    grad_ref[0, pl.ds(row, 8, stride=WIN), :],
                    grad_ref[1, pl.ds(row, 8, stride=WIN), :][:, :16],
                ),
                axis=1,
            )
            left = left + jnp.pad(both[:, :72], ((0, 0), (start, 184 - start)))
            right = right + jnp.pad(both[:, 72:], ((0, 0), (start, 184 - start)))
        rows.append(jnp.concatenate((left, right), axis=1))
    stacked = jnp.concatenate(rows, axis=0)
    high, low = two_pieces(stacked)
    packed = nt(high, lanes) + nt(low, lanes)
    places = sorted((start, b, a) for (b, a), start in offsets.items())
    return jnp.concatenate(
        [packed[b * 8 : b * 8 + 8, a * 23 : a * 23 + 23] for _, b, a in places], axis=1
    )


def folded(rows):
    half = rows.shape[0] // 2
    right = rows[:, 128:]
    return jnp.concatenate((rows[:, :128], jnp.concatenate((right[:half], right[half:]), axis=1)), axis=0)


def unfolded(rows):
    count = rows.shape[0] // 3 * 2
    right = jnp.concatenate((rows[count:, :64], rows[count:, 64:]), axis=0)
    return jnp.concatenate((rows[:count], right), axis=1)


def place(b):
    return b % 2 * 8 + b // 4 * 2 + b // 2 % 2


def pack_mlp(fc1, fc2, out_ref):
    for b in range(16):
        rows = [fc1[48 * b : 48 * b + 48]] + [part[12 * b : 12 * b + 12] for part in fc2]
        out_ref[place(b)] = folded(jnp.concatenate(rows, axis=0)).astype(BF)


def pack_attention(qkv, proj, table, gains, out_ref):
    table = jnp.concatenate((table, jnp.zeros((8, 256), F32)), axis=1)
    ends = jnp.concatenate((gains[0][:, 128:], gains[1][:, 128:]), axis=1)
    tail = jnp.concatenate((gains[0][:, :128], gains[1][:, :128], ends, jnp.zeros((5, 128), F32)), axis=0)
    for b in range(16):
        rows = jnp.concatenate((qkv[36 * b : 36 * b + 36], proj[12 * b : 12 * b + 12]), axis=0)
        own = table[:, 207 * b : 207 * b + 207]
        own = jnp.concatenate((own, jnp.zeros((8, 49), F32)), axis=1)
        chunk = jnp.concatenate((folded(rows), own[:, :128], own[:, 128:], tail), axis=0)
        out_ref[place(b)] = chunk.astype(BF)


def normed(u):
    mean = jnp.mean(u, -1, keepdims=True)
    centred = u - mean
    scale = lax.rsqrt(jnp.mean(centred * centred, -1, keepdims=True) + 1e-05)
    return centred * scale, scale


def normed_back(grad, unit, scale):
    mean = jnp.mean(grad, -1, keepdims=True)
    product = jnp.mean(grad * unit, -1, keepdims=True)
    return scale * (grad - mean - unit * product)


def head_masks():
    lane = lax.broadcasted_iota(jnp.int32, (1, DIM), 1) // HEAD
    return [(lane == h).astype(F32) for h in range(HEADS)]


def by_head(x, masks):
    return jnp.concatenate([x * m.astype(BF) for m in masks], axis=0)


def from_heads(x, masks):
    total = x[:WIN] * masks[0]
    for h in range(1, HEADS):
        total = total + x[h * WIN : h * WIN + WIN] * masks[h]
    return total


def forward(u, gains, w_qkv, w_proj, w_fc1, bias_ref, allowed, prob_ref, meanwhile=None):
    masks = head_masks()
    unit, _ = normed(u)
    n1 = (unit * gains[0:1]).astype(BF)
    q, k, v = (
        nn(n1, w_qkv[:, i * DIM : i * DIM + DIM]) for i in range(3)
    )
    joined = []
    for n in range(2):
        part = slice(n * WIN, n * WIN + WIN)
        scores = nt(by_head(k[part].astype(BF), masks), q[part].astype(BF))
        v_t = jnp.transpose(v[part]).astype(BF)
        out_t = []
        for h in range(HEADS):
            rows = slice(h * WIN, h * WIN + WIN)
            bias = jnp.concatenate((bias_ref[0, rows, :], bias_ref[1, rows, :16]), axis=1)
            s = scores[rows] * SCALE + bias
            if allowed is not None:
                s = jnp.where(allowed, s, -1e30)
            e = jnp.exp(s - jnp.max(s, 0, keepdims=True))
            p = (e * (1.0 / jnp.sum(e, 0, keepdims=True))).astype(BF)
            prob_ref[n, rows, :] = p
            out_t.append(nn(v_t[h * HEAD : h * HEAD + HEAD], p))
        joined.append(jnp.transpose(jnp.concatenate(out_t, axis=0)))
    o = jnp.concatenate(joined, axis=0).astype(BF)
    if meanwhile is not None:
        meanwhile()
    m = u + nn(o, w_proj[...])
    unit2, _ = normed(m)
    n2 = (unit2 * gains[1:2]).astype(BF)
    e = nn(n2, w_fc1[...])
    cdf = 0.5 * (1.0 + lax.erf(e * (0.5**0.5)))
    g = (e * cdf).astype(BF)

    def slope():
        return (cdf + e * jnp.exp(e * e * -0.5) * 0.3989422804014327).astype(BF)

    return q.astype(BF), k.astype(BF), v.astype(BF), o, m, g, slope


def back_mlp(cot, slope, w_fc2):
    y2 = cot.astype(BF)
    dg = nn(y2, w_fc2).astype(BF).astype(F32)
    return y2, (dg * slope.astype(F32)).astype(BF)


def back_middle(cot, y1, unit, scale, gain, w_fc1):
    dn = nt(y1, w_fc1).astype(BF).astype(F32)
    return cot + normed_back(dn * gain, unit, scale), jnp.sum(dn * unit, 0, keepdims=True)


def mlp_grads(y2, y1, g, unit, gain):
    n2 = (unit * gain).astype(BF)
    return tn(y1, n2), [tn(y2, g[:, DIM * i : DIM * i + DIM]) for i in range(4)]


def back_attention(do, q, k, v, prob_ref, grad_ref, meanwhile=None):
    masks = head_masks()
    dqs, dks, dvs = [], [], []
    for n in range(2):
        part = slice(n * WIN, n * WIN + WIN)
        do_n, q_n, k_n, v_n = do[part], q[part], k[part], v[part]
        dp = nt(by_head(v_n, masks), do_n)
        dvs.append(from_heads(nn(prob_ref[n], do_n), masks))
        k_t = jnp.transpose(k_n.astype(F32)).astype(BF)
        ds_all, dq_t = [], []
        for h in range(HEADS):
            rows = slice(h * WIN, h * WIN + WIN)
            p = prob_ref[n, rows, :].astype(F32)
            dp_h = dp[rows].astype(BF).astype(F32)
            ds = p * (dp_h - jnp.sum(p * dp_h, 0, keepdims=True))
            if n == 0:
                grad_ref[0, rows, :] = ds[:, :128]
                grad_ref[1, rows, :16] = ds[:, 128:]
            else:
                grad_ref[0, rows, :] += ds[:, :128]
                grad_ref[1, rows, :16] += ds[:, 128:]
            ds = (ds * SCALE).astype(BF)
            ds_all.append(ds)
            dq_t.append(nn(k_t[h * HEAD : h * HEAD + HEAD], ds))
            if n == 0 and h == 2 and meanwhile is not None:
                meanwhile()
        dqs.append(jnp.transpose(jnp.concatenate(dq_t, axis=0)))
        dks.append(from_heads(nn(jnp.concatenate(ds_all, axis=0), q_n), masks))
    return [jnp.concatenate(parts, axis=0).astype(BF) for parts in (dqs, dks, dvs)]


def back_input(dm, d_qkv, unit, scale, gain, w_qkv):
    dn = jnp.zeros((TOK, DIM), F32)
    for i in range(3):
        dn = dn + nt(d_qkv[i], w_qkv[:, i * DIM : i * DIM + DIM])
    dn = dn.astype(BF).astype(F32)
    return dm + normed_back(dn * gain, unit, scale), jnp.sum(dn * unit, 0, keepdims=True)


def qkv_grads(d_qkv, unit, gain):
    n1 = (unit * gain).astype(BF)
    return jnp.concatenate([tn(d, n1) for d in d_qkv], axis=0)


def quarters(x):
    return {
        (n, ih, half): x[n * WIN + ih * 72 + half * 36 :][:36]
        for n in range(2)
        for ih in range(2)
        for half in range(2)
    }


def padded(pieces, rows):
    have = sum(p.shape[0] for p in pieces)
    return jnp.concatenate(list(pieces) + [jnp.zeros((rows - have, DIM), F32)], axis=0).astype(BF)


OWN = ((0, 1, 1), (1, 1, 0), (1, 1, 1))
BY_LAT = ((0, 0, 1), (1, 0, 0), (1, 0, 1))
BY_LON = ((0, 1, 0),)
BY_BOTH = ((0, 0, 0),)


def shifted(have):
    order = []
    for n in range(2):
        for ih in range(2):
            order += [(n, ih, 1), ((n + 1) % 2, ih, 0)]
    return jnp.concatenate([have[key] for key in order], axis=0)


def unshifted(x):
    have = {}
    row = 0
    for n in range(2):
        for ih in range(2):
            for key in ((n, ih, 1), ((n + 1) % 2, ih, 0)):
                have[key] = x[row : row + 36]
                row += 36
    return have


def whole_block(have):
    return jnp.concatenate(
        [have[n, ih, half] for n in range(2) for ih in range(2) for half in range(2)], axis=0
    )


def flat_rows(ref):
    return jnp.concatenate([ref[z, i].astype(F32) for z in range(2) for i in range(6)], axis=0)


MESH = pl.DeviceIdType.MESH


def ring(names):
    sizes = [lax.axis_size(name) for name in names]
    me = 0
    for name, size in zip(names, sizes):
        me = me * size + lax.axis_index(name)
    total = 1
    for size in sizes:
        total *= size

    def at(index):
        where = {}
        for name, size in reversed(list(zip(names, sizes))):
            where[name] = lax.rem(index, size)
            index = index // size
        return where

    return me, total, at


def farthest_first(count):
    return sorted(range(1, count), key=lambda o: -min(o, count - o))


def kernel(state_in, cot_in, order_in, lanes_in, table_in, gains_in, w_qkv_in, w_proj_in, w_fc1_in, w_fc2_in,
           du_ref, qkv_ref, proj_ref, fc1_ref, fc2_ref, gain_ref, table_ref,
           state, cot, order, lanes, table, gains, w_qkv, w_proj, w_fc1, w_fc2,
           q_ref, k_ref, v_ref, o_ref, g_ref, slope_ref, prob_first, prob_second, bias_ref, grad_ref,
           mine_ref, own_ref, unit_ref, scale_ref, *rest):
    halos, rest = rest[:18], rest[18:]
    parts, got_a, sum_a, got_b = (rest[4 * i : 4 * i + 4] for i in range(4))
    rest = rest[16:]
    sent_d, got_d, sent_e, got_e, load, send_h, recv_h, send_a, recv_a, send_b, recv_b, send_d, recv_d = rest
    core = lax.axis_index("lon_2")
    chip, chip_count, chip_at = ring(LON[:2])
    lat_me, lat_count, lat_at = ring(LAT)
    lon_me, lon_count, lon_at = ring(LON)
    core_peer = {"lon_2": 1 - core}

    def chip_peer(o):
        return lax.rem(chip + o, chip_count)

    def lat_peer(o):
        return lax.rem(lat_me + o, lat_count)

    def neighbours(way):
        lat = lat_at(lax.rem(lat_me + way + lat_count, lat_count))
        lon = lon_at(lax.rem(lon_me + way + lon_count, lon_count))
        return lat, lon, {**lat, **lon}

    lower, upper = neighbours(-1), neighbours(1)
    peers = (
        [lat_at(lat_peer(o)) for o in farthest_first(lat_count)]
        + [chip_at(chip_peer(o)) for o in farthest_first(chip_count)]
        + [*reversed(lower), *reversed(upper), core_peer]
    )
    barrier = pltpu.get_barrier_semaphore()
    for device in peers:
        pl.semaphore_signal(barrier, inc=1, device_id=device, device_id_type=MESH)
    loads = [
        pltpu.make_async_copy(source, target, load.at[i])
        for i, (source, target) in enumerate(
            (
                (order_in, order),
                (state_in, state),
                (cot_in, cot),
                (table_in, table),
                (lanes_in, lanes),
                (gains_in, gains),
                (w_qkv_in, w_qkv),
                (w_proj_in, w_proj),
                (w_fc1_in, w_fc1),
                (w_fc2_in, w_fc2),
            )
        )
    ]
    for copy in loads:
        copy.start()

    def send(source, target, sems, i, device):
        copy = pltpu.make_async_remote_copy(
            src_ref=source, dst_ref=target, send_sem=sems[0].at[i], recv_sem=sems[1].at[i],
            device_id=device, device_id_type=MESH,
        )
        copy.start()
        return copy

    def table_of(block):
        return jnp.concatenate([table[block, h] for h in range(HEADS)] + [jnp.zeros((2, POS), F32)], axis=0)

    def exchange(step, targets):
        return [
            send(halos[6 * step + i], halos[6 * step + 3 + i], (send_h, recv_h), 3 * step + i, targets[i])
            for i in (2, 1, 0)
        ]

    def fill(step, have):
        for i, keys in enumerate((BY_LAT, BY_LON, BY_BOTH)):
            ref = halos[6 * step + i]
            ref[...] = padded([have[key] for key in keys], ref.shape[0])

    def arrived(step, own):
        have = {}
        for ref, keys in zip((own, *halos[6 * step + 3 : 6 * step + 6]), (OWN, BY_LAT, BY_LON, BY_BOTH)):
            rows = ref[...].astype(F32)
            for i, key in enumerate(keys):
                have[key] = rows[36 * i : 36 * i + 36]
        return have

    for copy in loads[:2]:
        copy.wait()
    perm = order[...]
    x = nn(perm, flat_rows(state).astype(BF))
    loads[2].wait()
    given = quarters(nn(perm, flat_rows(cot).astype(BF)))
    fill(0, given)
    for copy in loads[3:5]:
        copy.wait()
    expand_bias(table_of(0), lanes[...], False, bias_ref)
    for copy in loads[5:7]:
        copy.wait()
    first_gains, second_gains = gains[0], gains[1]

    def rest_of_loads():
        for copy in loads[7:]:
            copy.wait()

    q, k, v, o, m, g, slope = forward(
        x, first_gains, w_qkv[0], w_proj.at[0], w_fc1.at[0], bias_ref, None, prob_first, rest_of_loads
    )
    out = quarters(m + nt(g, w_fc2[0]))
    fill(1, out)
    pl.semaphore_wait(barrier, len(peers))
    flights = exchange(1, lower)
    later_flights = exchange(0, lower)
    own_ref[0] = padded([out[key] for key in OWN], 112)
    own_ref[1] = padded([given[key] for key in OWN], 112)
    for ref, value in ((q_ref, q), (k_ref, k), (v_ref, v), (o_ref, o), (g_ref, g), (slope_ref, slope())):
        ref[...] = value

    for i, value in enumerate((x, m)):
        unit_ref[i], scale_ref[i] = normed(value)

    expand_bias(table_of(1), lanes[...], True, bias_ref)
    row = lax.broadcasted_iota(jnp.int32, (WIN, WIN), 0)
    lane = lax.broadcasted_iota(jnp.int32, (WIN, WIN), 1)
    same_z = (row % 6 // 3) == (lane % 6 // 3)
    same_h = (row // 72) == (lane // 72)
    allowed = same_z & (same_h | (jnp.full((WIN, WIN), lat_me, jnp.int32) < lat_count - 1))
    grad_ref[...] = jnp.zeros_like(grad_ref)
    for flight in flights:
        flight.wait()
    u = shifted(arrived(1, own_ref.at[0]))
    q, k, v, o, m, g, slope = forward(
        u, second_gains, w_qkv[1], w_proj.at[1], w_fc1.at[1], bias_ref, allowed, prob_second
    )
    for flight in later_flights:
        flight.wait()
    cot_u = shifted(arrived(0, own_ref.at[1]))
    y2, y1 = back_mlp(cot_u, slope(), w_fc2[1])
    unit2, scale2 = normed(m)
    dm, gain2 = back_middle(cot_u, y1, unit2, scale2, second_gains[1:2], w_fc1[1])
    yp = dm.astype(BF)
    d_qkv = back_attention(nt(yp, w_proj[1]).astype(BF), q, k, v, prob_second, grad_ref)
    unit1, scale1 = normed(u)
    du, gain1 = back_input(dm, d_qkv, unit1, scale1, second_gains[0:1], w_qkv[1])
    have = unshifted(du)
    fill(2, have)
    flights = exchange(2, upper)
    mine_ref[...] = jnp.concatenate([have[key] for key in OWN] + [jnp.zeros((4, DIM), F32)], axis=0)

    flights_a, flights_b, done = [None] * 4, [None] * 4, [None] * 4

    def start_a(i):
        flights_a[i] = send(parts[i].at[pl.ds((1 - core) * 8, 8)], got_a[i], (send_a, recv_a), i, core_peer)

    def start_b(i):
        flights_a[i].wait()
        sum_a[i][...] = (parts[i][pl.ds(core * 8, 8)].astype(F32) + got_a[i][...].astype(F32)).astype(BF)
        flights_b[i] = [
            send(sum_a[i].at[chip_peer(o)], got_b[i].at[chip], (send_b, recv_b),
                 i * (chip_count - 1) + o - 1, chip_at(chip_peer(o)))
            for o in farthest_first(chip_count)
        ]
        got_b[i][pl.ds(chip, 1)] = sum_a[i][pl.ds(chip, 1)]

    def finish_b(i):
        for flight in flights_b[i]:
            flight.wait()
        chunk = got_b[i][0].astype(F32)
        for o in range(1, chip_count):
            chunk = chunk + got_b[i][o].astype(F32)
        if i % 2 == 0:
            rows = unfolded(chunk)
            done[i] = (jnp.transpose(rows[:48]), rows[48:])
        else:
            sums = jnp.concatenate((chunk[72:80], chunk[80:88]), axis=1)
            for h in range(HEADS):
                table_ref[1 - i // 2, h] = sums[h : h + 1, :207]
            pieces = [chunk[88 + r : 89 + r, 64 * c : 64 * c + 64] for r in range(2) for c in range(2)]
            ends = [chunk[90:91, :64], chunk[90:91, 64:]]
            gain = jnp.concatenate(pieces[:2] + ends[:1] + pieces[2:] + ends[1:], axis=0)
            done[i] = (jnp.transpose(unfolded(chunk[:72])), gain)

    pack_mlp(*mlp_grads(y2, y1, g, unit2, second_gains[1:2]), parts[0])
    start_a(0)
    pack_attention(
        qkv_grads(d_qkv, unit1, second_gains[0:1]), tn(yp, o), reduce_bias(grad_ref, lanes[...], True),
        (gain1, gain2), parts[1],
    )
    start_a(1)

    start_b(0)
    for flight in flights:
        flight.wait()
    start_b(1)
    cot_x = whole_block(arrived(2, mine_ref))
    y2, y1 = back_mlp(cot_x, slope_ref[...], w_fc2[0])
    unit2, scale2 = unit_ref[1], scale_ref[1]
    pack_mlp(*mlp_grads(y2, y1, g_ref[...], unit2, first_gains[1:2]), parts[2])
    start_a(2)
    dm, gain2 = back_middle(cot_x, y1, unit2, scale2, first_gains[1:2], w_fc1[0])
    yp = dm.astype(BF)
    do = nt(yp, w_proj[0]).astype(BF)
    d_qkv = back_attention(do, q_ref[...], k_ref[...], v_ref[...], prob_first, grad_ref, lambda: start_b(2))
    unit1, scale1 = unit_ref[0], scale_ref[0]
    du, gain1 = back_input(dm, d_qkv, unit1, scale1, first_gains[0:1], w_qkv[0])
    pack_attention(
        qkv_grads(d_qkv, unit1, first_gains[0:1]), tn(yp, o_ref[...]), reduce_bias(grad_ref, lanes[...], False),
        (gain1, gain2), parts[3],
    )
    start_a(3)
    finish_b(0)
    finish_b(1)
    start_b(3)
    finish_b(2)
    across = jnp.concatenate([done[1][0], done[2][0], done[0][0]], axis=1)
    for a in range(16):
        low_row, right = 12 * (a // 4), 48 * (a % 4)
        piece = jnp.concatenate(
            [across[12 * a : 12 * a + 12]]
            + [done[i][1][low_row : low_row + 12, right : right + 48] for i in (2, 0)]
            + [jnp.zeros((12, 16), F32)],
            axis=1,
        )
        sent_d[a] = jnp.concatenate((piece, jnp.zeros((4, 256), F32)), axis=0).astype(BF)

    def to_latitudes(source, target, first_sem):
        return [
            send(source.at[lat_peer(o)], target.at[lat_me], (send_d, recv_d), first_sem + o - 1, lat_at(lat_peer(o)))
            for o in farthest_first(lat_count)
        ]

    flights_d = to_latitudes(sent_d, got_d, 0)
    got_d[pl.ds(lat_me, 1)] = sent_d[pl.ds(lat_me, 1)]
    high, low = two_pieces(du)
    flat = tn(order[...], high) + tn(order[...], low)
    for z in range(2):
        for i in range(6):
            start = (z * 6 + i) * 24
            du_ref[z, i] = flat[start : start + 24]
    finish_b(3)
    gain = jnp.concatenate((done[3][1], done[1][1]), axis=0)
    for a in range(16):
        piece = jnp.concatenate((done[3][0][12 * a : 12 * a + 12], gain, jnp.zeros((12, 16), F32)), axis=1)
        sent_e[a] = jnp.concatenate((piece, jnp.zeros((4, 128), F32)), axis=0).astype(BF)
    flights_e = to_latitudes(sent_e, got_e, lat_count - 1)
    got_e[pl.ds(lat_me, 1)] = sent_e[pl.ds(lat_me, 1)]
    for flight in flights_d:
        flight.wait()

    def summed(ref):
        total = ref[0].astype(F32)
        for o in range(1, lat_count):
            total = total + ref[o].astype(F32)
        return total

    total = summed(got_d)
    qkv_ref[:, 1, :] = total[:12, :36]
    proj_ref[:, 1, :] = total[:12, 36:48]
    for i in range(2):
        fc1_ref[:, i, :] = total[:12, 48 + 48 * i : 96 + 48 * i]
        fc2_ref[:, i, :] = total[:12, 144 + 48 * i : 192 + 48 * i]
    for flight in flights_e:
        flight.wait()
    total = summed(got_e)
    qkv_ref[:, 0, :] = total[:12, :36]
    proj_ref[:, 0, :] = total[:12, 36:48]
    for r in range(4):
        gain_ref[r // 2, r % 2 : r % 2 + 1] = jnp.concatenate(
            [total[3 * r + c : 3 * r + c + 1, 48:112] for c in range(3)], axis=1
        )


def hand_over(*refs):
    for source, target in zip(refs[:7], refs[7:]):
        target[...] = source[...]


def body(state, out_cot, qkv_weight, proj_weight, fc1_weight, fc2_weight, norm_gain, bias_table):
    vmem = pl.BlockSpec(memory_space=pltpu.VMEM)
    dma = pltpu.SemaphoreType.DMA
    args = (
        state, out_cot, token_order(), lane_order(), bias_table.reshape(2, HEADS, 1, POS), norm_gain,
        qkv_weight, proj_weight, fc1_weight, jnp.swapaxes(fc2_weight, 1, 2),
    )
    buffers = [(a.shape, a.dtype) for a in args] + [((TOK, DIM), BF)] * 4 + [
        ((TOK, HID), BF),
        ((TOK, HID), BF),
        ((2, HEADS * WIN, WIN), BF),
        ((2, HEADS * WIN, WIN), BF),
        ((2, 8 * WIN, 128), F32),
        ((2, 8 * WIN, 128), F32),
        ((112, DIM), F32),
        ((2, 112, DIM), BF),
        ((2, TOK, DIM), F32),
        ((2, TOK, 1), F32),
    ]
    buffers += [((112, DIM), BF), ((48, DIM), BF), ((48, DIM), BF)] * 6
    rows = (144, 96, 144, 96)
    for lead in (16, 8, 8, 8):
        buffers += [((lead, r, 128), BF) for r in rows]
    buffers += [((16, 16, 256), BF), ((16, 16, 256), BF), ((16, 16, 128), BF), ((16, 16, 128), BF)]
    shapes = (
        (2, 6, 24, DIM), (12, 2, 36), (12, 2, 12), (12, 2, 48), (12, 2, 48), (2, 2, DIM), (2, 6, 1, 207)
    )
    outs = pl.pallas_call(
        kernel,
        in_specs=[pl.BlockSpec(memory_space=pltpu.HBM)] * 10,
        out_specs=[vmem] * 7,
        out_shape=[jax.ShapeDtypeStruct(s, F32) for s in shapes],
        scratch_shapes=[pltpu.VMEM(s, d) for s, d in buffers]
        + [dma((n,)) for n in (10, 9, 9, 4, 4, 28, 28, 30, 30)],
        compiler_params=pltpu.CompilerParams(
            collective_id=0, has_side_effects=True, vmem_limit_bytes=60 * 1024 * 1024
        ),
    )(*args)
    outs = pl.pallas_call(
        hand_over,
        in_specs=[vmem] * 7,
        out_specs=[vmem] * 7,
        out_shape=[jax.ShapeDtypeStruct(s, F32) for s in shapes],
        compiler_params=pltpu.CompilerParams(vmem_limit_bytes=60 * 1024 * 1024),
    )(*outs)
    state_grad, qkv, proj, fc1, fc2, gain, table = outs
    return (
        state_grad,
        jnp.swapaxes(qkv, 0, 1),
        jnp.swapaxes(proj, 0, 1),
        jnp.swapaxes(fc1, 0, 1),
        jnp.transpose(fc2, (1, 2, 0)),
        gain,
        table.reshape(2, 1, 1, HEADS, 207),
    )


def solution(mesh):
    split = Mesh(mesh.devices.reshape(8, 2, 4, 2, 2), ("lat_0", "lat_1", "lon_0", "lon_1", "lon_2"))
    placed = (
        P(None, LAT, LON, None),
        P(None, LAT, LON, None),
        P(),
        P(),
        P(),
        P(),
        P(),
        P(None, LAT, None, None, None),
    )
    return jax.shard_map(
        body,
        mesh=split,
        in_specs=placed,
        out_specs=(
            P(None, LAT, LON, None),
            P(None, LAT, LON),
            P(None, LAT, LON),
            P(None, LAT, LON),
            P(None, LAT, LON),
            P(),
            P(None, LAT, None, None, LON),
        ),
        check_vma=False,
    )
```
